512 devices in a mesh: normal: 4 (over z_lo), strike: 16 (over z_hi, y), depth: 8 (over x, core).
Axes of the slice: x: 4, y: 4, z: 16 (z_hi: 4, z_lo: 4; z = z_hi * 4 + z_lo), core: 2. Of those that a mesh axis runs over, the one named last changes fastest.
Arguments:
- field_now: float32 [3, 32, 256, 1024], P(None, 'normal', 'strike', 'depth'), may hold values from -6 to 6
- field_prev: float32 [3, 32, 256, 1024], P(None, 'normal', 'strike', 'depth'), may hold values from -6 to 6
- rigidity: bfloat16 [32, 256, 1024], P('normal', 'strike', 'depth'), may hold values from 1 to 2
- density: bfloat16 [32, 256, 1024], P('normal', 'strike', 'depth'), may hold values from 1 to 2
- fault_nodes: int32 [16, 8, 256], P('strike', 'depth'), may hold values from 0 to 2047, as said below
- patch_ids: int32 [16, 8, 256], P('strike', 'depth'), may hold values from 0 to 255, as said below
Outputs:
- field_next: float32 [3, 32, 256, 1024], P(None, 'normal', 'strike', 'depth')
- field_mid: float32 [3, 32, 256, 1024], P(None, 'normal', 'strike', 'depth')
- slip_gradient: float32 [256, 3], P(('strike', 'depth'))
The draws below stay inside these ranges and needn't reach their ends.
Inputs may be any that keep to these rules, and one draw needn't show every extreme that they name: `fault_nodes`: within one block the 256 entries are distinct. `patch_ids`: every patch holds exactly 128 pairs over all blocks.
All inputs are finite; a program needn't handle non-finite values.
Results may differ from the reference program's by a relative error of at most 0.0003.
Values may be sent and summed in bfloat16 or wider, within the bound.
No kernel may reach another device: no remote copies, remote signals or barrier semaphores. Data moves between devices by JAX's collectives and lax.ppermute only.
A program may use at most 64 MiB of HBM per device.

```python
import math
import jax
import jax.numpy as jnp
import numpy as np
from jax import lax

CY = 16
CZ = 128
PATCH_NODES = 128
FAULT_DEV = 256
PATCHES = 256
NX = 32
NY = 256
NZ = 1024
N_STRIKE = 16
N_DEPTH = 8


def draw_fault_nodes(key, part):
    key = jax.random.fold_in(key, 11)
    block_keys = jax.random.split(key, N_STRIKE * N_DEPTH)
    face_count = CY * CZ

    def one_block(block_key):
        shuffled = jax.random.permutation(block_key, face_count - 2) + 1
        ends = jnp.array([face_count - 1, 0], jnp.int32)
        return jnp.concatenate([ends, shuffled[:FAULT_DEV - 2].astype(jnp.int32)])
    return jax.vmap(one_block)(block_keys).reshape(N_STRIKE, N_DEPTH, FAULT_DEV)


def draw_patch_ids(key, part):
    key = jax.random.fold_in(key, 23)
    node_total = N_STRIKE * N_DEPTH * FAULT_DEV
    shuffled = jax.random.permutation(key, node_total)
    return (shuffled // PATCH_NODES).astype(jnp.int32).reshape(N_STRIKE, N_DEPTH, FAULT_DEV)


def block_scale(stream_key, extent, cuts, low, largest):
    level, own = 1.0, jax.random.fold_in(stream_key, 6)
    for dim, blocks in cuts:
        heights = jnp.exp(jax.random.uniform(jax.random.fold_in(own, dim), (blocks,), jnp.float32, low / len(cuts), largest / len(cuts)))
        level = level * jnp.repeat(heights, extent[dim] // blocks).reshape([-1 if axis == dim else 1 for axis in range(len(extent))])
    return level


def bell_draw(key, extent, width, most, shards=(), held_as=jnp.bfloat16):
    factor_of = block_scale(key, extent, shards, -0.22, 0.18) if shards else 1.0
    values = jax.random.normal(key, extent, jnp.float32) * width * factor_of
    return jnp.minimum(jnp.maximum(values, -most), most).astype(held_as)


def setup_inputs(seed: int = 0) -> dict:
    streams_of = jax.random.split(jax.random.key(seed), 7)
    return {
        "field_now": bell_draw(streams_of[0], (3, NX, NY, NZ), 1.0, 6.0, ((1, 4), (2, 16), (3, 8)), jnp.float32),
        "field_prev": bell_draw(streams_of[1], (3, NX, NY, NZ), 1.0, 6.0, ((1, 4), (2, 16), (3, 8)), jnp.float32),
        "rigidity": jnp.clip(1.0 + 1.0 * jax.random.uniform(streams_of[2], (NX, NY, NZ), jnp.float32) ** block_scale(streams_of[2], (NX, NY, NZ), ((0, 4), (1, 16), (2, 8)), -0.2, 0.2), 1.0, 2.0).astype(jnp.bfloat16),
        "density": jnp.clip(1.0 + 1.0 * jax.random.uniform(streams_of[3], (NX, NY, NZ), jnp.float32) ** block_scale(streams_of[3], (NX, NY, NZ), ((0, 4), (1, 16), (2, 8)), -0.2, 0.2), 1.0, 2.0).astype(jnp.bfloat16),
        "fault_nodes": draw_fault_nodes(jax.random.fold_in(streams_of[6], 71), 0),
        "patch_ids": draw_patch_ids(jax.random.fold_in(streams_of[6], 71), 0),
    }


DT = 0.03
HIGHEST_PRECISION = lax.Precision.HIGHEST

def gll_tables():
    spread_point = math.sqrt(3.0 / 7.0)
    points = np.array([-1.0, -spread_point, 0.0, spread_point, 1.0])
    weights = np.array([0.1, 49.0 / 90.0, 32.0 / 45.0, 49.0 / 90.0, 0.1]) * 0.5
    derivative = np.zeros((5, 5))
    for row_index in range(5):
        for col_index in range(5):
            if row_index == col_index:
                derivative[row_index, col_index] = sum((1.0 / (points[row_index] - points[other_index]) for other_index in range(5) if other_index != row_index))
            else:
                row_product = np.prod([points[row_index] - points[other_index] for other_index in range(5) if other_index != row_index])
                col_product = np.prod([points[col_index] - points[other_index] for other_index in range(5) if other_index != col_index])
                derivative[row_index, col_index] = row_product / (col_product * (points[row_index] - points[col_index]))
    return (weights, 2.0 * derivative)

def node_weights(count, weights):
    positions = np.arange(count)
    node_table = weights[positions % 4].copy()
    node_table[positions % 4 == 0] = 2.0 * weights[0]
    node_table[0] = weights[0]
    return node_table

def element_view(values):
    count_elems = values.shape[-1] // 4
    blocks = values.reshape(values.shape[:-1] + (count_elems, 4))
    closing = jnp.concatenate([blocks[..., 1:, 0], jnp.zeros(values.shape[:-1] + (1,), values.dtype)], axis=-1)
    return jnp.concatenate([blocks, closing[..., None]], axis=-1)

def element_terms(values, rigid_field, weights, derivative):
    grads = jnp.einsum('...ea,ba->...eb', element_view(values), derivative, precision=HIGHEST_PRECISION)
    fluxes = grads * weights * element_view(rigid_field)
    return jnp.einsum('...eb,ba->...ea', fluxes, derivative, precision=HIGHEST_PRECISION)

def assemble(terms):
    closing = terms[..., 4]
    carried = jnp.concatenate([jnp.zeros(terms.shape[:-2] + (1,), terms.dtype), closing[..., :-1]], axis=-1)
    nodes = terms[..., :4].at[..., 0].add(carried)
    return nodes.reshape(terms.shape[:-2] + (-1,))

def stiffness(component, rigid_field, tables):
    weights, derivative, weight_x, weight_y, weight_z = tables
    x_terms = element_terms(jnp.moveaxis(component, 0, -1), jnp.moveaxis(rigid_field, 0, -1), weights, derivative)
    face_weight = weight_y[:, None] * weight_z[None, :]
    x_force = jnp.moveaxis(assemble(x_terms) * face_weight[:, :, None], -1, 0)
    middle = NX // 8
    traction = 0.5 * (x_terms[:, :, middle - 1, 4] - x_terms[:, :, middle, 0]) * face_weight
    y_terms = element_terms(jnp.moveaxis(component, 1, -1), jnp.moveaxis(rigid_field, 1, -1), weights, derivative)
    y_force = jnp.moveaxis(assemble(y_terms) * (weight_x[:, None] * weight_z[None, :])[:, :, None], -1, 1)
    z_terms = element_terms(component, rigid_field, weights, derivative)
    z_force = assemble(z_terms) * (weight_x[:, None] * weight_y[None, :])[:, :, None]
    return (x_force + y_force + z_force, traction)

def reference(field_now, field_prev, rigidity, density, fault_nodes, patch_ids):
    weights_np, derivative_np = gll_tables()
    float_type = field_now.dtype
    weights = jnp.asarray(weights_np, float_type)
    derivative = jnp.asarray(derivative_np, float_type)
    weight_x = jnp.asarray(node_weights(NX, weights_np), float_type)
    weight_y = jnp.asarray(node_weights(NY, weights_np), float_type)
    weight_z = jnp.asarray(node_weights(NZ, weights_np), float_type)
    tables = (weights, derivative, weight_x, weight_y, weight_z)
    rigid_field = rigidity.astype(jnp.float32)
    mass = density.astype(jnp.float32) * weight_x[:, None, None] * weight_y[None, :, None] * weight_z[None, None, :]
    current, previous = (field_now, field_prev)
    collected = jnp.zeros((3, N_STRIKE, N_DEPTH, FAULT_DEV), jnp.float32)
    index_table = jnp.broadcast_to(fault_nodes[None], (3,) + fault_nodes.shape)
    states = []
    for step_index in range(2):
        force, traction = lax.map(lambda component: stiffness(component, rigid_field, tables), current)
        blocks = traction.reshape(3, N_STRIKE, CY, N_DEPTH, CZ).transpose(0, 1, 3, 2, 4).reshape(3, N_STRIKE, N_DEPTH, CY * CZ)
        collected = collected + jnp.take_along_axis(blocks, index_table, axis=3)
        following = 2.0 * current - previous - DT * DT * force / mass
        previous, current = (current, following)
        states.append(current)
    gradient = jax.ops.segment_sum(collected.reshape(3, -1).T, patch_ids.reshape(-1), num_segments=PATCHES)
    return (current, states[0], gradient)
```

```python
import functools
import math

import jax
import jax.numpy as jnp
import numpy as np
from jax import lax
from jax.experimental import pallas as pl
from jax.experimental.pallas import tpu as pltpu
from jax.sharding import PartitionSpec as P

DT = 0.03
NXL, NYL, NZL = 8, 16, 128
ROWS = NXL * NYL
F32 = jnp.float32
HIGHEST = lax.Precision.HIGHEST


def gll_tables():
    spread = math.sqrt(3.0 / 7.0)
    points = np.array([-1.0, -spread, 0.0, spread, 1.0])
    weights = np.array([0.1, 49.0 / 90.0, 32.0 / 45.0, 49.0 / 90.0, 0.1]) * 0.5
    derivative = np.zeros((5, 5))
    for b in range(5):
        for a in range(5):
            if a == b:
                derivative[b, a] = sum(1.0 / (points[b] - points[o]) for o in range(5) if o != b)
            else:
                row = np.prod([points[b] - points[o] for o in range(5) if o != b and o != a])
                col = np.prod([points[a] - points[o] for o in range(5) if o != a and o != b])
                derivative[b, a] = row / (col * (points[a] - points[b]))
    return weights, 2.0 * derivative


WQ, D = gll_tables()
W0 = float(WQ[0])
NODE_W = np.array([2 * WQ[0], WQ[1], WQ[2], WQ[3], 2 * WQ[0]])
E = (WQ[:, None] * D).T / NODE_W[:, None]
KAPPA = float(E[4, 4])


def total(pairs):
    acc = None
    for const, arr in pairs:
        if abs(const) < 1e-12:
            continue
        term = arr * np.float32(const)
        acc = term if acc is None else acc + term
    return acc


def element(v, r):
    twice = v[2] + v[2]
    s0, s1 = v[0] + v[4] - twice, v[1] + v[3] - twice
    d0, d1 = v[0] - v[4], v[1] - v[3]
    ev = [total([((D[b, 0] + D[b, 4]) / 2, s0), ((D[b, 1] + D[b, 3]) / 2, s1)]) for b in (0, 1)]
    od = [total([((D[b, 0] - D[b, 4]) / 2, d0), ((D[b, 1] - D[b, 3]) / 2, d1)]) for b in (0, 1)]
    g2 = total([(D[2, 0], d0), (D[2, 1], d1)])
    q = [r[0] * (od[0] + ev[0]), r[1] * (od[1] + ev[1]), r[2] * g2, r[3] * (od[1] - ev[1]), r[4] * (od[0] - ev[0])]
    p0, m0, p1, m1 = q[0] + q[4], q[0] - q[4], q[1] + q[3], q[1] - q[3]
    ec = [total([((E[a, 0] + E[a, 4]) / 2, p0), ((E[a, 1] + E[a, 3]) / 2, p1), (E[a, 2], q[2])]) for a in (0, 1)]
    oc = [total([((E[a, 0] - E[a, 4]) / 2, m0), ((E[a, 1] - E[a, 3]) / 2, m1)]) for a in (0, 1)]
    c2 = total([(E[2, 0], m0), (E[2, 1], m1)])
    return [oc[0] + ec[0], oc[1] + ec[1], c2, oc[1] - ec[1], oc[0] - ec[0]]


def first_term(v, r):
    twice = v[2] + v[2]
    s0, s1 = v[0] + v[4] - twice, v[1] + v[3] - twice
    d0, d1 = v[0] - v[4], v[1] - v[3]
    ev = [total([((D[b, 0] + D[b, 4]) / 2, s0), ((D[b, 1] + D[b, 3]) / 2, s1)]) for b in (0, 1)]
    od = [total([((D[b, 0] - D[b, 4]) / 2, d0), ((D[b, 1] - D[b, 3]) / 2, d1)]) for b in (0, 1)]
    g2 = total([(D[2, 0], d0), (D[2, 1], d1)])
    q = [r[0] * (od[0] + ev[0]), r[1] * (od[1] + ev[1]), r[2] * g2, r[3] * (od[1] - ev[1]), r[4] * (od[0] - ev[0])]
    return total([(E[0, b], q[b]) for b in range(5)])


def open_terms(v, r):
    flux = [r[b] * total([(D[b, a], v[a]) for a in range(4)]) for b in range(4)]
    part = total([(E[4, b], flux[b]) for b in range(4)])
    grad = total([(D[4, a], v[a]) for a in range(4)])
    return part, grad


def open_scale(r):
    return total([(E[4, b] * D[b, 4], r[b]) for b in range(4)])


def rolled(x, shift):
    shift = shift % NZL
    return x if shift == 0 else pltpu.roll(x, shift, 1)


def lane_of():
    return lax.broadcasted_iota(jnp.int32, (8, NZL), 1)


def lane_table(phase, values):
    out = jnp.full((8, NZL), np.float32(values[0]), F32)
    for b in range(1, 4):
        out = jnp.where(phase == b, np.float32(values[b]), out)
    return out


def x_rows(x, half):
    return pl.ds(x * NYL + half * 8, 8)


def y_rows(y):
    return pl.ds(y, 8, stride=NYL)


def first_lanes(read, read_r, lane):
    out = jnp.zeros((8, NZL), F32)
    for k in range(16):
        rows = pl.ds(8 * k, 8)
        for c in range(3 if read_r is None else 4):
            src = read_r(rows) if c == 3 else read(c, rows)
            out = jnp.where(lane == 4 * k + c, rolled(src, 4 * k + c), out)
    return out


def last_lanes(read, lane):
    out = jnp.zeros((8, NZL), F32)
    for k in range(16):
        out = jnp.where((lane >> 2) == k, rolled(read(pl.ds(8 * k, 8)), 4 * k + 4), out)
    return out


def interleaved(parts, lane, base):
    out = jnp.zeros((8, NZL), F32)
    for j, part in enumerate(parts):
        if part is None:
            continue
        out = jnp.where((lane >= base) & (lane < base + 64) & ((lane & 3) == j), rolled(part, base + j - 3), out)
    return out


def widen(src, dst):
    for x in range(NXL):
        dst[pl.ds(x * NYL, NYL), :] = src[pl.ds(x * NYL, NYL), :].astype(F32)


def pack_kernel(now, rig, xu, xd, yu, yd, zu, zd, rw):
    widen(rig, rw)
    lane = lane_of()
    for half in range(2):
        r = [rw[x_rows(4 + a, half), :] for a in range(4)]
        xu[pl.ds(96 + 8 * half, 8), :] = open_scale(r)
        xd[pl.ds(48 + 8 * half, 8), :] = rw[x_rows(0, half), :]
        for c in range(3):
            part, grad = open_terms([now[c, x_rows(4 + a, half), :] for a in range(4)], r)
            xu[pl.ds(16 * c + 8 * half, 8), :] = part
            xu[pl.ds(48 + 16 * c + 8 * half, 8), :] = grad
            xd[pl.ds(16 * c + 8 * half, 8), :] = now[c, x_rows(0, half), :]
    r = [rw[y_rows(12 + a), :] for a in range(4)]
    yu[pl.ds(48, 8), :] = open_scale(r)
    yd[pl.ds(24, 8), :] = rw[y_rows(0), :]
    for c in range(3):
        part, grad = open_terms([now[c, y_rows(12 + a), :] for a in range(4)], r)
        yu[pl.ds(8 * c, 8), :] = part
        yu[pl.ds(24 + 8 * c, 8), :] = grad
        yd[pl.ds(8 * c, 8), :] = now[c, y_rows(0), :]
    back = lambda t: [rolled(t, 3 - a) for a in range(4)]
    r = back(last_lanes(lambda rows: rw[rows, :], lane))
    parts, grads = [], []
    for c in range(3):
        part, grad = open_terms(back(last_lanes(lambda rows: now[c, rows, :], lane)), r)
        parts.append(part)
        grads.append(grad)
    zu[...] = jnp.where(
        lane < 64, interleaved(parts + [open_scale(r)], lane, 0), interleaved(grads + [None], lane, 64)
    )
    zd[...] = first_lanes(lambda c, rows: now[c, rows, :], lambda rows: rw[rows, :], lane)


def from_fourth(tile, lane):
    phase = lane & 3
    out = tile
    for j in range(3):
        out = jnp.where(phase == j, rolled(tile, j - 3), out)
    return out


def advance(now, prev, rw, low, high_v, high_r, scale, ghost_z, ghost_rz, closing_z, index, store, acc, on_first):
    index_x, index_y, index_z = index
    at_x = jnp.where(index_x == 0, 2.0, 1.0).astype(F32)
    at_y = jnp.where(index_y == 0, 2.0, 1.0).astype(F32)
    at_z = jnp.where(index_z == 0, 2.0, 1.0).astype(F32)

    def along_y(c, carry):
        v = [now[c, y_rows(y), :] for y in range(NYL)] + [high_v[1][pl.ds(8 * c, 8), :]]
        r = [rw[y_rows(y), :] for y in range(NYL)] + [high_r[1][...]]
        carried = low[1](c, v[0])
        for e in range(4):
            terms = element(v[4 * e : 4 * e + 5], r[4 * e : 4 * e + 5])
            head = terms[0] * at_y if e == 0 else terms[0]
            acc[c, y_rows(4 * e), :] = head + carried
            for a in range(1, 4):
                acc[c, y_rows(4 * e + a), :] = terms[a]
            carried = terms[4]
        return carry

    lax.fori_loop(0, 3, along_y, 0)

    lane = lane_of()
    phase = lane & 3
    gm = [lane_table(phase, [D[b, b - k] if b >= k else 0 for b in range(4)]) for k in range(4)]
    gp = [None] + [lane_table(phase, [D[b, b + k] if b + k <= 4 else 0 for b in range(4)]) for k in range(1, 5)]
    cm = [lane_table(phase, [E[a, a - k] if a >= k else 0 for a in range(4)]) for k in range(4)]
    cp = [None] + [lane_table(phase, [E[a, a + k] if a + k <= 3 else 0 for a in range(4)]) for k in range(1, 4)]
    c_close = lane_table(phase, [E[a, 4] for a in range(4)])
    last = [lane_table(phase, [0, 0, 0, E[4, b]]) for b in range(5)]
    first = lane == 0
    edge = jnp.where(first, at_z, jnp.float32(1.0))

    def along_xz(n, carry):
        c, half = n >> 1, n & 1
        offset = half * 8
        rows = [pl.ds(pl.multiple_of(x * NYL + offset, 8), 8) for x in range(NXL)]
        plane = pl.ds(pl.multiple_of(16 * c + offset, 8), 8)
        v = [now[c, rows[x], :] for x in range(NXL)] + [high_v[0][plane, :]]
        r = [rw[rows[x], :] for x in range(NXL)] + [high_r[0][pl.ds(pl.multiple_of(offset, 8), 8), :]]
        carried = low[0](c, offset, plane, v[0])
        back = NZL - (4 * half + c)
        ghost_v = pltpu.roll(ghost_z, back, 1)
        ghost_r = pltpu.roll(ghost_rz, NZL - 4 * half, 1)
        closing = pltpu.roll(closing_z, back, 1)
        for e in range(2):
            terms = element(v[4 * e : 4 * e + 5], r[4 * e : 4 * e + 5])
            if e == 0:
                on_first(c, plane, carried, terms[0])
            for a in range(4):
                x = 4 * e + a
                force = terms[a] + acc[c, rows[x], :]
                if a == 0:
                    force = (terms[0] * at_x if e == 0 else terms[0]) + carried + acc[c, rows[x], :]
                vx = jnp.where(first, rolled(ghost_v, -8 * x), v[x])
                rx = jnp.where(first, rolled(ghost_r, -8 * x), r[x])
                vm = [v[x]] + [rolled(v[x], k) for k in range(1, 4)]
                vp = [None] + [rolled(vx, -k) for k in range(1, 5)]
                g = gm[0] * v[x]
                for k in range(1, 4):
                    g = g + gm[k] * vm[k]
                for k in range(1, 5):
                    g = g + gp[k] * vp[k]
                g4 = total([(D[4, 0], vm[3]), (D[4, 1], vm[2]), (D[4, 2], vm[1]), (D[4, 3], vm[0]), (D[4, 4], vp[1])])
                q = r[x] * g
                q4 = jnp.where(phase == 3, rolled(rx, -1) * g4, 0.0)
                qm = [q] + [rolled(q, k) for k in range(1, 4)]
                own = cm[0] * q
                for k in range(1, 4):
                    own = own + cm[k] * qm[k]
                for k in range(1, 4):
                    own = own + cp[k] * rolled(q, -k)
                pair = q4 + rolled(q4, -1)
                own = own + c_close * (pair + rolled(pair, -2))
                tail = last[3] * q + last[4] * q4
                for b in range(3):
                    tail = tail + last[b] * qm[3 - b]
                tail = jnp.where(first, rolled(closing, -8 * x), rolled(tail, 1))
                force = force + own * edge + tail
                after = (v[x] + v[x]) - prev[c, rows[x], :] - scale[rows[x], :] * force
                store(c, x, rows[x], plane, after)
            carried = terms[4]
        return carry

    lax.fori_loop(0, 6, along_xz, 0)


def step_scale(rho, scale):
    for x in range(NXL):
        rows = pl.ds(x * NYL, NYL)
        scale[rows, :] = np.float32(DT * DT) / rho[rows, :].astype(F32)


def axis_weight(pos, is_first):
    phase = pos & 3
    out = jnp.full(pos.shape, np.float32(2 * W0), F32)
    for b in range(1, 4):
        out = jnp.where(phase == b, np.float32(WQ[b]), out)
    return jnp.where((pos == 0) & is_first, np.float32(W0), out)


def first_kernel(
    middle, now, prev, rig, rho, xu, xd, yu, yd, zu, zd, zd_own,
    out, xu2, xd2, yu2, yd2, zu2, zd2, mx, my, mz, slip,
    rw, scale, acc, early,
):
    index = (lax.axis_index("normal"), lax.axis_index("strike"), lax.axis_index("depth"))
    widen(rig, rw)
    step_scale(rho, scale)
    lane = lane_of()
    has = [(i > 0).astype(F32) for i in index]
    for half in range(2):
        rows = pl.ds(8 * half, 8)
        mx[rows, :] = (xu[pl.ds(96 + 8 * half, 8), :] + np.float32(KAPPA * D[4, 4]) * rw[x_rows(0, half), :]) * has[0]
    my[...] = (yu[pl.ds(48, 8), :] + np.float32(KAPPA * D[4, 4]) * rw[y_rows(0), :]) * has[1]
    own, above = zd_own[...], zu[...]
    r_first = from_fourth(own, lane)
    scale_z = (from_fourth(above, lane) + np.float32(KAPPA * D[4, 4]) * r_first) * has[2]
    mz[...] = scale_z
    closing_z = above + np.float32(KAPPA) * r_first * rolled(above, 64) + scale_z * own
    kappa = np.float32(KAPPA)

    def low_x(c, offset, plane, v0):
        rows = pl.ds(pl.multiple_of(offset, 8), 8)
        grad = xu[pl.ds(pl.multiple_of(48 + 16 * c + offset, 8), 8), :]
        return xu[plane, :] + kappa * rw[rows, :] * grad + mx[rows, :] * v0

    def low_y(c, v0):
        grad = yu[pl.ds(pl.multiple_of(24 + 8 * c, 8), 8), :]
        return yu[pl.ds(pl.multiple_of(8 * c, 8), 8), :] + kappa * rw[y_rows(0), :] * grad + my[...] * v0

    def store(c, x, rows, plane, after):
        out[c, rows, :] = after
        if x == 0:
            xd2[plane, :] = after

    def on_first(c, plane, carried, term):
        early[plane, :] = carried - term

    below = zd[...]
    advance(
        now, prev, rw, (low_x, low_y), (xd, yd), (xd.at[pl.ds(48, 16)], yd.at[pl.ds(24, 8)]), scale,
        below, rolled(below, -3), closing_z, index, store, acc, on_first,
    )

    on_one, on_two = index[0] == middle - 1, index[0] == middle
    for half in range(2):
        rows = pl.ds(8 * half, 8)
        r = [rw[x_rows(x, half), :] for x in range(8)] + [xd[pl.ds(48 + 8 * half, 8), :]]
        y_pos = lax.broadcasted_iota(jnp.int32, (8, NZL), 0) + 8 * half
        face = axis_weight(y_pos, index[1] == 0) * axis_weight(lane, index[2] == 0) * np.float32(W0)
        for c in range(3):
            plane = pl.ds(16 * c + 8 * half, 8)
            v = [out[c, x_rows(x, half), :] for x in range(8)]
            part, grad = open_terms(v[4:], r[4:8])
            sent = part + kappa * r[8] * grad
            xu2[plane, :] = sent
            here = early[plane, :] + mx[rows, :] * v[0] - first_term(v[:5], r[:5])
            slip[plane, :] = face * jnp.where(on_one, sent, jnp.where(on_two, here, 0.0))
    r = [rw[y_rows(12 + a), :] for a in range(4)]
    for c in range(3):
        part, grad = open_terms([out[c, y_rows(12 + a), :] for a in range(4)], r)
        yu2[pl.ds(8 * c, 8), :] = part + kappa * yd[pl.ds(24, 8), :] * grad
        yd2[pl.ds(8 * c, 8), :] = out[c, y_rows(0), :]
    back = lambda t: [rolled(t, 3 - a) for a in range(4)]
    r = back(last_lanes(lambda rows: rw[rows, :], lane))
    sent = []
    for c in range(3):
        part, grad = open_terms(back(last_lanes(lambda rows: out[c, rows, :], lane)), r)
        sent.append(part + kappa * below * grad)
    zu2[...] = interleaved(sent + [None], lane, 0)
    zd2[...] = first_lanes(lambda c, rows: out[c, rows, :], None, lane)


def second_kernel(
    now, prev, rig, rho, xu2, xd2, yu2, yd2, zu2, zd2, zd2_own, mx, my, mz, xd, yd, zd,
    out, rw, scale, acc,
):
    index = (lax.axis_index("normal"), lax.axis_index("strike"), lax.axis_index("depth"))
    widen(rig, rw)
    step_scale(rho, scale)
    closing_z = zu2[...] + mz[...] * zd2_own[...]

    def low_x(c, offset, plane, v0):
        return xu2[plane, :] + mx[pl.ds(pl.multiple_of(offset, 8), 8), :] * v0

    def low_y(c, v0):
        return yu2[pl.ds(pl.multiple_of(8 * c, 8), 8), :] + my[...] * v0

    def store(c, x, rows, plane, after):
        out[c, rows, :] = after

    advance(
        now, prev, rw, (low_x, low_y), (xd2, yd2), (xd.at[pl.ds(48, 16)], yd.at[pl.ds(24, 8)]), scale,
        zd2[...], rolled(zd[...], -3), closing_z, index, store, acc, lambda *args: None,
    )


def patch_kernel(copies, count_d, count_s, slip, nodes, ids, out):
    pairs = nodes.shape[-1]
    node = nodes[...]
    hot_z = (lax.broadcasted_iota(jnp.int32, (NZL, pairs), 0) == (node & (NZL - 1))).astype(F32)
    at_z = jnp.dot(slip[...], hot_z, precision=HIGHEST, preferred_element_type=F32)
    row_y = lax.broadcasted_iota(jnp.int32, (NYL, pairs), 0) == (node >> 7)
    patch = ids[...]
    owner = patch >> 1
    owner_d = owner & (count_d - 1)
    slot = ((owner >> (count_d.bit_length() - 1)) << 1) + (patch & 1)
    hot_slot = lax.broadcasted_iota(jnp.int32, (32, pairs), 0) == slot
    spread = []
    for c in range(3):
        picked = jnp.sum(jnp.where(row_y, at_z[NYL * c : NYL * (c + 1), :], 0.0), axis=0, keepdims=True)
        spread.append(jnp.where(hot_slot, picked, 0.0))
    spread.append(jnp.zeros((32, pairs), F32))
    hot_d = (lax.broadcasted_iota(jnp.int32, (8, pairs), 0) == owner_d).astype(F32)
    tile = lax.dot_general(
        hot_d, jnp.concatenate(spread, axis=0), (((1,), (1,)), ((), ())), precision=HIGHEST,
        preferred_element_type=F32,
    )
    for n in range(copies):
        out[pl.ds(count_d * n, count_d), :] = tile[:count_d, :]


def final_kernel(tiles, out):
    mine = lax.axis_index("strike") * 2
    summed = jnp.sum(tiles[...], axis=0, keepdims=True)
    lane = lax.broadcasted_iota(jnp.int32, (2, NZL), 1)
    place = lax.broadcasted_iota(jnp.int32, (2, NZL), 0)
    for c in range(3):
        hit = lane == 32 * c + mine + place
        out[:, pl.ds(c, 1)] = jnp.sum(jnp.where(hit, summed, 0.0), axis=1, keepdims=True)


def call(kernel, name, outs, scratch=(), flops=0, moved=0):
    return pl.pallas_call(
        kernel,
        out_shape=[jax.ShapeDtypeStruct(shape, F32) for shape in outs],
        scratch_shapes=[pltpu.VMEM(shape, F32) for shape in scratch],
        compiler_params=pltpu.CompilerParams(vmem_limit_bytes=16 * 2**20),
        cost_estimate=pl.CostEstimate(flops=flops, bytes_accessed=moved, transcendentals=0),
        name=name,
    )


def upward(value, axis):
    count = lax.axis_size(axis)
    return lax.ppermute(value, axis, [(i, i + 1) for i in range(count - 1)])


def downward(value, axis):
    count = lax.axis_size(axis)
    return lax.ppermute(value, axis, [(i + 1, i) for i in range(count - 1)])


def exchange(messages):
    axes = ("normal", "normal", "strike", "strike", "depth", "depth")
    return [
        (upward if i % 2 == 0 else downward)(message, axis) for i, (message, axis) in enumerate(zip(messages, axes))
    ]


def local(field_now, field_prev, rigidity, density, fault_nodes, patch_ids):
    count_n, count_s, count_d = (lax.axis_size(a) for a in ("normal", "strike", "depth"))
    flat = (3, ROWS, NZL)
    now, prev = field_now.reshape(flat), field_prev.reshape(flat)
    rig, rho = rigidity.reshape(ROWS, NZL), density.reshape(ROWS, NZL)
    sent = call(
        pack_kernel, "pack", [(112, NZL), (64, NZL), (56, NZL), (32, NZL), (8, NZL), (8, NZL)], [(ROWS, NZL)],
        flops=2_000_000, moved=400_000,
    )(now, rig)
    got = exchange(sent)
    mid, *rest = call(
        functools.partial(first_kernel, count_n // 2), "first",
        [flat, (48, NZL), (48, NZL), (24, NZL), (24, NZL), (8, NZL), (8, NZL), (16, NZL), (8, NZL), (8, NZL), (48, NZL)],
        [(ROWS, NZL), (ROWS, NZL), flat, (48, NZL)], flops=10_000_000, moved=900_000,
    )(now, prev, rig, rho, *got, sent[5])
    sent2, weights, slip = rest[:6], rest[6:9], rest[9]
    got2 = exchange(sent2)
    nodes, ids = fault_nodes.reshape(1, -1), patch_ids.reshape(1, -1)
    (tiles,) = call(
        functools.partial(patch_kernel, count_n, count_d, count_s), "patch", [(count_n * count_d, NZL)],
        flops=10_000_000, moved=60_000,
    )(slip, nodes, ids)
    tiles = lax.all_to_all(tiles, ("normal", "depth"), 0, 0, tiled=True)
    row = jnp.sum(tiles, axis=0, keepdims=True)
    rows = lax.all_to_all(jnp.broadcast_to(row, (count_s, NZL)), "strike", 0, 0, tiled=True)
    (share,) = call(final_kernel, "final", [(2, 3)], flops=10_000, moved=10_000)(rows)
    (following,) = call(
        second_kernel, "second", [flat], [(ROWS, NZL), (ROWS, NZL), flat], flops=10_000_000, moved=900_000,
    )(mid, now, rig, rho, *got2, sent2[5], *weights, got[1], got[3], got[5])
    return following.reshape(field_now.shape), mid.reshape(field_now.shape), share


def solution(mesh):
    field = P(None, "normal", "strike", "depth")
    cells = P("normal", "strike", "depth")
    pairs = P("strike", "depth", None)
    return jax.shard_map(
        local,
        mesh=mesh,
        in_specs=(field, field, cells, cells, pairs, pairs),
        out_specs=(field, field, P(("strike", "depth"), None)),
        check_vma=False,
    )
```

```python
import functools
import math

import jax
import jax.numpy as jnp
import numpy as np
from jax import lax
from jax.experimental import pallas as pl
from jax.experimental.pallas import tpu as pltpu
from jax.sharding import PartitionSpec as P

DT = 0.03
NXL, NYL, NZL = 8, 16, 128
ROWS = NXL * NYL
F32 = jnp.float32
HIGHEST = lax.Precision.HIGHEST


def gll_tables():
    spread = math.sqrt(3.0 / 7.0)
    points = np.array([-1.0, -spread, 0.0, spread, 1.0])
    weights = np.array([0.1, 49.0 / 90.0, 32.0 / 45.0, 49.0 / 90.0, 0.1]) * 0.5
    derivative = np.zeros((5, 5))
    for b in range(5):
        for a in range(5):
            if a == b:
                derivative[b, a] = sum(1.0 / (points[b] - points[o]) for o in range(5) if o != b)
            else:
                row = np.prod([points[b] - points[o] for o in range(5) if o != b and o != a])
                col = np.prod([points[a] - points[o] for o in range(5) if o != a and o != b])
                derivative[b, a] = row / (col * (points[a] - points[b]))
    return weights, 2.0 * derivative


WQ, D = gll_tables()
W0 = float(WQ[0])
NODE_W = np.array([2 * WQ[0], WQ[1], WQ[2], WQ[3], 2 * WQ[0]])
E = (WQ[:, None] * D).T / NODE_W[:, None]
KAPPA = float(E[4, 4])


def total(pairs):
    acc = None
    for const, arr in pairs:
        if abs(const) < 1e-12:
            continue
        term = arr * np.float32(const)
        acc = term if acc is None else acc + term
    return acc


def element(v, r):
    twice = v[2] + v[2]
    s0, s1 = v[0] + v[4] - twice, v[1] + v[3] - twice
    d0, d1 = v[0] - v[4], v[1] - v[3]
    ev = [total([((D[b, 0] + D[b, 4]) / 2, s0), ((D[b, 1] + D[b, 3]) / 2, s1)]) for b in (0, 1)]
    od = [total([((D[b, 0] - D[b, 4]) / 2, d0), ((D[b, 1] - D[b, 3]) / 2, d1)]) for b in (0, 1)]
    g2 = total([(D[2, 0], d0), (D[2, 1], d1)])
    q = [r[0] * (od[0] + ev[0]), r[1] * (od[1] + ev[1]), r[2] * g2, r[3] * (od[1] - ev[1]), r[4] * (od[0] - ev[0])]
    p0, m0, p1, m1 = q[0] + q[4], q[0] - q[4], q[1] + q[3], q[1] - q[3]
    ec = [total([((E[a, 0] + E[a, 4]) / 2, p0), ((E[a, 1] + E[a, 3]) / 2, p1), (E[a, 2], q[2])]) for a in (0, 1)]
    oc = [total([((E[a, 0] - E[a, 4]) / 2, m0), ((E[a, 1] - E[a, 3]) / 2, m1)]) for a in (0, 1)]
    c2 = total([(E[2, 0], m0), (E[2, 1], m1)])
    return [oc[0] + ec[0], oc[1] + ec[1], c2, oc[1] - ec[1], oc[0] - ec[0]]


def first_term(v, r):
    twice = v[2] + v[2]
    s0, s1 = v[0] + v[4] - twice, v[1] + v[3] - twice
    d0, d1 = v[0] - v[4], v[1] - v[3]
    ev = [total([((D[b, 0] + D[b, 4]) / 2, s0), ((D[b, 1] + D[b, 3]) / 2, s1)]) for b in (0, 1)]
    od = [total([((D[b, 0] - D[b, 4]) / 2, d0), ((D[b, 1] - D[b, 3]) / 2, d1)]) for b in (0, 1)]
    g2 = total([(D[2, 0], d0), (D[2, 1], d1)])
    q = [r[0] * (od[0] + ev[0]), r[1] * (od[1] + ev[1]), r[2] * g2, r[3] * (od[1] - ev[1]), r[4] * (od[0] - ev[0])]
    return total([(E[0, b], q[b]) for b in range(5)])


def open_terms(v, r):
    flux = [r[b] * total([(D[b, a], v[a]) for a in range(4)]) for b in range(4)]
    part = total([(E[4, b], flux[b]) for b in range(4)])
    grad = total([(D[4, a], v[a]) for a in range(4)])
    return part, grad


def open_scale(r):
    return total([(E[4, b] * D[b, 4], r[b]) for b in range(4)])


def rolled(x, shift):
    shift = shift % NZL
    return x if shift == 0 else pltpu.roll(x, shift, 1)


def lane_of():
    return lax.broadcasted_iota(jnp.int32, (8, NZL), 1)


def lane_table(phase, values):
    out = jnp.full((8, NZL), np.float32(values[0]), F32)
    for b in range(1, 4):
        out = jnp.where(phase == b, np.float32(values[b]), out)
    return out


def x_rows(x, half):
    return pl.ds(x * NYL + half * 8, 8)


def y_rows(y):
    return pl.ds(y, 8, stride=NYL)


def first_lanes(read, read_r, lane):
    out = jnp.zeros((8, NZL), F32)
    for k in range(16):
        rows = pl.ds(8 * k, 8)
        for c in range(3 if read_r is None else 4):
            src = read_r(rows) if c == 3 else read(c, rows)
            out = jnp.where(lane == 4 * k + c, rolled(src, 4 * k + c), out)
    return out


def last_lanes(read, lane):
    out = jnp.zeros((8, NZL), F32)
    for k in range(16):
        out = jnp.where((lane >> 2) == k, rolled(read(pl.ds(8 * k, 8)), 4 * k + 4), out)
    return out


def interleaved(parts, lane, base):
    out = jnp.zeros((8, NZL), F32)
    for j, part in enumerate(parts):
        if part is None:
            continue
        out = jnp.where((lane >= base) & (lane < base + 64) & ((lane & 3) == j), rolled(part, base + j - 3), out)
    return out


def widen(src, dst):
    for x in range(NXL):
        dst[pl.ds(x * NYL, NYL), :] = src[pl.ds(x * NYL, NYL), :].astype(F32)


def sides(ref, up, down):
    return ref.at[pl.ds(0, up)], ref.at[pl.ds(up, down)]


def neighbours(gathered, index, count, up, down, low, high):
    below = pl.multiple_of(jnp.maximum(index - 1, 0) * (up + down), 8)
    above = pl.multiple_of(jnp.minimum(index + 1, count - 1) * (up + down) + up, 8)
    low[...] = jnp.where(index > 0, gathered[pl.ds(below, up), :], 0.0)
    high[...] = jnp.where(index < count - 1, gathered[pl.ds(above, down), :], 0.0)


FIRST_ROWS = ((112, 64), (56, 32), (8, 8))
SECOND_ROWS = ((48, 48), (24, 24), (8, 8))


def pack_kernel(now, rig, hx, hy, hz, rw):
    (xu, xd), (yu, yd), (zu, zd) = (sides(ref, *n) for ref, n in zip((hx, hy, hz), FIRST_ROWS))
    widen(rig, rw)
    lane = lane_of()
    for half in range(2):
        r = [rw[x_rows(4 + a, half), :] for a in range(4)]
        xu[pl.ds(96 + 8 * half, 8), :] = open_scale(r)
        xd[pl.ds(48 + 8 * half, 8), :] = rw[x_rows(0, half), :]
        for c in range(3):
            part, grad = open_terms([now[c, x_rows(4 + a, half), :] for a in range(4)], r)
            xu[pl.ds(16 * c + 8 * half, 8), :] = part
            xu[pl.ds(48 + 16 * c + 8 * half, 8), :] = grad
            xd[pl.ds(16 * c + 8 * half, 8), :] = now[c, x_rows(0, half), :]
    r = [rw[y_rows(12 + a), :] for a in range(4)]
    yu[pl.ds(48, 8), :] = open_scale(r)
    yd[pl.ds(24, 8), :] = rw[y_rows(0), :]
    for c in range(3):
        part, grad = open_terms([now[c, y_rows(12 + a), :] for a in range(4)], r)
        yu[pl.ds(8 * c, 8), :] = part
        yu[pl.ds(24 + 8 * c, 8), :] = grad
        yd[pl.ds(8 * c, 8), :] = now[c, y_rows(0), :]
    back = lambda t: [rolled(t, 3 - a) for a in range(4)]
    r = back(last_lanes(lambda rows: rw[rows, :], lane))
    parts, grads = [], []
    for c in range(3):
        part, grad = open_terms(back(last_lanes(lambda rows: now[c, rows, :], lane)), r)
        parts.append(part)
        grads.append(grad)
    zu[...] = jnp.where(
        lane < 64, interleaved(parts + [open_scale(r)], lane, 0), interleaved(grads + [None], lane, 64)
    )
    zd[...] = first_lanes(lambda c, rows: now[c, rows, :], lambda rows: rw[rows, :], lane)


def from_fourth(tile, lane):
    phase = lane & 3
    out = tile
    for j in range(3):
        out = jnp.where(phase == j, rolled(tile, j - 3), out)
    return out


def advance(now, prev, rw, low, high_v, high_r, scale, ghost_z, ghost_rz, closing_z, index, store, acc, on_first):
    index_x, index_y, index_z = index
    at_x = jnp.where(index_x == 0, 2.0, 1.0).astype(F32)
    at_y = jnp.where(index_y == 0, 2.0, 1.0).astype(F32)
    at_z = jnp.where(index_z == 0, 2.0, 1.0).astype(F32)

    def along_y(c, carry):
        v = [now[c, y_rows(y), :] for y in range(NYL)] + [high_v[1][pl.ds(8 * c, 8), :]]
        r = [rw[y_rows(y), :] for y in range(NYL)] + [high_r[1][...]]
        carried = low[1](c, v[0])
        for e in range(4):
            terms = element(v[4 * e : 4 * e + 5], r[4 * e : 4 * e + 5])
            head = terms[0] * at_y if e == 0 else terms[0]
            acc[c, y_rows(4 * e), :] = head + carried
            for a in range(1, 4):
                acc[c, y_rows(4 * e + a), :] = terms[a]
            carried = terms[4]
        return carry

    lax.fori_loop(0, 3, along_y, 0)

    lane = lane_of()
    phase = lane & 3
    gm = [lane_table(phase, [D[b, b - k] if b >= k else 0 for b in range(4)]) for k in range(4)]
    gp = [None] + [lane_table(phase, [D[b, b + k] if b + k <= 4 else 0 for b in range(4)]) for k in range(1, 5)]
    cm = [lane_table(phase, [E[a, a - k] if a >= k else 0 for a in range(4)]) for k in range(4)]
    cp = [None] + [lane_table(phase, [E[a, a + k] if a + k <= 3 else 0 for a in range(4)]) for k in range(1, 4)]
    c_close = lane_table(phase, [E[a, 4] for a in range(4)])
    last = [lane_table(phase, [0, 0, 0, E[4, b]]) for b in range(5)]
    first = lane == 0
    edge = jnp.where(first, at_z, jnp.float32(1.0))

    def along_xz(n, carry):
        c, half = n >> 1, n & 1
        offset = half * 8
        rows = [pl.ds(pl.multiple_of(x * NYL + offset, 8), 8) for x in range(NXL)]
        plane = pl.ds(pl.multiple_of(16 * c + offset, 8), 8)
        v = [now[c, rows[x], :] for x in range(NXL)] + [high_v[0][plane, :]]
        r = [rw[rows[x], :] for x in range(NXL)] + [high_r[0][pl.ds(pl.multiple_of(offset, 8), 8), :]]
        carried = low[0](c, offset, plane, v[0])
        back = NZL - (4 * half + c)
        ghost_v = pltpu.roll(ghost_z, back, 1)
        ghost_r = pltpu.roll(ghost_rz, NZL - 4 * half, 1)
        closing = pltpu.roll(closing_z, back, 1)
        for e in range(2):
            terms = element(v[4 * e : 4 * e + 5], r[4 * e : 4 * e + 5])
            if e == 0:
                on_first(c, plane, carried, terms[0])
            for a in range(4):
                x = 4 * e + a
                force = terms[a] + acc[c, rows[x], :]
                if a == 0:
                    force = (terms[0] * at_x if e == 0 else terms[0]) + carried + acc[c, rows[x], :]
                vx = jnp.where(first, rolled(ghost_v, -8 * x), v[x])
                rx = jnp.where(first, rolled(ghost_r, -8 * x), r[x])
                vm = [v[x]] + [rolled(v[x], k) for k in range(1, 4)]
                vp = [None] + [rolled(vx, -k) for k in range(1, 5)]
                g = gm[0] * v[x]
                for k in range(1, 4):
                    g = g + gm[k] * vm[k]
                for k in range(1, 5):
                    g = g + gp[k] * vp[k]
                g4 = total([(D[4, 0], vm[3]), (D[4, 1], vm[2]), (D[4, 2], vm[1]), (D[4, 3], vm[0]), (D[4, 4], vp[1])])
                q = r[x] * g
                q4 = jnp.where(phase == 3, rolled(rx, -1) * g4, 0.0)
                qm = [q] + [rolled(q, k) for k in range(1, 4)]
                own = cm[0] * q
                for k in range(1, 4):
                    own = own + cm[k] * qm[k]
                for k in range(1, 4):
                    own = own + cp[k] * rolled(q, -k)
                pair = q4 + rolled(q4, -1)
                own = own + c_close * (pair + rolled(pair, -2))
                tail = last[3] * q + last[4] * q4
                for b in range(3):
                    tail = tail + last[b] * qm[3 - b]
                tail = jnp.where(first, rolled(closing, -8 * x), rolled(tail, 1))
                force = force + own * edge + tail
                after = (v[x] + v[x]) - prev[c, rows[x], :] - scale[rows[x], :] * force
                store(c, x, rows[x], plane, after)
            carried = terms[4]
        return carry

    lax.fori_loop(0, 6, along_xz, 0)


def step_scale(rho, scale):
    for x in range(NXL):
        rows = pl.ds(x * NYL, NYL)
        scale[rows, :] = np.float32(DT * DT) / rho[rows, :].astype(F32)


def axis_weight(pos, is_first):
    phase = pos & 3
    out = jnp.full(pos.shape, np.float32(2 * W0), F32)
    for b in range(1, 4):
        out = jnp.where(phase == b, np.float32(WQ[b]), out)
    return jnp.where((pos == 0) & is_first, np.float32(W0), out)


def first_kernel(
    counts, now, prev, rig, rho, gx, gy, gz, hz,
    out, hx2, hy2, hz2, mx, my, mz, slip, xd, yd, zd,
    rw, scale, acc, early, xu, yu, zu,
):
    middle = counts[0] // 2
    index = (lax.axis_index("normal"), lax.axis_index("strike"), lax.axis_index("depth"))
    for d, (ref, low, high) in enumerate(((gx, xu, xd), (gy, yu, yd), (gz, zu, zd))):
        neighbours(ref, index[d], counts[d], *FIRST_ROWS[d], low, high)
    zd_own = hz.at[pl.ds(8, 8)]
    (xu2, xd2), (yu2, yd2), (zu2, zd2) = (sides(ref, *n) for ref, n in zip((hx2, hy2, hz2), SECOND_ROWS))
    widen(rig, rw)
    step_scale(rho, scale)
    lane = lane_of()
    has = [(i > 0).astype(F32) for i in index]
    for half in range(2):
        rows = pl.ds(8 * half, 8)
        mx[rows, :] = (xu[pl.ds(96 + 8 * half, 8), :] + np.float32(KAPPA * D[4, 4]) * rw[x_rows(0, half), :]) * has[0]
    my[...] = (yu[pl.ds(48, 8), :] + np.float32(KAPPA * D[4, 4]) * rw[y_rows(0), :]) * has[1]
    own, above = zd_own[...], zu[...]
    r_first = from_fourth(own, lane)
    scale_z = (from_fourth(above, lane) + np.float32(KAPPA * D[4, 4]) * r_first) * has[2]
    mz[...] = scale_z
    closing_z = above + np.float32(KAPPA) * r_first * rolled(above, 64) + scale_z * own
    kappa = np.float32(KAPPA)

    def low_x(c, offset, plane, v0):
        rows = pl.ds(pl.multiple_of(offset, 8), 8)
        grad = xu[pl.ds(pl.multiple_of(48 + 16 * c + offset, 8), 8), :]
        return xu[plane, :] + kappa * rw[rows, :] * grad + mx[rows, :] * v0

    def low_y(c, v0):
        grad = yu[pl.ds(pl.multiple_of(24 + 8 * c, 8), 8), :]
        return yu[pl.ds(pl.multiple_of(8 * c, 8), 8), :] + kappa * rw[y_rows(0), :] * grad + my[...] * v0

    def store(c, x, rows, plane, after):
        out[c, rows, :] = after
        if x == 0:
            xd2[plane, :] = after

    def on_first(c, plane, carried, term):
        early[plane, :] = carried - term

    below = zd[...]
    advance(
        now, prev, rw, (low_x, low_y), (xd, yd), (xd.at[pl.ds(48, 16)], yd.at[pl.ds(24, 8)]), scale,
        below, rolled(below, -3), closing_z, index, store, acc, on_first,
    )

    on_one, on_two = index[0] == middle - 1, index[0] == middle
    for half in range(2):
        rows = pl.ds(8 * half, 8)
        r = [rw[x_rows(x, half), :] for x in range(8)] + [xd[pl.ds(48 + 8 * half, 8), :]]
        y_pos = lax.broadcasted_iota(jnp.int32, (8, NZL), 0) + 8 * half
        face = axis_weight(y_pos, index[1] == 0) * axis_weight(lane, index[2] == 0) * np.float32(W0)
        for c in range(3):
            plane = pl.ds(16 * c + 8 * half, 8)
            v = [out[c, x_rows(x, half), :] for x in range(8)]
            part, grad = open_terms(v[4:], r[4:8])
            sent = part + kappa * r[8] * grad
            xu2[plane, :] = sent
            here = early[plane, :] + mx[rows, :] * v[0] - first_term(v[:5], r[:5])
            slip[plane, :] = face * jnp.where(on_one, sent, jnp.where(on_two, here, 0.0))
    r = [rw[y_rows(12 + a), :] for a in range(4)]
    for c in range(3):
        part, grad = open_terms([out[c, y_rows(12 + a), :] for a in range(4)], r)
        yu2[pl.ds(8 * c, 8), :] = part + kappa * yd[pl.ds(24, 8), :] * grad
        yd2[pl.ds(8 * c, 8), :] = out[c, y_rows(0), :]
    back = lambda t: [rolled(t, 3 - a) for a in range(4)]
    r = back(last_lanes(lambda rows: rw[rows, :], lane))
    sent = []
    for c in range(3):
        part, grad = open_terms(back(last_lanes(lambda rows: out[c, rows, :], lane)), r)
        sent.append(part + kappa * below * grad)
    zu2[...] = interleaved(sent + [None], lane, 0)
    zd2[...] = first_lanes(lambda c, rows: out[c, rows, :], None, lane)


def second_kernel(
    counts, now, prev, rig, rho, gx, gy, gz, hz, mx, my, mz, xd, yd, zd,
    out, rw, scale, acc, xu2, xd2, yu2, yd2, zu2, zd2,
):
    index = (lax.axis_index("normal"), lax.axis_index("strike"), lax.axis_index("depth"))
    for d, (ref, low, high) in enumerate(((gx, xu2, xd2), (gy, yu2, yd2), (gz, zu2, zd2))):
        neighbours(ref, index[d], counts[d], *SECOND_ROWS[d], low, high)
    zd2_own = hz.at[pl.ds(8, 8)]
    widen(rig, rw)
    step_scale(rho, scale)
    closing_z = zu2[...] + mz[...] * zd2_own[...]

    def low_x(c, offset, plane, v0):
        return xu2[plane, :] + mx[pl.ds(pl.multiple_of(offset, 8), 8), :] * v0

    def low_y(c, v0):
        return yu2[pl.ds(pl.multiple_of(8 * c, 8), 8), :] + my[...] * v0

    def store(c, x, rows, plane, after):
        out[c, rows, :] = after

    advance(
        now, prev, rw, (low_x, low_y), (xd2, yd2), (xd.at[pl.ds(48, 16)], yd.at[pl.ds(24, 8)]), scale,
        zd2[...], rolled(zd[...], -3), closing_z, index, store, acc, lambda *args: None,
    )


def patch_kernel(count_d, slip, nodes, ids, out):
    pairs = nodes.shape[-1]
    node = nodes[...]
    hot_z = (lax.broadcasted_iota(jnp.int32, (NZL, pairs), 0) == (node & (NZL - 1))).astype(F32)
    at_z = jnp.dot(slip[...], hot_z, precision=HIGHEST, preferred_element_type=F32)
    row_y = lax.broadcasted_iota(jnp.int32, (NYL, pairs), 0) == (node >> 7)
    patch = ids[...]
    owner = patch >> 1
    owner_d = owner & (count_d - 1)
    slot = ((owner >> (count_d.bit_length() - 1)) << 1) + (patch & 1)
    hot_slot = lax.broadcasted_iota(jnp.int32, (32, pairs), 0) == slot
    spread = []
    for c in range(3):
        picked = jnp.sum(jnp.where(row_y, at_z[NYL * c : NYL * (c + 1), :], 0.0), axis=0, keepdims=True)
        spread.append(jnp.where(hot_slot, picked, 0.0))
    spread.append(jnp.zeros((32, pairs), F32))
    hot_d = (lax.broadcasted_iota(jnp.int32, (8, pairs), 0) == owner_d).astype(F32)
    out[...] = lax.dot_general(
        hot_d, jnp.concatenate(spread, axis=0), (((1,), (1,)), ((), ())), precision=HIGHEST,
        preferred_element_type=F32,
    )


def final_kernel(tiles, out):
    mine = lax.axis_index("strike") * 2
    row = lax.broadcasted_iota(jnp.int32, (8, NZL), 0) == lax.axis_index("depth")
    summed = jnp.sum(jnp.where(row, tiles[...], 0.0), axis=0, keepdims=True)
    lane = lax.broadcasted_iota(jnp.int32, (2, NZL), 1)
    place = lax.broadcasted_iota(jnp.int32, (2, NZL), 0)
    for c in range(3):
        hit = lane == 32 * c + mine + place
        out[:, pl.ds(c, 1)] = jnp.sum(jnp.where(hit, summed, 0.0), axis=1, keepdims=True)


def call(kernel, name, outs, scratch=(), flops=0, moved=0):
    return pl.pallas_call(
        kernel,
        out_shape=[jax.ShapeDtypeStruct(shape, F32) for shape in outs],
        scratch_shapes=[pltpu.VMEM(shape, F32) for shape in scratch],
        compiler_params=pltpu.CompilerParams(vmem_limit_bytes=16 * 2**20),
        cost_estimate=pl.CostEstimate(flops=flops, bytes_accessed=moved, transcendentals=0),
        name=name,
    )


def exchange(messages):
    return [
        lax.all_gather(message, axis, axis=0, tiled=True)
        for message, axis in zip(messages, ("normal", "strike", "depth"))
    ]


def local(field_now, field_prev, rigidity, density, fault_nodes, patch_ids):
    axes = ("normal", "strike", "depth")
    counts = tuple(lax.axis_size(a) for a in axes)
    flat = (3, ROWS, NZL)
    now, prev = field_now.reshape(flat), field_prev.reshape(flat)
    rig, rho = rigidity.reshape(ROWS, NZL), density.reshape(ROWS, NZL)
    first_sizes = [(up + down, NZL) for up, down in FIRST_ROWS]
    second_sizes = [(up + down, NZL) for up, down in SECOND_ROWS]
    sent = call(pack_kernel, "pack", first_sizes, [(ROWS, NZL)], flops=2_000_000, moved=400_000)(now, rig)
    got = exchange(sent)
    mid, *rest = call(
        functools.partial(first_kernel, counts), "first",
        [flat] + second_sizes + [(16, NZL), (8, NZL), (8, NZL), (48, NZL)] + [(n[1], NZL) for n in FIRST_ROWS],
        [(ROWS, NZL), (ROWS, NZL), flat, (48, NZL)] + [(n[0], NZL) for n in FIRST_ROWS],
        flops=10_000_000, moved=900_000,
    )(now, prev, rig, rho, *got, sent[2])
    sent2, weights, slip, kept = rest[:3], rest[3:6], rest[6], rest[7:]
    nodes, ids = fault_nodes.reshape(1, -1), patch_ids.reshape(1, -1)
    (tile,) = call(
        functools.partial(patch_kernel, counts[2]), "patch", [(8, NZL)], flops=10_000_000, moved=60_000,
    )(slip, nodes, ids)
    sums = lax.psum(tile, axes)
    got2 = exchange(sent2)
    (share,) = call(final_kernel, "final", [(2, 3)], flops=10_000, moved=10_000)(sums)
    (following,) = call(
        functools.partial(second_kernel, counts), "second", [flat],
        [(ROWS, NZL), (ROWS, NZL), flat] + [(n, NZL) for pair in SECOND_ROWS for n in pair],
        flops=10_000_000, moved=900_000,
    )(mid, now, rig, rho, *got2, sent2[2], *weights, *kept)
    return following.reshape(field_now.shape), mid.reshape(field_now.shape), share


def solution(mesh):
    field = P(None, "normal", "strike", "depth")
    cells = P("normal", "strike", "depth")
    pairs = P("strike", "depth", None)
    return jax.shard_map(
        local,
        mesh=mesh,
        in_specs=(field, field, cells, cells, pairs, pairs),
        out_specs=(field, field, P(("strike", "depth"), None)),
        check_vma=False,
    )
```

```python
import functools
import math

import jax
import jax.numpy as jnp
import numpy as np
from jax import lax
from jax.experimental import pallas as pl
from jax.experimental.pallas import tpu as pltpu
from jax.sharding import PartitionSpec as P

DT = 0.03
NXL, NYL, NZL = 8, 16, 128
ROWS = NXL * NYL
F32 = jnp.float32
HIGHEST = lax.Precision.HIGHEST


def gll_tables():
    spread = math.sqrt(3.0 / 7.0)
    points = np.array([-1.0, -spread, 0.0, spread, 1.0])
    weights = np.array([0.1, 49.0 / 90.0, 32.0 / 45.0, 49.0 / 90.0, 0.1]) * 0.5
    derivative = np.zeros((5, 5))
    for b in range(5):
        for a in range(5):
            if a == b:
                derivative[b, a] = sum(1.0 / (points[b] - points[o]) for o in range(5) if o != b)
            else:
                row = np.prod([points[b] - points[o] for o in range(5) if o != b and o != a])
                col = np.prod([points[a] - points[o] for o in range(5) if o != a and o != b])
                derivative[b, a] = row / (col * (points[a] - points[b]))
    return weights, 2.0 * derivative


WQ, D = gll_tables()
W0 = float(WQ[0])
NODE_W = np.array([2 * WQ[0], WQ[1], WQ[2], WQ[3], 2 * WQ[0]])
E = (WQ[:, None] * D).T / NODE_W[:, None]
KAPPA = float(E[4, 4])


def total(pairs):
    acc = None
    for const, arr in pairs:
        if abs(const) < 1e-12:
            continue
        term = arr * np.float32(const)
        acc = term if acc is None else acc + term
    return acc


def element(v, r):
    twice = v[2] + v[2]
    s0, s1 = v[0] + v[4] - twice, v[1] + v[3] - twice
    d0, d1 = v[0] - v[4], v[1] - v[3]
    ev = [total([((D[b, 0] + D[b, 4]) / 2, s0), ((D[b, 1] + D[b, 3]) / 2, s1)]) for b in (0, 1)]
    od = [total([((D[b, 0] - D[b, 4]) / 2, d0), ((D[b, 1] - D[b, 3]) / 2, d1)]) for b in (0, 1)]
    g2 = total([(D[2, 0], d0), (D[2, 1], d1)])
    q = [r[0] * (od[0] + ev[0]), r[1] * (od[1] + ev[1]), r[2] * g2, r[3] * (od[1] - ev[1]), r[4] * (od[0] - ev[0])]
    p0, m0, p1, m1 = q[0] + q[4], q[0] - q[4], q[1] + q[3], q[1] - q[3]
    ec = [total([((E[a, 0] + E[a, 4]) / 2, p0), ((E[a, 1] + E[a, 3]) / 2, p1), (E[a, 2], q[2])]) for a in (0, 1)]
    oc = [total([((E[a, 0] - E[a, 4]) / 2, m0), ((E[a, 1] - E[a, 3]) / 2, m1)]) for a in (0, 1)]
    c2 = total([(E[2, 0], m0), (E[2, 1], m1)])
    return [oc[0] + ec[0], oc[1] + ec[1], c2, oc[1] - ec[1], oc[0] - ec[0]]


def first_term(v, r):
    twice = v[2] + v[2]
    s0, s1 = v[0] + v[4] - twice, v[1] + v[3] - twice
    d0, d1 = v[0] - v[4], v[1] - v[3]
    ev = [total([((D[b, 0] + D[b, 4]) / 2, s0), ((D[b, 1] + D[b, 3]) / 2, s1)]) for b in (0, 1)]
    od = [total([((D[b, 0] - D[b, 4]) / 2, d0), ((D[b, 1] - D[b, 3]) / 2, d1)]) for b in (0, 1)]
    g2 = total([(D[2, 0], d0), (D[2, 1], d1)])
    q = [r[0] * (od[0] + ev[0]), r[1] * (od[1] + ev[1]), r[2] * g2, r[3] * (od[1] - ev[1]), r[4] * (od[0] - ev[0])]
    return total([(E[0, b], q[b]) for b in range(5)])


def open_terms(v, r):
    flux = [r[b] * total([(D[b, a], v[a]) for a in range(4)]) for b in range(4)]
    part = total([(E[4, b], flux[b]) for b in range(4)])
    grad = total([(D[4, a], v[a]) for a in range(4)])
    return part, grad


def open_scale(r):
    return total([(E[4, b] * D[b, 4], r[b]) for b in range(4)])


def rolled(x, shift):
    shift = shift % NZL
    return x if shift == 0 else pltpu.roll(x, shift, 1)


def lane_of():
    return lax.broadcasted_iota(jnp.int32, (8, NZL), 1)


def lane_table(phase, values):
    out = jnp.full((8, NZL), np.float32(values[0]), F32)
    for b in range(1, 4):
        out = jnp.where(phase == b, np.float32(values[b]), out)
    return out


def x_rows(x, half):
    return pl.ds(x * NYL + half * 8, 8)


def y_rows(y):
    return pl.ds(y, 8, stride=NYL)


def first_lanes(read, read_r, lane):
    out = jnp.zeros((8, NZL), F32)
    for k in range(16):
        rows = pl.ds(8 * k, 8)
        for c in range(3 if read_r is None else 4):
            src = read_r(rows) if c == 3 else read(c, rows)
            out = jnp.where(lane == 4 * k + c, rolled(src, 4 * k + c), out)
    return out


def last_lanes(read, lane):
    out = jnp.zeros((8, NZL), F32)
    for k in range(16):
        out = jnp.where((lane >> 2) == k, rolled(read(pl.ds(8 * k, 8)), 4 * k + 4), out)
    return out


def interleaved(parts, lane, base):
    out = jnp.zeros((8, NZL), F32)
    for j, part in enumerate(parts):
        if part is None:
            continue
        out = jnp.where((lane >= base) & (lane < base + 64) & ((lane & 3) == j), rolled(part, base + j - 3), out)
    return out


def widen(src, dst):
    for x in range(NXL):
        dst[pl.ds(x * NYL, NYL), :] = src[pl.ds(x * NYL, NYL), :].astype(F32)


FIRST_ROWS = ((112, 64), (56, 32), (8, 8))
SECOND_ROWS = ((48, 48), (24, 24), (8, 8))


def place():
    return tuple(lax.axis_index(axis) for axis in ("normal", "strike", "depth"))


def paired(index, up, down, near, far):
    even = (index & 1) == 0
    rows = pl.ds(0, down.shape[0])
    near[...] = up[...]
    far[...] = up[...]
    near[rows, :] = jnp.where(even, up[rows, :], down[...])
    far[rows, :] = jnp.where(even, down[...], up[rows, :])


def unpaired(index, near, far, low, high):
    even = (index & 1) == 0
    rows = pl.ds(0, high.shape[0])
    low[...] = jnp.where(even, far[...], near[...])
    high[...] = jnp.where(even, near[rows, :], far[rows, :])


def beside(index, count, got, stride, low, high):
    below = pl.multiple_of(jnp.maximum(index - 1, 0) * stride, 8)
    above = pl.multiple_of(jnp.minimum(index + 1, count - 1) * stride, 8)
    low[...] = jnp.where(index > 0, got[pl.ds(below, low.shape[0]), :], 0.0)
    high[...] = jnp.where(index < count - 1, got[pl.ds(above, high.shape[0]), :], 0.0)


def pack_kernel(
    now_hbm, rig_hbm, xa, xb, ya, yb, za, zb, zd, now, rig, rw, xu, xd, yu, yd, zu, sems,
):
    copies = [pltpu.make_async_copy(rig_hbm, rig, sems.at[0]), pltpu.make_async_copy(now_hbm, now, sems.at[1])]
    for copy in copies:
        copy.start()
    for copy in copies:
        copy.wait()
    widen(rig, rw)
    lane = lane_of()
    for half in range(2):
        r = [rw[x_rows(4 + a, half), :] for a in range(4)]
        xu[pl.ds(96 + 8 * half, 8), :] = open_scale(r)
        xd[pl.ds(48 + 8 * half, 8), :] = rw[x_rows(0, half), :]
        for c in range(3):
            part, grad = open_terms([now[c, x_rows(4 + a, half), :] for a in range(4)], r)
            xu[pl.ds(16 * c + 8 * half, 8), :] = part
            xu[pl.ds(48 + 16 * c + 8 * half, 8), :] = grad
            xd[pl.ds(16 * c + 8 * half, 8), :] = now[c, x_rows(0, half), :]
    r = [rw[y_rows(12 + a), :] for a in range(4)]
    yu[pl.ds(48, 8), :] = open_scale(r)
    yd[pl.ds(24, 8), :] = rw[y_rows(0), :]
    for c in range(3):
        part, grad = open_terms([now[c, y_rows(12 + a), :] for a in range(4)], r)
        yu[pl.ds(8 * c, 8), :] = part
        yu[pl.ds(24 + 8 * c, 8), :] = grad
        yd[pl.ds(8 * c, 8), :] = now[c, y_rows(0), :]
    back = lambda t: [rolled(t, 3 - a) for a in range(4)]
    r = back(last_lanes(lambda rows: rw[rows, :], lane))
    parts, grads = [], []
    for c in range(3):
        part, grad = open_terms(back(last_lanes(lambda rows: now[c, rows, :], lane)), r)
        parts.append(part)
        grads.append(grad)
    zu[...] = jnp.where(
        lane < 64, interleaved(parts + [open_scale(r)], lane, 0), interleaved(grads + [None], lane, 64)
    )
    zd[...] = first_lanes(lambda c, rows: now[c, rows, :], lambda rows: rw[rows, :], lane)
    index = place()
    paired(index[0], xu, xd, xa, xb)
    paired(index[1], yu, yd, ya, yb)
    paired(index[2], zu, zd, za, zb)


def from_fourth(tile, lane):
    phase = lane & 3
    out = tile
    for j in range(3):
        out = jnp.where(phase == j, rolled(tile, j - 3), out)
    return out


def advance(now, prev, rw, low, high_v, high_r, scale, ghost_z, ghost_rz, closing_z, index, store, acc, on_first):
    index_x, index_y, index_z = index
    at_x = jnp.where(index_x == 0, 2.0, 1.0).astype(F32)
    at_y = jnp.where(index_y == 0, 2.0, 1.0).astype(F32)
    at_z = jnp.where(index_z == 0, 2.0, 1.0).astype(F32)

    def along_y(c, carry):
        v = [now[c, y_rows(y), :] for y in range(NYL)] + [high_v[1][pl.ds(8 * c, 8), :]]
        r = [rw[y_rows(y), :] for y in range(NYL)] + [high_r[1][...]]
        carried = low[1](c, v[0])
        for e in range(4):
            terms = element(v[4 * e : 4 * e + 5], r[4 * e : 4 * e + 5])
            head = terms[0] * at_y if e == 0 else terms[0]
            acc[c, y_rows(4 * e), :] = head + carried
            for a in range(1, 4):
                acc[c, y_rows(4 * e + a), :] = terms[a]
            carried = terms[4]
        return carry

    lax.fori_loop(0, 3, along_y, 0)

    lane = lane_of()
    phase = lane & 3
    gm = [lane_table(phase, [D[b, b - k] if b >= k else 0 for b in range(4)]) for k in range(4)]
    gp = [None] + [lane_table(phase, [D[b, b + k] if b + k <= 4 else 0 for b in range(4)]) for k in range(1, 5)]
    cm = [lane_table(phase, [E[a, a - k] if a >= k else 0 for a in range(4)]) for k in range(4)]
    cp = [None] + [lane_table(phase, [E[a, a + k] if a + k <= 3 else 0 for a in range(4)]) for k in range(1, 4)]
    c_close = lane_table(phase, [E[a, 4] for a in range(4)])
    last = [lane_table(phase, [0, 0, 0, E[4, b]]) for b in range(5)]
    first = lane == 0
    edge = jnp.where(first, at_z, jnp.float32(1.0))

    def along_xz(n, carry):
        c, half = n >> 1, n & 1
        offset = half * 8
        rows = [pl.ds(pl.multiple_of(x * NYL + offset, 8), 8) for x in range(NXL)]
        plane = pl.ds(pl.multiple_of(16 * c + offset, 8), 8)
        v = [now[c, rows[x], :] for x in range(NXL)] + [high_v[0][plane, :]]
        r = [rw[rows[x], :] for x in range(NXL)] + [high_r[0][pl.ds(pl.multiple_of(offset, 8), 8), :]]
        carried = low[0](c, offset, plane, v[0])
        back = NZL - (4 * half + c)
        ghost_v = pltpu.roll(ghost_z, back, 1)
        ghost_r = pltpu.roll(ghost_rz, NZL - 4 * half, 1)
        closing = pltpu.roll(closing_z, back, 1)
        for e in range(2):
            terms = element(v[4 * e : 4 * e + 5], r[4 * e : 4 * e + 5])
            if e == 0:
                on_first(c, plane, carried, terms[0])
            for a in range(4):
                x = 4 * e + a
                force = terms[a] + acc[c, rows[x], :]
                if a == 0:
                    force = (terms[0] * at_x if e == 0 else terms[0]) + carried + acc[c, rows[x], :]
                vx = jnp.where(first, rolled(ghost_v, -8 * x), v[x])
                rx = jnp.where(first, rolled(ghost_r, -8 * x), r[x])
                vm = [v[x]] + [rolled(v[x], k) for k in range(1, 4)]
                vp = [None] + [rolled(vx, -k) for k in range(1, 5)]
                g = gm[0] * v[x]
                for k in range(1, 4):
                    g = g + gm[k] * vm[k]
                for k in range(1, 5):
                    g = g + gp[k] * vp[k]
                g4 = total([(D[4, 0], vm[3]), (D[4, 1], vm[2]), (D[4, 2], vm[1]), (D[4, 3], vm[0]), (D[4, 4], vp[1])])
                q = r[x] * g
                q4 = jnp.where(phase == 3, rolled(rx, -1) * g4, 0.0)
                qm = [q] + [rolled(q, k) for k in range(1, 4)]
                own = cm[0] * q
                for k in range(1, 4):
                    own = own + cm[k] * qm[k]
                for k in range(1, 4):
                    own = own + cp[k] * rolled(q, -k)
                pair = q4 + rolled(q4, -1)
                own = own + c_close * (pair + rolled(pair, -2))
                tail = last[3] * q + last[4] * q4
                for b in range(3):
                    tail = tail + last[b] * qm[3 - b]
                tail = jnp.where(first, rolled(closing, -8 * x), rolled(tail, 1))
                force = force + own * edge + tail
                after = (v[x] + v[x]) - prev[c, rows[x], :] - scale[rows[x], :] * force
                store(c, x, rows[x], plane, after)
            carried = terms[4]
        return carry

    lax.fori_loop(0, 6, along_xz, 0)


def step_scale(rho, scale):
    for x in range(NXL):
        rows = pl.ds(x * NYL, NYL)
        scale[rows, :] = np.float32(DT * DT) / rho[rows, :].astype(F32)


def axis_weight(pos, is_first):
    phase = pos & 3
    out = jnp.full(pos.shape, np.float32(2 * W0), F32)
    for b in range(1, 4):
        out = jnp.where(phase == b, np.float32(WQ[b]), out)
    return jnp.where((pos == 0) & is_first, np.float32(W0), out)


def first_kernel(
    counts, now, prev, rig, rho, xa, xb, ya, yb, za, zb, zd_own, nodes, ids,
    out, kept, to_normal, ya2, yb2, zu2, zd2, mx, my, mz, xd, yd, zd,
    rw, scale, acc, early, slip, xu, yu, zu, xu2, xd2, yu2, yd2,
):
    middle = counts[0] // 2
    index = place()
    unpaired(index[0], xa, xb, xu, xd)
    unpaired(index[1], ya, yb, yu, yd)
    unpaired(index[2], za, zb, zu, zd)
    widen(rig, rw)
    step_scale(rho, scale)
    lane = lane_of()
    has = [(i > 0).astype(F32) for i in index]
    for half in range(2):
        rows = pl.ds(8 * half, 8)
        mx[rows, :] = (xu[pl.ds(96 + 8 * half, 8), :] + np.float32(KAPPA * D[4, 4]) * rw[x_rows(0, half), :]) * has[0]
    my[...] = (yu[pl.ds(48, 8), :] + np.float32(KAPPA * D[4, 4]) * rw[y_rows(0), :]) * has[1]
    own, above = zd_own[...], zu[...]
    r_first = from_fourth(own, lane)
    scale_z = (from_fourth(above, lane) + np.float32(KAPPA * D[4, 4]) * r_first) * has[2]
    mz[...] = scale_z
    closing_z = above + np.float32(KAPPA) * r_first * rolled(above, 64) + scale_z * own
    kappa = np.float32(KAPPA)

    def low_x(c, offset, plane, v0):
        rows = pl.ds(pl.multiple_of(offset, 8), 8)
        grad = xu[pl.ds(pl.multiple_of(48 + 16 * c + offset, 8), 8), :]
        return xu[plane, :] + kappa * rw[rows, :] * grad + mx[rows, :] * v0

    def low_y(c, v0):
        grad = yu[pl.ds(pl.multiple_of(24 + 8 * c, 8), 8), :]
        return yu[pl.ds(pl.multiple_of(8 * c, 8), 8), :] + kappa * rw[y_rows(0), :] * grad + my[...] * v0

    def store(c, x, rows, plane, after):
        out[c, rows, :] = after
        kept[c, rows, :] = after
        if x == 0:
            xd2[plane, :] = after

    def on_first(c, plane, carried, term):
        early[plane, :] = carried - term

    below = zd[...]
    advance(
        now, prev, rw, (low_x, low_y), (xd, yd), (xd.at[pl.ds(48, 16)], yd.at[pl.ds(24, 8)]), scale,
        below, rolled(below, -3), closing_z, index, store, acc, on_first,
    )

    on_one, on_two = index[0] == middle - 1, index[0] == middle
    for half in range(2):
        rows = pl.ds(8 * half, 8)
        r = [rw[x_rows(x, half), :] for x in range(8)] + [xd[pl.ds(48 + 8 * half, 8), :]]
        y_pos = lax.broadcasted_iota(jnp.int32, (8, NZL), 0) + 8 * half
        face = axis_weight(y_pos, index[1] == 0) * axis_weight(lane, index[2] == 0) * np.float32(W0)
        for c in range(3):
            plane = pl.ds(16 * c + 8 * half, 8)
            v = [out[c, x_rows(x, half), :] for x in range(8)]
            part, grad = open_terms(v[4:], r[4:8])
            sent = part + kappa * r[8] * grad
            xu2[plane, :] = sent
            here = early[plane, :] + mx[rows, :] * v[0] - first_term(v[:5], r[:5])
            slip[plane, :] = face * jnp.where(on_one, sent, jnp.where(on_two, here, 0.0))
    r = [rw[y_rows(12 + a), :] for a in range(4)]
    for c in range(3):
        part, grad = open_terms([out[c, y_rows(12 + a), :] for a in range(4)], r)
        yu2[pl.ds(8 * c, 8), :] = part + kappa * yd[pl.ds(24, 8), :] * grad
        yd2[pl.ds(8 * c, 8), :] = out[c, y_rows(0), :]
    back = lambda t: [rolled(t, 3 - a) for a in range(4)]
    r = back(last_lanes(lambda rows: rw[rows, :], lane))
    sent = []
    for c in range(3):
        part, grad = open_terms(back(last_lanes(lambda rows: out[c, rows, :], lane)), r)
        sent.append(part + kappa * below * grad)
    zu2[...] = interleaved(sent + [None], lane, 0)
    zd2[...] = first_lanes(lambda c, rows: out[c, rows, :], None, lane)
    paired(index[1], yu2, yd2, ya2, yb2)
    tile = patch_tile(counts[2], slip[...], nodes[...], ids[...])
    for n in range(counts[0]):
        to_normal[pl.ds(56 * n, 48), :] = jnp.where(n > index[0], xu2[...], xd2[...])
        to_normal[pl.ds(56 * n + 48, 8), :] = tile


def relay_kernel(counts, got, zu2, zd2, to_depth):
    index = lax.axis_index("depth")
    tile = got[pl.ds(48, 8), :]
    for n in range(1, counts[0]):
        tile = tile + got[pl.ds(56 * n + 48, 8), :]
    for d in range(counts[2]):
        to_depth[pl.ds(16 * d, 8), :] = jnp.where(d > index, zu2[...], zd2[...])
        to_depth[pl.ds(16 * d + 8, 8), :] = jnp.broadcast_to(tile[d : d + 1, :], (8, NZL))


def sum_kernel(counts, got, to_strike):
    row = got[pl.ds(8, 8), :]
    for d in range(1, counts[2]):
        row = row + got[pl.ds(16 * d + 8, 8), :]
    for half in range(counts[1] // 8 or 1):
        to_strike[pl.ds(8 * half, min(8, counts[1])), :] = row[: min(8, counts[1]), :]


def second_kernel(
    counts, now, prev, rig, rho, got_x, ya2, yb2, got_z, zd2_own, mx, my, mz, xd, yd, zd,
    out, rw, scale, acc, xu2, xd2, yu2, yd2, zu2, zd2,
):
    index = place()
    beside(index[0], counts[0], got_x, 56, xu2, xd2)
    unpaired(index[1], ya2, yb2, yu2, yd2)
    beside(index[2], counts[2], got_z, 16, zu2, zd2)
    widen(rig, rw)
    step_scale(rho, scale)
    closing_z = zu2[...] + mz[...] * zd2_own[...]

    def low_x(c, offset, plane, v0):
        return xu2[plane, :] + mx[pl.ds(pl.multiple_of(offset, 8), 8), :] * v0

    def low_y(c, v0):
        return yu2[pl.ds(pl.multiple_of(8 * c, 8), 8), :] + my[...] * v0

    def store(c, x, rows, plane, after):
        out[c, rows, :] = after

    advance(
        now, prev, rw, (low_x, low_y), (xd2, yd2), (xd.at[pl.ds(48, 16)], yd.at[pl.ds(24, 8)]), scale,
        zd2[...], rolled(zd[...], -3), closing_z, index, store, acc, lambda *args: None,
    )


def patch_tile(count_d, slip, node, patch):
    pairs = node.shape[-1]
    hot_z = (lax.broadcasted_iota(jnp.int32, (NZL, pairs), 0) == (node & (NZL - 1))).astype(F32)
    at_z = jnp.dot(slip, hot_z, precision=HIGHEST, preferred_element_type=F32)
    row_y = lax.broadcasted_iota(jnp.int32, (NYL, pairs), 0) == (node >> 7)
    owner = patch >> 1
    owner_d = owner & (count_d - 1)
    slot = ((owner >> (count_d.bit_length() - 1)) << 1) + (patch & 1)
    hot_slot = lax.broadcasted_iota(jnp.int32, (32, pairs), 0) == slot
    spread = []
    for c in range(3):
        picked = jnp.sum(jnp.where(row_y, at_z[NYL * c : NYL * (c + 1), :], 0.0), axis=0, keepdims=True)
        spread.append(jnp.where(hot_slot, picked, 0.0))
    spread.append(jnp.zeros((32, pairs), F32))
    hot_d = (lax.broadcasted_iota(jnp.int32, (8, pairs), 0) == owner_d).astype(F32)
    return lax.dot_general(
        hot_d, jnp.concatenate(spread, axis=0), (((1,), (1,)), ((), ())), precision=HIGHEST,
        preferred_element_type=F32,
    )


def final_kernel(tiles, out):
    mine = lax.axis_index("strike") * 2
    summed = jnp.sum(tiles[...], axis=0, keepdims=True)
    lane = lax.broadcasted_iota(jnp.int32, (2, NZL), 1)
    place = lax.broadcasted_iota(jnp.int32, (2, NZL), 0)
    for c in range(3):
        hit = lane == 32 * c + mine + place
        out[:, pl.ds(c, 1)] = jnp.sum(jnp.where(hit, summed, 0.0), axis=1, keepdims=True)


def call(kernel, name, outs, scratch=(), flops=0, moved=0, in_specs=None):
    specs = {} if in_specs is None else {"in_specs": in_specs}
    return pl.pallas_call(
        kernel,
        out_shape=[jax.ShapeDtypeStruct(shape, F32) for shape in outs],
        scratch_shapes=[pltpu.VMEM(shape, F32) if isinstance(shape, tuple) else shape for shape in scratch],
        compiler_params=pltpu.CompilerParams(vmem_limit_bytes=16 * 2**20),
        cost_estimate=pl.CostEstimate(flops=flops, bytes_accessed=moved, transcendentals=0),
        name=name,
        **specs,
    )


def swap_near(value, axis):
    return lax.ppermute(value, axis, [(i, i ^ 1) for i in range(lax.axis_size(axis))])


def swap_far(value, axis):
    lower = range(1, lax.axis_size(axis) - 1, 2)
    return lax.ppermute(value, axis, [(i, i + 1) for i in lower] + [(i + 1, i) for i in lower])


def local(field_now, field_prev, rigidity, density, fault_nodes, patch_ids):
    axes = ("normal", "strike", "depth")
    counts = tuple(lax.axis_size(a) for a in axes)
    flat, block, tile = (3, ROWS, NZL), (ROWS, NZL), (8, NZL)
    now, prev = field_now.reshape(flat), field_prev.reshape(flat)
    rig, rho = rigidity.reshape(block), density.reshape(block)
    nodes, ids = fault_nodes.reshape(1, -1), patch_ids.reshape(1, -1)
    ups = [(up, NZL) for up, _ in FIRST_ROWS]
    downs = [(down, NZL) for _, down in FIRST_ROWS]
    xa, xb, ya, yb, za, zb, zd = call(
        pack_kernel, "pack", [shape for shape in ups for _ in range(2)] + [tile],
        [pltpu.VMEM(flat, F32), pltpu.VMEM(block, jnp.bfloat16), block, ups[0], downs[0], ups[1], downs[1], ups[2],
         pltpu.SemaphoreType.DMA((2,))],
        flops=2_000_000, moved=400_000, in_specs=[pl.BlockSpec(memory_space=pl.ANY)] * 2,
    )(now, rig)
    ya, yb = swap_near(ya, "strike"), swap_far(yb, "strike")
    xa, xb = swap_near(xa, "normal"), swap_far(xb, "normal")
    zb, za = swap_far(zb, "depth"), swap_near(za, "depth")
    mid, kept, to_normal, ya2, yb2, zu2, zd2, *held = call(
        functools.partial(first_kernel, counts), "first",
        [flat, flat, (56 * counts[0], NZL), (24, NZL), (24, NZL), tile, tile, (16, NZL), tile, tile] + downs,
        [block, block, flat, (48, NZL), (48, NZL)] + ups + [(48, NZL), (48, NZL), (24, NZL), (24, NZL)],
        flops=10_000_000, moved=900_000,
    )(now, prev, rig, rho, xa, xb, ya, yb, za, zb, zd, nodes, ids)
    ya2, yb2 = swap_near(ya2, "strike"), swap_far(yb2, "strike")
    got_x = lax.all_to_all(to_normal, "normal", 0, 0, tiled=True)
    (to_depth,) = call(
        functools.partial(relay_kernel, counts), "relay", [(16 * counts[2], NZL)], flops=10_000, moved=200_000,
    )(got_x, zu2, zd2)
    got_z = lax.all_to_all(to_depth, "depth", 0, 0, tiled=True)
    (to_strike,) = call(
        functools.partial(sum_kernel, counts), "add", [(counts[1], NZL)], flops=10_000, moved=80_000,
    )(got_z)
    got_s = lax.all_to_all(to_strike, "strike", 0, 0, tiled=True)
    (share,) = call(final_kernel, "final", [(2, 3)], flops=10_000, moved=10_000)(got_s)
    (following,) = call(
        functools.partial(second_kernel, counts), "second", [flat],
        [block, block, flat] + [(n, NZL) for pair in SECOND_ROWS for n in pair],
        flops=10_000_000, moved=900_000,
    )(kept, now, rig, rho, got_x, ya2, yb2, got_z, zd2, *held)
    return following.reshape(field_now.shape), mid.reshape(field_now.shape), share


def solution(mesh):
    field = P(None, "normal", "strike", "depth")
    cells = P("normal", "strike", "depth")
    pairs = P("strike", "depth", None)
    return jax.shard_map(
        local,
        mesh=mesh,
        in_specs=(field, field, cells, cells, pairs, pairs),
        out_specs=(field, field, P(("strike", "depth"), None)),
        check_vma=False,
    )
```

```python
import functools
import math

import jax
import jax.numpy as jnp
import numpy as np
from jax import lax
from jax.experimental import pallas as pl
from jax.experimental.pallas import tpu as pltpu
from jax.sharding import PartitionSpec as P

DT = 0.03
NXL, NYL, NZL = 8, 16, 128
ROWS = NXL * NYL
F32 = jnp.float32
HIGHEST = lax.Precision.HIGHEST


def gll_tables():
    spread = math.sqrt(3.0 / 7.0)
    points = np.array([-1.0, -spread, 0.0, spread, 1.0])
    weights = np.array([0.1, 49.0 / 90.0, 32.0 / 45.0, 49.0 / 90.0, 0.1]) * 0.5
    derivative = np.zeros((5, 5))
    for b in range(5):
        for a in range(5):
            if a == b:
                derivative[b, a] = sum(1.0 / (points[b] - points[o]) for o in range(5) if o != b)
            else:
                row = np.prod([points[b] - points[o] for o in range(5) if o != b and o != a])
                col = np.prod([points[a] - points[o] for o in range(5) if o != a and o != b])
                derivative[b, a] = row / (col * (points[a] - points[b]))
    return weights, 2.0 * derivative


WQ, D = gll_tables()
W0 = float(WQ[0])
NODE_W = np.array([2 * WQ[0], WQ[1], WQ[2], WQ[3], 2 * WQ[0]])
E = (WQ[:, None] * D).T / NODE_W[:, None]
KAPPA = float(E[4, 4])


def total(pairs):
    acc = None
    for const, arr in pairs:
        if abs(const) < 1e-12:
            continue
        term = arr * np.float32(const)
        acc = term if acc is None else acc + term
    return acc


def element(v, r):
    twice = v[2] + v[2]
    s0, s1 = v[0] + v[4] - twice, v[1] + v[3] - twice
    d0, d1 = v[0] - v[4], v[1] - v[3]
    ev = [total([((D[b, 0] + D[b, 4]) / 2, s0), ((D[b, 1] + D[b, 3]) / 2, s1)]) for b in (0, 1)]
    od = [total([((D[b, 0] - D[b, 4]) / 2, d0), ((D[b, 1] - D[b, 3]) / 2, d1)]) for b in (0, 1)]
    g2 = total([(D[2, 0], d0), (D[2, 1], d1)])
    q = [r[0] * (od[0] + ev[0]), r[1] * (od[1] + ev[1]), r[2] * g2, r[3] * (od[1] - ev[1]), r[4] * (od[0] - ev[0])]
    p0, m0, p1, m1 = q[0] + q[4], q[0] - q[4], q[1] + q[3], q[1] - q[3]
    ec = [total([((E[a, 0] + E[a, 4]) / 2, p0), ((E[a, 1] + E[a, 3]) / 2, p1), (E[a, 2], q[2])]) for a in (0, 1)]
    oc = [total([((E[a, 0] - E[a, 4]) / 2, m0), ((E[a, 1] - E[a, 3]) / 2, m1)]) for a in (0, 1)]
    c2 = total([(E[2, 0], m0), (E[2, 1], m1)])
    return [oc[0] + ec[0], oc[1] + ec[1], c2, oc[1] - ec[1], oc[0] - ec[0]]


def first_term(v, r):
    twice = v[2] + v[2]
    s0, s1 = v[0] + v[4] - twice, v[1] + v[3] - twice
    d0, d1 = v[0] - v[4], v[1] - v[3]
    ev = [total([((D[b, 0] + D[b, 4]) / 2, s0), ((D[b, 1] + D[b, 3]) / 2, s1)]) for b in (0, 1)]
    od = [total([((D[b, 0] - D[b, 4]) / 2, d0), ((D[b, 1] - D[b, 3]) / 2, d1)]) for b in (0, 1)]
    g2 = total([(D[2, 0], d0), (D[2, 1], d1)])
    q = [r[0] * (od[0] + ev[0]), r[1] * (od[1] + ev[1]), r[2] * g2, r[3] * (od[1] - ev[1]), r[4] * (od[0] - ev[0])]
    return total([(E[0, b], q[b]) for b in range(5)])


def open_terms(v, r):
    flux = [r[b] * total([(D[b, a], v[a]) for a in range(4)]) for b in range(4)]
    part = total([(E[4, b], flux[b]) for b in range(4)])
    grad = total([(D[4, a], v[a]) for a in range(4)])
    return part, grad


def open_scale(r):
    return total([(E[4, b] * D[b, 4], r[b]) for b in range(4)])


def rolled(x, shift):
    shift = shift % NZL
    return x if shift == 0 else pltpu.roll(x, shift, 1)


def lane_of():
    return lax.broadcasted_iota(jnp.int32, (8, NZL), 1)


def lane_table(phase, values):
    out = jnp.full((8, NZL), np.float32(values[0]), F32)
    for b in range(1, 4):
        out = jnp.where(phase == b, np.float32(values[b]), out)
    return out


def x_rows(x, half):
    return pl.ds(x * NYL + half * 8, 8)


def y_rows(y):
    return pl.ds(y, 8, stride=NYL)


def first_lanes(read, read_r, lane):
    out = jnp.zeros((8, NZL), F32)
    for k in range(16):
        rows = pl.ds(8 * k, 8)
        for c in range(3 if read_r is None else 4):
            src = read_r(rows) if c == 3 else read(c, rows)
            out = jnp.where(lane == 4 * k + c, rolled(src, 4 * k + c), out)
    return out


def last_lanes(read, lane):
    out = jnp.zeros((8, NZL), F32)
    for k in range(16):
        out = jnp.where((lane >> 2) == k, rolled(read(pl.ds(8 * k, 8)), 4 * k + 4), out)
    return out


def interleaved(parts, lane, base):
    out = jnp.zeros((8, NZL), F32)
    for j, part in enumerate(parts):
        if part is None:
            continue
        out = jnp.where((lane >= base) & (lane < base + 64) & ((lane & 3) == j), rolled(part, base + j - 3), out)
    return out


def widen(src, dst):
    for x in range(NXL):
        dst[pl.ds(x * NYL, NYL), :] = src[pl.ds(x * NYL, NYL), :].astype(F32)


X_UP, X_DOWN = 112, 64
Y_UP, Y_DOWN = 136, 64


def place():
    return tuple(lax.axis_index(axis) for axis in ("normal", "strike", "depth"))


def paired(index, up, down, near, far):
    even = (index & 1) == 0
    rows = pl.ds(0, down.shape[0])
    near[...] = up[...]
    far[...] = up[...]
    near[rows, :] = jnp.where(even, up[rows, :], down[...])
    far[rows, :] = jnp.where(even, down[...], up[rows, :])


def unpaired(index, near, far, low, high):
    even = (index & 1) == 0
    rows = pl.ds(0, high.shape[0])
    low[...] = jnp.where(even, far[...], near[...])
    high[...] = jnp.where(even, near[rows, :], far[rows, :])


def beside(index, count, got, stride, low, high):
    below = pl.multiple_of(jnp.maximum(index - 1, 0) * stride, 8)
    above = pl.multiple_of(jnp.minimum(index + 1, count - 1) * stride, 8)
    low[...] = jnp.where(index > 0, got[pl.ds(below, low.shape[0]), :], 0.0)
    high[...] = jnp.where(index < count - 1, got[pl.ds(above, high.shape[0]), :], 0.0)


def pack_kernel(now_hbm, rig_hbm, xa, xb, za, zb, zd, now, rig, rw, xu, xd, zu, sems):
    copies = [pltpu.make_async_copy(rig_hbm, rig, sems.at[0]), pltpu.make_async_copy(now_hbm, now, sems.at[1])]
    for copy in copies:
        copy.start()
    for copy in copies:
        copy.wait()
    widen(rig, rw)
    lane = lane_of()
    for half in range(2):
        r = [rw[x_rows(4 + a, half), :] for a in range(4)]
        xu[pl.ds(96 + 8 * half, 8), :] = open_scale(r)
        xd[pl.ds(48 + 8 * half, 8), :] = rw[x_rows(0, half), :]
        for c in range(3):
            part, grad = open_terms([now[c, x_rows(4 + a, half), :] for a in range(4)], r)
            xu[pl.ds(16 * c + 8 * half, 8), :] = part
            xu[pl.ds(48 + 16 * c + 8 * half, 8), :] = grad
            xd[pl.ds(16 * c + 8 * half, 8), :] = now[c, x_rows(0, half), :]
    back = lambda t: [rolled(t, 3 - a) for a in range(4)]
    r = back(last_lanes(lambda rows: rw[rows, :], lane))
    parts, grads = [], []
    for c in range(3):
        part, grad = open_terms(back(last_lanes(lambda rows: now[c, rows, :], lane)), r)
        parts.append(part)
        grads.append(grad)
    zu[...] = jnp.where(
        lane < 64, interleaved(parts + [open_scale(r)], lane, 0), interleaved(grads + [None], lane, 64)
    )
    zd[...] = first_lanes(lambda c, rows: now[c, rows, :], lambda rows: rw[rows, :], lane)
    index = place()
    paired(index[0], xu, xd, xa, xb)
    paired(index[2], zu, zd, za, zb)


def from_fourth(tile, lane):
    phase = lane & 3
    out = tile
    for j in range(3):
        out = jnp.where(phase == j, rolled(tile, j - 3), out)
    return out


def advance(now, prev, rw, low, high_v, high_r, scale, ghost_z, ghost_rz, closing_z, index, store, acc, on_first):
    index_x, index_y, index_z = index
    at_x = jnp.where(index_x == 0, 2.0, 1.0).astype(F32)
    at_y = jnp.where(index_y == 0, 2.0, 1.0).astype(F32)
    at_z = jnp.where(index_z == 0, 2.0, 1.0).astype(F32)

    def along_y(c, carry):
        none = jnp.zeros((8, NZL), F32)
        v = [now[c, y_rows(y), :] for y in range(NYL)] + [high_v[1][pl.ds(8 * c, 8), :] if high_v[1] is not None else none]
        r = [rw[y_rows(y), :] for y in range(NYL)] + [high_r[1][...] if high_r[1] is not None else none]
        carried = low[1](c, v[0]) if low[1] is not None else none
        for e in range(4):
            terms = element(v[4 * e : 4 * e + 5], r[4 * e : 4 * e + 5])
            head = terms[0] * at_y if e == 0 else terms[0]
            acc[c, y_rows(4 * e), :] = head + carried
            for a in range(1, 4):
                acc[c, y_rows(4 * e + a), :] = terms[a]
            carried = terms[4]
        return carry

    lax.fori_loop(0, 3, along_y, 0)

    lane = lane_of()
    phase = lane & 3
    gm = [lane_table(phase, [D[b, b - k] if b >= k else 0 for b in range(4)]) for k in range(4)]
    gp = [None] + [lane_table(phase, [D[b, b + k] if b + k <= 4 else 0 for b in range(4)]) for k in range(1, 5)]
    cm = [lane_table(phase, [E[a, a - k] if a >= k else 0 for a in range(4)]) for k in range(4)]
    cp = [None] + [lane_table(phase, [E[a, a + k] if a + k <= 3 else 0 for a in range(4)]) for k in range(1, 4)]
    c_close = lane_table(phase, [E[a, 4] for a in range(4)])
    last = [lane_table(phase, [0, 0, 0, E[4, b]]) for b in range(5)]
    first = lane == 0
    edge = jnp.where(first, at_z, jnp.float32(1.0))

    def along_xz(n, carry):
        c, half = n >> 1, n & 1
        offset = half * 8
        rows = [pl.ds(pl.multiple_of(x * NYL + offset, 8), 8) for x in range(NXL)]
        plane = pl.ds(pl.multiple_of(16 * c + offset, 8), 8)
        v = [now[c, rows[x], :] for x in range(NXL)] + [high_v[0][plane, :]]
        r = [rw[rows[x], :] for x in range(NXL)] + [high_r[0][pl.ds(pl.multiple_of(offset, 8), 8), :]]
        carried = low[0](c, offset, plane, v[0])
        back = NZL - (4 * half + c)
        ghost_v = pltpu.roll(ghost_z, back, 1)
        ghost_r = pltpu.roll(ghost_rz, NZL - 4 * half, 1)
        closing = pltpu.roll(closing_z, back, 1)
        for e in range(2):
            terms = element(v[4 * e : 4 * e + 5], r[4 * e : 4 * e + 5])
            if e == 0:
                on_first(c, plane, carried, terms[0])
            for a in range(4):
                x = 4 * e + a
                force = terms[a] + acc[c, rows[x], :]
                if a == 0:
                    force = (terms[0] * at_x if e == 0 else terms[0]) + carried + acc[c, rows[x], :]
                vx = jnp.where(first, rolled(ghost_v, -8 * x), v[x])
                rx = jnp.where(first, rolled(ghost_r, -8 * x), r[x])
                vm = [v[x]] + [rolled(v[x], k) for k in range(1, 4)]
                vp = [None] + [rolled(vx, -k) for k in range(1, 5)]
                g = gm[0] * v[x]
                for k in range(1, 4):
                    g = g + gm[k] * vm[k]
                for k in range(1, 5):
                    g = g + gp[k] * vp[k]
                g4 = total([(D[4, 0], vm[3]), (D[4, 1], vm[2]), (D[4, 2], vm[1]), (D[4, 3], vm[0]), (D[4, 4], vp[1])])
                q = r[x] * g
                q4 = jnp.where(phase == 3, rolled(rx, -1) * g4, 0.0)
                qm = [q] + [rolled(q, k) for k in range(1, 4)]
                own = cm[0] * q
                for k in range(1, 4):
                    own = own + cm[k] * qm[k]
                for k in range(1, 4):
                    own = own + cp[k] * rolled(q, -k)
                pair = q4 + rolled(q4, -1)
                own = own + c_close * (pair + rolled(pair, -2))
                tail = last[3] * q + last[4] * q4
                for b in range(3):
                    tail = tail + last[b] * qm[3 - b]
                tail = jnp.where(first, rolled(closing, -8 * x), rolled(tail, 1))
                force = force + own * edge + tail
                after = (v[x] + v[x]) - prev[c, rows[x], :] - scale[rows[x], :] * force
                store(c, x, rows[x], plane, after)
            carried = terms[4]
        return carry

    lax.fori_loop(0, 6, along_xz, 0)


def step_scale(rho, scale):
    for x in range(NXL):
        rows = pl.ds(x * NYL, NYL)
        scale[rows, :] = np.float32(DT * DT) / rho[rows, :].astype(F32)


def axis_weight(pos, is_first):
    phase = pos & 3
    out = jnp.full(pos.shape, np.float32(2 * W0), F32)
    for b in range(1, 4):
        out = jnp.where(phase == b, np.float32(WQ[b]), out)
    return jnp.where((pos == 0) & is_first, np.float32(W0), out)


def half_kernel(
    counts, now, prev, rig, rho, xa, xb, za, zb, zd_own,
    base, ya, yb, early, mx, mz, xd, zd, rw, scale,
    acc, xu, zu, yu, yd,
):
    index = place()
    unpaired(index[0], xa, xb, xu, xd)
    unpaired(index[2], za, zb, zu, zd)
    widen(rig, rw)
    step_scale(rho, scale)
    lane = lane_of()
    has_x, has_z = (index[0] > 0).astype(F32), (index[2] > 0).astype(F32)
    kappa, diagonal = np.float32(KAPPA), np.float32(KAPPA * D[4, 4])
    for half in range(2):
        rows = pl.ds(8 * half, 8)
        mx[rows, :] = (xu[pl.ds(96 + 8 * half, 8), :] + diagonal * rw[x_rows(0, half), :]) * has_x
    own, above = zd_own[...], zu[...]
    r_first = from_fourth(own, lane)
    scale_z = (from_fourth(above, lane) + diagonal * r_first) * has_z
    mz[...] = scale_z
    closing_z = above + kappa * r_first * rolled(above, 64) + scale_z * own

    def low_x(c, offset, plane, v0):
        rows = pl.ds(pl.multiple_of(offset, 8), 8)
        grad = xu[pl.ds(pl.multiple_of(48 + 16 * c + offset, 8), 8), :]
        return xu[plane, :] + kappa * rw[rows, :] * grad + mx[rows, :] * v0

    def store(c, x, rows, plane, after):
        base[c, rows, :] = after

    def on_first(c, plane, carried, term):
        early[plane, :] = carried - term

    below = zd[...]
    advance(
        now, prev, rw, (low_x, None), (xd, None), (xd.at[pl.ds(48, 16)], None), scale,
        below, rolled(below, -3), closing_z, index, store, acc, on_first,
    )

    r = [rw[y_rows(12 + a), :] for a in range(4)]
    by_value, by_flux = open_response([scale[y_rows(12 + a), :] for a in range(4)], r)
    planes = [open_scale(r), *open_terms(by_value, r), *open_terms(by_flux, r)]
    for n, plane in enumerate(planes):
        yu[pl.ds(96 + 8 * n, 8), :] = plane
    for c in range(3):
        planes = open_terms([now[c, y_rows(12 + a), :] for a in range(4)], r)
        planes += open_terms([base[c, y_rows(12 + a), :] for a in range(4)], r)
        for n, plane in enumerate(planes):
            yu[pl.ds(24 * n + 8 * c, 8), :] = plane
        yd[pl.ds(8 * c, 8), :] = now[c, y_rows(0), :]
        yd[pl.ds(24 + 8 * c, 8), :] = base[c, y_rows(0), :]
    yd[pl.ds(48, 8), :] = rw[y_rows(0), :]
    yd[pl.ds(56, 8), :] = scale[y_rows(0), :]
    paired(index[1], yu, yd, ya, yb)


def open_response(scale, r):
    by_value = [scale[a] * total([(E[a, b] * D[b, 4], r[b]) for b in range(4)]) for a in range(4)]
    by_flux = [scale[a] * np.float32(E[a, 4]) for a in range(4)]
    return by_value, by_flux


def whole_kernel(
    counts, base, now, rw, scale, early, ya, yb, mx, xd, zd, nodes, ids,
    out, kept, to_normal, zu2, zd2, my, y_low, y_high, r_high,
    slip, yu, yd, xu2, xd2,
):
    middle = counts[0] // 2
    index = place()
    lane = lane_of()
    kappa, diagonal = np.float32(KAPPA), np.float32(KAPPA * D[4, 4])
    d44 = np.float32(D[4, 4])
    unpaired(index[1], ya, yb, yu, yd)
    for c in range(3):
        for k in range(16):
            rows = pl.ds(8 * k, 8)
            values = base[c, rows, :]
            out[c, rows, :] = values
            kept[c, rows, :] = values
    r = [rw[y_rows(12 + a), :] for a in range(4)]
    by_value, by_flux = open_response([scale[y_rows(12 + a), :] for a in range(4)], r)
    own_scale = open_scale(r)
    r0, s0 = rw[y_rows(0), :], scale[y_rows(0), :]
    r_above, s_above = yd[pl.ds(48, 8), :], yd[pl.ds(56, 8), :]
    r_high[...] = r_above
    gain, value_part, value_grad, flux_part, flux_grad = (yu[pl.ds(96 + 8 * n, 8), :] for n in range(5))
    gain = (gain + diagonal * r0) * (index[1] > 0).astype(F32)
    my[...] = gain
    for c in range(3):
        plane = pl.ds(8 * c, 8)
        part, grad, part2, grad2 = (yu[pl.ds(24 * n + 8 * c, 8), :] for n in range(4))
        v0 = now[c, y_rows(0), :]
        after = base[c, y_rows(0), :] - s0 * (part + kappa * r0 * grad + gain * v0)
        out[c, y_rows(0), :] = after
        kept[c, y_rows(0), :] = after
        flux = r0 * (grad + d44 * v0)
        y_low[plane, :] = (part2 - value_part * v0 - flux_part * flux) + kappa * r0 * (
            grad2 - value_grad * v0 - flux_grad * flux
        )
        above = yd[plane, :]
        part, grad = open_terms([now[c, y_rows(12 + a), :] for a in range(4)], r)
        flux = r_above * (grad + d44 * above)
        y_high[plane, :] = yd[pl.ds(24 + 8 * c, 8), :] - s_above * (part + own_scale * above + kappa * flux)
        for a in range(4):
            after = base[c, y_rows(12 + a), :] - by_value[a] * above - by_flux[a] * flux
            out[c, y_rows(12 + a), :] = after
            kept[c, y_rows(12 + a), :] = after

    on_one, on_two = index[0] == middle - 1, index[0] == middle
    for half in range(2):
        rows = pl.ds(8 * half, 8)
        r = [rw[x_rows(x, half), :] for x in range(8)] + [xd[pl.ds(48 + 8 * half, 8), :]]
        y_pos = lax.broadcasted_iota(jnp.int32, (8, NZL), 0) + 8 * half
        face = axis_weight(y_pos, index[1] == 0) * axis_weight(lane, index[2] == 0) * np.float32(W0)
        for c in range(3):
            plane = pl.ds(16 * c + 8 * half, 8)
            v = [out[c, x_rows(x, half), :] for x in range(8)]
            part, grad = open_terms(v[4:], r[4:8])
            sent = part + kappa * r[8] * grad
            xu2[plane, :] = sent
            xd2[plane, :] = v[0]
            here = early[plane, :] + mx[rows, :] * v[0] - first_term(v[:5], r[:5])
            slip[plane, :] = face * jnp.where(on_one, sent, jnp.where(on_two, here, 0.0))
    back = lambda t: [rolled(t, 3 - a) for a in range(4)]
    r = back(last_lanes(lambda rows: rw[rows, :], lane))
    sent = []
    for c in range(3):
        part, grad = open_terms(back(last_lanes(lambda rows: out[c, rows, :], lane)), r)
        sent.append(part + kappa * zd[...] * grad)
    zu2[...] = interleaved(sent + [None], lane, 0)
    zd2[...] = first_lanes(lambda c, rows: out[c, rows, :], None, lane)
    tile = patch_tile(counts[2], slip[...], nodes[...], ids[...])
    for n in range(counts[0]):
        to_normal[pl.ds(56 * n, 48), :] = jnp.where(n > index[0], xu2[...], xd2[...])
        to_normal[pl.ds(56 * n + 48, 8), :] = tile


def relay_kernel(counts, got, zu2, zd2, to_depth):
    index = lax.axis_index("depth")
    tile = got[pl.ds(48, 8), :]
    for n in range(1, counts[0]):
        tile = tile + got[pl.ds(56 * n + 48, 8), :]
    for d in range(counts[2]):
        to_depth[pl.ds(16 * d, 8), :] = jnp.where(d > index, zu2[...], zd2[...])
        to_depth[pl.ds(16 * d + 8, 8), :] = jnp.broadcast_to(tile[d : d + 1, :], (8, NZL))


def sum_kernel(counts, got, to_strike):
    row = got[pl.ds(8, 8), :]
    for d in range(1, counts[2]):
        row = row + got[pl.ds(16 * d + 8, 8), :]
    for half in range(counts[1] // 8 or 1):
        to_strike[pl.ds(8 * half, min(8, counts[1])), :] = row[: min(8, counts[1]), :]


def second_kernel(
    counts, now, prev, rw, scale, got_x, got_z, zd2_own, mx, my, mz, xd, zd, y_low, y_high, r_high,
    out, acc, xu2, xd2, zu2, zd2,
):
    index = place()
    beside(index[0], counts[0], got_x, 56, xu2, xd2)
    beside(index[2], counts[2], got_z, 16, zu2, zd2)
    closing_z = zu2[...] + mz[...] * zd2_own[...]

    def low_x(c, offset, plane, v0):
        return xu2[plane, :] + mx[pl.ds(pl.multiple_of(offset, 8), 8), :] * v0

    def low_y(c, v0):
        return y_low[pl.ds(pl.multiple_of(8 * c, 8), 8), :] + my[...] * v0

    def store(c, x, rows, plane, after):
        out[c, rows, :] = after

    advance(
        now, prev, rw, (low_x, low_y), (xd2, y_high), (xd.at[pl.ds(48, 16)], r_high), scale,
        zd2[...], rolled(zd[...], -3), closing_z, index, store, acc, lambda *args: None,
    )


def patch_tile(count_d, slip, node, patch):
    pairs = node.shape[-1]
    hot_z = (lax.broadcasted_iota(jnp.int32, (NZL, pairs), 0) == (node & (NZL - 1))).astype(F32)
    at_z = jnp.dot(slip, hot_z, precision=HIGHEST, preferred_element_type=F32)
    row_y = lax.broadcasted_iota(jnp.int32, (NYL, pairs), 0) == (node >> 7)
    owner = patch >> 1
    owner_d = owner & (count_d - 1)
    slot = ((owner >> (count_d.bit_length() - 1)) << 1) + (patch & 1)
    hot_slot = lax.broadcasted_iota(jnp.int32, (32, pairs), 0) == slot
    spread = []
    for c in range(3):
        picked = jnp.sum(jnp.where(row_y, at_z[NYL * c : NYL * (c + 1), :], 0.0), axis=0, keepdims=True)
        spread.append(jnp.where(hot_slot, picked, 0.0))
    spread.append(jnp.zeros((32, pairs), F32))
    hot_d = (lax.broadcasted_iota(jnp.int32, (8, pairs), 0) == owner_d).astype(F32)
    return lax.dot_general(
        hot_d, jnp.concatenate(spread, axis=0), (((1,), (1,)), ((), ())), precision=HIGHEST,
        preferred_element_type=F32,
    )


def final_kernel(tiles, out):
    mine = lax.axis_index("strike") * 2
    summed = jnp.sum(tiles[...], axis=0, keepdims=True)
    lane = lax.broadcasted_iota(jnp.int32, (2, NZL), 1)
    place = lax.broadcasted_iota(jnp.int32, (2, NZL), 0)
    for c in range(3):
        hit = lane == 32 * c + mine + place
        out[:, pl.ds(c, 1)] = jnp.sum(jnp.where(hit, summed, 0.0), axis=1, keepdims=True)


def call(kernel, name, outs, scratch=(), flops=0, moved=0, in_specs=None):
    specs = {} if in_specs is None else {"in_specs": in_specs}
    return pl.pallas_call(
        kernel,
        out_shape=[jax.ShapeDtypeStruct(shape, F32) for shape in outs],
        scratch_shapes=[pltpu.VMEM(shape, F32) if isinstance(shape, tuple) else shape for shape in scratch],
        compiler_params=pltpu.CompilerParams(vmem_limit_bytes=16 * 2**20),
        cost_estimate=pl.CostEstimate(flops=flops, bytes_accessed=moved, transcendentals=0),
        name=name,
        **specs,
    )


def swap_near(value, axis):
    return lax.ppermute(value, axis, [(i, i ^ 1) for i in range(lax.axis_size(axis))])


def swap_far(value, axis):
    lower = range(1, lax.axis_size(axis) - 1, 2)
    return lax.ppermute(value, axis, [(i, i + 1) for i in lower] + [(i + 1, i) for i in lower])


def local(field_now, field_prev, rigidity, density, fault_nodes, patch_ids):
    axes = ("normal", "strike", "depth")
    counts = tuple(lax.axis_size(a) for a in axes)
    flat, block, tile = (3, ROWS, NZL), (ROWS, NZL), (8, NZL)
    now, prev = field_now.reshape(flat), field_prev.reshape(flat)
    rig, rho = rigidity.reshape(block), density.reshape(block)
    nodes, ids = fault_nodes.reshape(1, -1), patch_ids.reshape(1, -1)
    x_up, x_down, y_up, y_down = ((n, NZL) for n in (X_UP, X_DOWN, Y_UP, Y_DOWN))
    faces, strip = (48, NZL), (24, NZL)
    xa, xb, za, zb, zd_own = call(
        pack_kernel, "pack", [x_up, x_up, tile, tile, tile],
        [pltpu.VMEM(flat, F32), pltpu.VMEM(block, jnp.bfloat16), block, x_up, x_down, tile,
         pltpu.SemaphoreType.DMA((2,))],
        flops=2_000_000, moved=400_000, in_specs=[pl.BlockSpec(memory_space=pl.ANY)] * 2,
    )(now, rig)
    xa, xb = swap_near(xa, "normal"), swap_far(xb, "normal")
    zb, za = swap_far(zb, "depth"), swap_near(za, "depth")
    base, ya, yb, early, mx, mz, xd, zd, rw, scale = call(
        functools.partial(half_kernel, counts), "half",
        [flat, y_up, y_up, faces, (16, NZL), tile, x_down, tile, block, block],
        [flat, x_up, tile, y_up, y_down], flops=10_000_000, moved=900_000,
    )(now, prev, rig, rho, xa, xb, za, zb, zd_own)
    yb, ya = swap_far(yb, "strike"), swap_near(ya, "strike")
    mid, kept, to_normal, zu2, zd2, my, y_low, y_high, r_high = call(
        functools.partial(whole_kernel, counts), "whole",
        [flat, flat, (56 * counts[0], NZL), tile, tile, tile, strip, strip, tile],
        [faces, y_up, y_down, faces, faces], flops=2_000_000, moved=900_000,
    )(base, now, rw, scale, early, ya, yb, mx, xd, zd, nodes, ids)
    got_x = lax.all_to_all(to_normal, "normal", 0, 0, tiled=True)
    (to_depth,) = call(
        functools.partial(relay_kernel, counts), "relay", [(16 * counts[2], NZL)], flops=10_000, moved=200_000,
    )(got_x, zu2, zd2)
    got_z = lax.all_to_all(to_depth, "depth", 0, 0, tiled=True)
    (to_strike,) = call(
        functools.partial(sum_kernel, counts), "add", [(counts[1], NZL)], flops=10_000, moved=80_000,
    )(got_z)
    got_s = lax.all_to_all(to_strike, "strike", 0, 0, tiled=True)
    (share,) = call(final_kernel, "final", [(2, 3)], flops=10_000, moved=10_000)(got_s)
    (following,) = call(
        functools.partial(second_kernel, counts), "second", [flat], [flat, faces, faces, tile, tile],
        flops=10_000_000, moved=900_000,
    )(kept, now, rw, scale, got_x, got_z, zd2, mx, my, mz, xd, zd, y_low, y_high, r_high)
    return following.reshape(field_now.shape), mid.reshape(field_now.shape), share


def solution(mesh):
    field = P(None, "normal", "strike", "depth")
    cells = P("normal", "strike", "depth")
    pairs = P("strike", "depth", None)
    return jax.shard_map(
        local,
        mesh=mesh,
        in_specs=(field, field, cells, cells, pairs, pairs),
        out_specs=(field, field, P(("strike", "depth"), None)),
        check_vma=False,
    )
```

```python
import functools
import math

import jax
import jax.numpy as jnp
import numpy as np
from jax import lax
from jax.experimental import pallas as pl
from jax.experimental.pallas import tpu as pltpu
from jax.sharding import PartitionSpec as P

DT = 0.03
NXL, NYL, NZL = 8, 16, 128
ROWS = NXL * NYL
F32 = jnp.float32
HIGHEST = lax.Precision.HIGHEST


def gll_tables():
    spread = math.sqrt(3.0 / 7.0)
    points = np.array([-1.0, -spread, 0.0, spread, 1.0])
    weights = np.array([0.1, 49.0 / 90.0, 32.0 / 45.0, 49.0 / 90.0, 0.1]) * 0.5
    derivative = np.zeros((5, 5))
    for b in range(5):
        for a in range(5):
            if a == b:
                derivative[b, a] = sum(1.0 / (points[b] - points[o]) for o in range(5) if o != b)
            else:
                row = np.prod([points[b] - points[o] for o in range(5) if o != b and o != a])
                col = np.prod([points[a] - points[o] for o in range(5) if o != a and o != b])
                derivative[b, a] = row / (col * (points[a] - points[b]))
    return weights, 2.0 * derivative


WQ, D = gll_tables()
W0 = float(WQ[0])
NODE_W = np.array([2 * WQ[0], WQ[1], WQ[2], WQ[3], 2 * WQ[0]])
E = (WQ[:, None] * D).T / NODE_W[:, None]
KAPPA = float(E[4, 4])


def total(pairs):
    acc = None
    for const, arr in pairs:
        if abs(const) < 1e-12:
            continue
        term = arr * np.float32(const)
        acc = term if acc is None else acc + term
    return acc


def element(v, r):
    twice = v[2] + v[2]
    s0, s1 = v[0] + v[4] - twice, v[1] + v[3] - twice
    d0, d1 = v[0] - v[4], v[1] - v[3]
    ev = [total([((D[b, 0] + D[b, 4]) / 2, s0), ((D[b, 1] + D[b, 3]) / 2, s1)]) for b in (0, 1)]
    od = [total([((D[b, 0] - D[b, 4]) / 2, d0), ((D[b, 1] - D[b, 3]) / 2, d1)]) for b in (0, 1)]
    g2 = total([(D[2, 0], d0), (D[2, 1], d1)])
    q = [r[0] * (od[0] + ev[0]), r[1] * (od[1] + ev[1]), r[2] * g2, r[3] * (od[1] - ev[1]), r[4] * (od[0] - ev[0])]
    p0, m0, p1, m1 = q[0] + q[4], q[0] - q[4], q[1] + q[3], q[1] - q[3]
    ec = [total([((E[a, 0] + E[a, 4]) / 2, p0), ((E[a, 1] + E[a, 3]) / 2, p1), (E[a, 2], q[2])]) for a in (0, 1)]
    oc = [total([((E[a, 0] - E[a, 4]) / 2, m0), ((E[a, 1] - E[a, 3]) / 2, m1)]) for a in (0, 1)]
    c2 = total([(E[2, 0], m0), (E[2, 1], m1)])
    return [oc[0] + ec[0], oc[1] + ec[1], c2, oc[1] - ec[1], oc[0] - ec[0]]


def first_term(v, r):
    twice = v[2] + v[2]
    s0, s1 = v[0] + v[4] - twice, v[1] + v[3] - twice
    d0, d1 = v[0] - v[4], v[1] - v[3]
    ev = [total([((D[b, 0] + D[b, 4]) / 2, s0), ((D[b, 1] + D[b, 3]) / 2, s1)]) for b in (0, 1)]
    od = [total([((D[b, 0] - D[b, 4]) / 2, d0), ((D[b, 1] - D[b, 3]) / 2, d1)]) for b in (0, 1)]
    g2 = total([(D[2, 0], d0), (D[2, 1], d1)])
    q = [r[0] * (od[0] + ev[0]), r[1] * (od[1] + ev[1]), r[2] * g2, r[3] * (od[1] - ev[1]), r[4] * (od[0] - ev[0])]
    return total([(E[0, b], q[b]) for b in range(5)])


def open_terms(v, r):
    flux = [r[b] * total([(D[b, a], v[a]) for a in range(4)]) for b in range(4)]
    part = total([(E[4, b], flux[b]) for b in range(4)])
    grad = total([(D[4, a], v[a]) for a in range(4)])
    return part, grad


def open_scale(r):
    return total([(E[4, b] * D[b, 4], r[b]) for b in range(4)])


def rolled(x, shift):
    shift = shift % NZL
    return x if shift == 0 else pltpu.roll(x, shift, 1)


def lane_of():
    return lax.broadcasted_iota(jnp.int32, (8, NZL), 1)


def lane_table(phase, values):
    out = jnp.full((8, NZL), np.float32(values[0]), F32)
    for b in range(1, 4):
        out = jnp.where(phase == b, np.float32(values[b]), out)
    return out


def x_rows(x, half):
    return pl.ds(x * NYL + half * 8, 8)


def y_rows(y):
    return pl.ds(y, 8, stride=NYL)


def first_lanes(read, read_r, lane):
    out = jnp.zeros((8, NZL), F32)
    for k in range(16):
        rows = pl.ds(8 * k, 8)
        for c in range(3 if read_r is None else 4):
            src = read_r(rows) if c == 3 else read(c, rows)
            out = jnp.where(lane == 4 * k + c, rolled(src, 4 * k + c), out)
    return out


def last_lanes(read, lane):
    out = jnp.zeros((8, NZL), F32)
    for k in range(16):
        out = jnp.where((lane >> 2) == k, rolled(read(pl.ds(8 * k, 8)), 4 * k + 4), out)
    return out


def interleaved(parts, lane, base):
    out = jnp.zeros((8, NZL), F32)
    for j, part in enumerate(parts):
        if part is None:
            continue
        out = jnp.where((lane >= base) & (lane < base + 64) & ((lane & 3) == j), rolled(part, base + j - 3), out)
    return out


def widen(src, dst):
    for x in range(NXL):
        dst[pl.ds(x * NYL, NYL), :] = src[pl.ds(x * NYL, NYL), :].astype(F32)


X_UP, X_DOWN = 112, 64
Y_UP, Y_DOWN = 136, 64


def place():
    return tuple(lax.axis_index(axis) for axis in ("normal", "strike", "depth"))


def paired(index, up, down, near, far):
    even = (index & 1) == 0
    rows = pl.ds(0, down.shape[0])
    near[...] = up[...]
    far[...] = up[...]
    near[rows, :] = jnp.where(even, up[rows, :], down[...])
    far[rows, :] = jnp.where(even, down[...], up[rows, :])


def unpaired(index, near, far, low, high):
    even = (index & 1) == 0
    rows = pl.ds(0, high.shape[0])
    low[...] = jnp.where(even, far[...], near[...])
    high[...] = jnp.where(even, near[rows, :], far[rows, :])


def beside(index, count, got, stride, low, high):
    below = pl.multiple_of(jnp.maximum(index - 1, 0) * stride, 8)
    above = pl.multiple_of(jnp.minimum(index + 1, count - 1) * stride, 8)
    low[...] = jnp.where(index > 0, got[pl.ds(below, low.shape[0]), :], 0.0)
    high[...] = jnp.where(index < count - 1, got[pl.ds(above, high.shape[0]), :], 0.0)


def pack_kernel(now_hbm, rig_hbm, xa, xb, za, zb, zd, now, rig, rw, xu, xd, zu, sems):
    copies = [pltpu.make_async_copy(rig_hbm, rig, sems.at[0]), pltpu.make_async_copy(now_hbm, now, sems.at[1])]
    for copy in copies:
        copy.start()
    for copy in copies:
        copy.wait()
    widen(rig, rw)
    lane = lane_of()
    for half in range(2):
        r = [rw[x_rows(4 + a, half), :] for a in range(4)]
        xu[pl.ds(96 + 8 * half, 8), :] = open_scale(r)
        xd[pl.ds(48 + 8 * half, 8), :] = rw[x_rows(0, half), :]
        for c in range(3):
            part, grad = open_terms([now[c, x_rows(4 + a, half), :] for a in range(4)], r)
            xu[pl.ds(16 * c + 8 * half, 8), :] = part
            xu[pl.ds(48 + 16 * c + 8 * half, 8), :] = grad
            xd[pl.ds(16 * c + 8 * half, 8), :] = now[c, x_rows(0, half), :]
    back = lambda t: [rolled(t, 3 - a) for a in range(4)]
    r = back(last_lanes(lambda rows: rw[rows, :], lane))
    parts, grads = [], []
    for c in range(3):
        part, grad = open_terms(back(last_lanes(lambda rows: now[c, rows, :], lane)), r)
        parts.append(part)
        grads.append(grad)
    zu[...] = jnp.where(
        lane < 64, interleaved(parts + [open_scale(r)], lane, 0), interleaved(grads + [None], lane, 64)
    )
    zd[...] = first_lanes(lambda c, rows: now[c, rows, :], lambda rows: rw[rows, :], lane)
    index = place()
    paired(index[0], xu, xd, xa, xb)
    paired(index[2], zu, zd, za, zb)


def from_fourth(tile, lane):
    phase = lane & 3
    out = tile
    for j in range(3):
        out = jnp.where(phase == j, rolled(tile, j - 3), out)
    return out


def advance(now, prev, rw, low, high_v, high_r, scale, ghost_z, ghost_rz, closing_z, index, store, acc, on_first):
    index_x, index_y, index_z = index
    at_x = jnp.where(index_x == 0, 2.0, 1.0).astype(F32)
    at_y = jnp.where(index_y == 0, 2.0, 1.0).astype(F32)
    at_z = jnp.where(index_z == 0, 2.0, 1.0).astype(F32)

    def along_y(c, carry):
        none = jnp.zeros((8, NZL), F32)
        v = [now[c, y_rows(y), :] for y in range(NYL)] + [high_v[1][pl.ds(8 * c, 8), :] if high_v[1] is not None else none]
        r = [rw[y_rows(y), :] for y in range(NYL)] + [high_r[1][...] if high_r[1] is not None else none]
        carried = low[1](c, v[0]) if low[1] is not None else none
        for e in range(4):
            terms = element(v[4 * e : 4 * e + 5], r[4 * e : 4 * e + 5])
            head = terms[0] * at_y if e == 0 else terms[0]
            acc[c, y_rows(4 * e), :] = head + carried
            for a in range(1, 4):
                acc[c, y_rows(4 * e + a), :] = terms[a]
            carried = terms[4]
        return carry

    lax.fori_loop(0, 3, along_y, 0)

    lane = lane_of()
    phase = lane & 3
    gm = [lane_table(phase, [D[b, b - k] if b >= k else 0 for b in range(4)]) for k in range(4)]
    gp = [None] + [lane_table(phase, [D[b, b + k] if b + k <= 4 else 0 for b in range(4)]) for k in range(1, 5)]
    cm = [lane_table(phase, [E[a, a - k] if a >= k else 0 for a in range(4)]) for k in range(4)]
    cp = [None] + [lane_table(phase, [E[a, a + k] if a + k <= 3 else 0 for a in range(4)]) for k in range(1, 4)]
    c_close = lane_table(phase, [E[a, 4] for a in range(4)])
    last = [lane_table(phase, [0, 0, 0, E[4, b]]) for b in range(5)]
    first = lane == 0
    edge = jnp.where(first, at_z, jnp.float32(1.0))

    def along_xz(n, carry):
        c, half = n >> 1, n & 1
        offset = half * 8
        rows = [pl.ds(pl.multiple_of(x * NYL + offset, 8), 8) for x in range(NXL)]
        plane = pl.ds(pl.multiple_of(16 * c + offset, 8), 8)
        v = [now[c, rows[x], :] for x in range(NXL)] + [high_v[0][plane, :]]
        r = [rw[rows[x], :] for x in range(NXL)] + [high_r[0][pl.ds(pl.multiple_of(offset, 8), 8), :]]
        carried = low[0](c, offset, plane, v[0])
        back = NZL - (4 * half + c)
        ghost_v = pltpu.roll(ghost_z, back, 1)
        ghost_r = pltpu.roll(ghost_rz, NZL - 4 * half, 1)
        closing = pltpu.roll(closing_z, back, 1)
        for e in range(2):
            terms = element(v[4 * e : 4 * e + 5], r[4 * e : 4 * e + 5])
            if e == 0:
                on_first(c, plane, carried, terms[0])
            for a in range(4):
                x = 4 * e + a
                force = terms[a] + acc[c, rows[x], :]
                if a == 0:
                    force = (terms[0] * at_x if e == 0 else terms[0]) + carried + acc[c, rows[x], :]
                vx = jnp.where(first, rolled(ghost_v, -8 * x), v[x])
                rx = jnp.where(first, rolled(ghost_r, -8 * x), r[x])
                vm = [v[x]] + [rolled(v[x], k) for k in range(1, 4)]
                vp = [None] + [rolled(vx, -k) for k in range(1, 5)]
                g = gm[0] * v[x]
                for k in range(1, 4):
                    g = g + gm[k] * vm[k]
                for k in range(1, 5):
                    g = g + gp[k] * vp[k]
                g4 = total([(D[4, 0], vm[3]), (D[4, 1], vm[2]), (D[4, 2], vm[1]), (D[4, 3], vm[0]), (D[4, 4], vp[1])])
                q = r[x] * g
                q4 = jnp.where(phase == 3, rolled(rx, -1) * g4, 0.0)
                qm = [q] + [rolled(q, k) for k in range(1, 4)]
                own = cm[0] * q
                for k in range(1, 4):
                    own = own + cm[k] * qm[k]
                for k in range(1, 4):
                    own = own + cp[k] * rolled(q, -k)
                pair = q4 + rolled(q4, -1)
                own = own + c_close * (pair + rolled(pair, -2))
                tail = last[3] * q + last[4] * q4
                for b in range(3):
                    tail = tail + last[b] * qm[3 - b]
                tail = jnp.where(first, rolled(closing, -8 * x), rolled(tail, 1))
                force = force + own * edge + tail
                after = (v[x] + v[x]) - prev[c, rows[x], :] - scale[rows[x], :] * force
                store(c, x, rows[x], plane, after)
            carried = terms[4]
        return carry

    lax.fori_loop(0, 6, along_xz, 0)


def step_scale(rho, scale):
    for x in range(NXL):
        rows = pl.ds(x * NYL, NYL)
        scale[rows, :] = np.float32(DT * DT) / rho[rows, :].astype(F32)


def axis_weight(pos, is_first):
    phase = pos & 3
    out = jnp.full(pos.shape, np.float32(2 * W0), F32)
    for b in range(1, 4):
        out = jnp.where(phase == b, np.float32(WQ[b]), out)
    return jnp.where((pos == 0) & is_first, np.float32(W0), out)


def half_kernel(
    counts, now, prev, rig, rho, xa, xb, za, zb, zd_own,
    base, yb, ya, early, mx, mz, xd, zd, rw, scale,
    acc, xu, zu, yu, yd,
):
    index = place()
    unpaired(index[0], xa, xb, xu, xd)
    unpaired(index[2], za, zb, zu, zd)
    widen(rig, rw)
    step_scale(rho, scale)
    lane = lane_of()
    has_x, has_z = (index[0] > 0).astype(F32), (index[2] > 0).astype(F32)
    kappa, diagonal = np.float32(KAPPA), np.float32(KAPPA * D[4, 4])
    for half in range(2):
        rows = pl.ds(8 * half, 8)
        mx[rows, :] = (xu[pl.ds(96 + 8 * half, 8), :] + diagonal * rw[x_rows(0, half), :]) * has_x
    own, above = zd_own[...], zu[...]
    r_first = from_fourth(own, lane)
    scale_z = (from_fourth(above, lane) + diagonal * r_first) * has_z
    mz[...] = scale_z
    closing_z = above + kappa * r_first * rolled(above, 64) + scale_z * own

    def low_x(c, offset, plane, v0):
        rows = pl.ds(pl.multiple_of(offset, 8), 8)
        grad = xu[pl.ds(pl.multiple_of(48 + 16 * c + offset, 8), 8), :]
        return xu[plane, :] + kappa * rw[rows, :] * grad + mx[rows, :] * v0

    def store(c, x, rows, plane, after):
        base[c, rows, :] = after

    def on_first(c, plane, carried, term):
        early[plane, :] = carried - term

    below = zd[...]
    advance(
        now, prev, rw, (low_x, None), (xd, None), (xd.at[pl.ds(48, 16)], None), scale,
        below, rolled(below, -3), closing_z, index, store, acc, on_first,
    )

    r = [rw[y_rows(12 + a), :] for a in range(4)]
    by_value, by_flux = open_response([scale[y_rows(12 + a), :] for a in range(4)], r)
    planes = [open_scale(r), *open_terms(by_value, r), *open_terms(by_flux, r)]
    for n, plane in enumerate(planes):
        yu[pl.ds(96 + 8 * n, 8), :] = plane
    for c in range(3):
        planes = open_terms([now[c, y_rows(12 + a), :] for a in range(4)], r)
        planes += open_terms([base[c, y_rows(12 + a), :] for a in range(4)], r)
        for n, plane in enumerate(planes):
            yu[pl.ds(24 * n + 8 * c, 8), :] = plane
        yd[pl.ds(8 * c, 8), :] = now[c, y_rows(0), :]
        yd[pl.ds(24 + 8 * c, 8), :] = base[c, y_rows(0), :]
    yd[pl.ds(48, 8), :] = rw[y_rows(0), :]
    yd[pl.ds(56, 8), :] = scale[y_rows(0), :]
    paired(index[1], yu, yd, ya, yb)


def open_response(scale, r):
    by_value = [scale[a] * total([(E[a, b] * D[b, 4], r[b]) for b in range(4)]) for a in range(4)]
    by_flux = [scale[a] * np.float32(E[a, 4]) for a in range(4)]
    return by_value, by_flux


def whole_kernel(
    counts, base, now, rw, scale, early, yb, ya, mx, xd, zd, nodes_hbm, ids_hbm,
    out, kept, to_depth, xa2, xb2, zd2, my, y_low, y_high, r_high,
    slip, yu, yd, xu2, xd2, zu2, nodes, ids, sems,
):
    middle = counts[0] // 2
    index = place()
    lane = lane_of()
    kappa, diagonal = np.float32(KAPPA), np.float32(KAPPA * D[4, 4])
    d44 = np.float32(D[4, 4])
    copies = [pltpu.make_async_copy(nodes_hbm, nodes, sems.at[0]), pltpu.make_async_copy(ids_hbm, ids, sems.at[1])]
    for copy in copies:
        copy.start()
    unpaired(index[1], ya, yb, yu, yd)
    for c in range(3):
        for k in range(16):
            rows = pl.ds(8 * k, 8)
            values = base[c, rows, :]
            out[c, rows, :] = values
            kept[c, rows, :] = values
    r = [rw[y_rows(12 + a), :] for a in range(4)]
    by_value, by_flux = open_response([scale[y_rows(12 + a), :] for a in range(4)], r)
    own_scale = open_scale(r)
    r0, s0 = rw[y_rows(0), :], scale[y_rows(0), :]
    r_above, s_above = yd[pl.ds(48, 8), :], yd[pl.ds(56, 8), :]
    r_high[...] = r_above
    gain, value_part, value_grad, flux_part, flux_grad = (yu[pl.ds(96 + 8 * n, 8), :] for n in range(5))
    gain = (gain + diagonal * r0) * (index[1] > 0).astype(F32)
    my[...] = gain
    for c in range(3):
        plane = pl.ds(8 * c, 8)
        part, grad, part2, grad2 = (yu[pl.ds(24 * n + 8 * c, 8), :] for n in range(4))
        v0 = now[c, y_rows(0), :]
        after = base[c, y_rows(0), :] - s0 * (part + kappa * r0 * grad + gain * v0)
        out[c, y_rows(0), :] = after
        kept[c, y_rows(0), :] = after
        flux = r0 * (grad + d44 * v0)
        y_low[plane, :] = (part2 - value_part * v0 - flux_part * flux) + kappa * r0 * (
            grad2 - value_grad * v0 - flux_grad * flux
        )
        above = yd[plane, :]
        part, grad = open_terms([now[c, y_rows(12 + a), :] for a in range(4)], r)
        flux = r_above * (grad + d44 * above)
        y_high[plane, :] = yd[pl.ds(24 + 8 * c, 8), :] - s_above * (part + own_scale * above + kappa * flux)
        for a in range(4):
            after = base[c, y_rows(12 + a), :] - by_value[a] * above - by_flux[a] * flux
            out[c, y_rows(12 + a), :] = after
            kept[c, y_rows(12 + a), :] = after

    on_one, on_two = index[0] == middle - 1, index[0] == middle
    for half in range(2):
        rows = pl.ds(8 * half, 8)
        r = [rw[x_rows(x, half), :] for x in range(8)] + [xd[pl.ds(48 + 8 * half, 8), :]]
        y_pos = lax.broadcasted_iota(jnp.int32, (8, NZL), 0) + 8 * half
        face = axis_weight(y_pos, index[1] == 0) * axis_weight(lane, index[2] == 0) * np.float32(W0)
        for c in range(3):
            plane = pl.ds(16 * c + 8 * half, 8)
            v = [out[c, x_rows(x, half), :] for x in range(8)]
            part, grad = open_terms(v[4:], r[4:8])
            sent = part + kappa * r[8] * grad
            xu2[plane, :] = sent
            xd2[plane, :] = v[0]
            here = early[plane, :] + mx[rows, :] * v[0] - first_term(v[:5], r[:5])
            slip[plane, :] = face * jnp.where(on_one, sent, jnp.where(on_two, here, 0.0))
    back = lambda t: [rolled(t, 3 - a) for a in range(4)]
    r = back(last_lanes(lambda rows: rw[rows, :], lane))
    sent = []
    for c in range(3):
        part, grad = open_terms(back(last_lanes(lambda rows: out[c, rows, :], lane)), r)
        sent.append(part + kappa * zd[...] * grad)
    zu2[...] = interleaved(sent + [None], lane, 0)
    zd2[...] = first_lanes(lambda c, rows: out[c, rows, :], None, lane)
    paired(index[0], xu2, xd2, xa2, xb2)
    for copy in copies:
        copy.wait()
    tile = patch_tile(counts[2], slip[...], nodes[...], ids[...])
    for d in range(counts[2]):
        to_depth[pl.ds(16 * d, 8), :] = jnp.where(d > index[2], zu2[...], zd2[...])
        to_depth[pl.ds(16 * d + 8, 8), :] = jnp.broadcast_to(tile[d : d + 1, :], (8, NZL))


def sum_kernel(counts, got, to_face):
    row = got[pl.ds(8, 8), :]
    for d in range(1, counts[2]):
        row = row + got[pl.ds(16 * d + 8, 8), :]
    for k in range(counts[0] * counts[1] // 8):
        to_face[pl.ds(8 * k, 8), :] = row


def second_kernel(
    counts, now, prev, rw, scale, xa2, xb2, got_z, zd2_own, mx, my, mz, xd, zd, y_low, y_high, r_high,
    out, acc, xu2, xd2, zu2, zd2,
):
    index = place()
    unpaired(index[0], xa2, xb2, xu2, xd2)
    beside(index[2], counts[2], got_z, 16, zu2, zd2)
    closing_z = zu2[...] + mz[...] * zd2_own[...]

    def low_x(c, offset, plane, v0):
        return xu2[plane, :] + mx[pl.ds(pl.multiple_of(offset, 8), 8), :] * v0

    def low_y(c, v0):
        return y_low[pl.ds(pl.multiple_of(8 * c, 8), 8), :] + my[...] * v0

    def store(c, x, rows, plane, after):
        out[c, rows, :] = after

    advance(
        now, prev, rw, (low_x, low_y), (xd2, y_high), (xd.at[pl.ds(48, 16)], r_high), scale,
        zd2[...], rolled(zd[...], -3), closing_z, index, store, acc, lambda *args: None,
    )


def patch_tile(count_d, slip, node, patch):
    pairs = node.shape[-1]
    hot_z = (lax.broadcasted_iota(jnp.int32, (NZL, pairs), 0) == (node & (NZL - 1))).astype(F32)
    at_z = jnp.dot(slip, hot_z, precision=HIGHEST, preferred_element_type=F32)
    row_y = lax.broadcasted_iota(jnp.int32, (NYL, pairs), 0) == (node >> 7)
    owner = patch >> 1
    owner_d = owner & (count_d - 1)
    slot = ((owner >> (count_d.bit_length() - 1)) << 1) + (patch & 1)
    hot_slot = lax.broadcasted_iota(jnp.int32, (32, pairs), 0) == slot
    spread = []
    for c in range(3):
        picked = jnp.sum(jnp.where(row_y, at_z[NYL * c : NYL * (c + 1), :], 0.0), axis=0, keepdims=True)
        spread.append(jnp.where(hot_slot, picked, 0.0))
    spread.append(jnp.zeros((32, pairs), F32))
    hot_d = (lax.broadcasted_iota(jnp.int32, (8, pairs), 0) == owner_d).astype(F32)
    return lax.dot_general(
        hot_d, jnp.concatenate(spread, axis=0), (((1,), (1,)), ((), ())), precision=HIGHEST,
        preferred_element_type=F32,
    )


def final_kernel(tiles, out):
    mine = lax.axis_index("strike") * 2
    summed = jnp.sum(tiles[...], axis=0, keepdims=True)
    lane = lax.broadcasted_iota(jnp.int32, (2, NZL), 1)
    place = lax.broadcasted_iota(jnp.int32, (2, NZL), 0)
    for c in range(3):
        hit = lane == 32 * c + mine + place
        out[:, pl.ds(c, 1)] = jnp.sum(jnp.where(hit, summed, 0.0), axis=1, keepdims=True)


def call(kernel, name, outs, scratch=(), flops=0, moved=0, in_specs=None):
    specs = {} if in_specs is None else {"in_specs": in_specs}
    return pl.pallas_call(
        kernel,
        out_shape=[jax.ShapeDtypeStruct(shape, F32) for shape in outs],
        scratch_shapes=[pltpu.VMEM(shape, F32) if isinstance(shape, tuple) else shape for shape in scratch],
        compiler_params=pltpu.CompilerParams(vmem_limit_bytes=16 * 2**20),
        cost_estimate=pl.CostEstimate(flops=flops, bytes_accessed=moved, transcendentals=0),
        name=name,
        **specs,
    )


def swap_near(value, axis):
    return lax.ppermute(value, axis, [(i, i ^ 1) for i in range(lax.axis_size(axis))])


def swap_far(value, axis):
    lower = range(1, lax.axis_size(axis) - 1, 2)
    return lax.ppermute(value, axis, [(i, i + 1) for i in lower] + [(i + 1, i) for i in lower])


def local(field_now, field_prev, rigidity, density, fault_nodes, patch_ids):
    axes = ("normal", "strike", "depth")
    counts = tuple(lax.axis_size(a) for a in axes)
    flat, block, tile = (3, ROWS, NZL), (ROWS, NZL), (8, NZL)
    now, prev = field_now.reshape(flat), field_prev.reshape(flat)
    rig, rho = rigidity.reshape(block), density.reshape(block)
    nodes, ids = fault_nodes.reshape(1, -1), patch_ids.reshape(1, -1)
    x_up, x_down, y_up, y_down = ((n, NZL) for n in (X_UP, X_DOWN, Y_UP, Y_DOWN))
    faces, strip = (48, NZL), (24, NZL)
    xa, xb, za, zb, zd_own = call(
        pack_kernel, "pack", [x_up, x_up, tile, tile, tile],
        [pltpu.VMEM(flat, F32), pltpu.VMEM(block, jnp.bfloat16), block, x_up, x_down, tile,
         pltpu.SemaphoreType.DMA((2,))],
        flops=2_000_000, moved=400_000, in_specs=[pl.BlockSpec(memory_space=pltpu.HBM)] * 2,
    )(now, rig)
    xa, xb = swap_near(xa, "normal"), swap_far(xb, "normal")
    zb, za = swap_far(zb, "depth"), swap_near(za, "depth")
    base, yb, ya, early, mx, mz, xd, zd, rw, scale = call(
        functools.partial(half_kernel, counts), "half",
        [flat, y_up, y_up, faces, (16, NZL), tile, x_down, tile, block, block],
        [flat, x_up, tile, y_up, y_down], flops=10_000_000, moved=900_000,
    )(now, prev, rig, rho, xa, xb, za, zb, zd_own)
    yb, ya = swap_far(yb, "strike"), swap_near(ya, "strike")
    inside, outside = pl.BlockSpec(memory_space=pltpu.VMEM), pl.BlockSpec(memory_space=pltpu.HBM)
    mid, kept, to_depth, xa2, xb2, zd2, my, y_low, y_high, r_high = call(
        functools.partial(whole_kernel, counts), "whole",
        [flat, flat, (16 * counts[2], NZL), faces, faces, tile, tile, strip, strip, tile],
        [faces, y_up, y_down, faces, faces, tile, pltpu.VMEM(nodes.shape, jnp.int32), pltpu.VMEM(ids.shape, jnp.int32),
         pltpu.SemaphoreType.DMA((2,))],
        flops=2_000_000, moved=900_000, in_specs=[inside] * 10 + [outside] * 2,
    )(base, now, rw, scale, early, yb, ya, mx, xd, zd, nodes, ids)
    got_z = lax.all_to_all(to_depth, "depth", 0, 0, tiled=True)
    (to_face,) = call(
        functools.partial(sum_kernel, counts), "add", [(counts[0] * counts[1], NZL)], flops=10_000, moved=80_000,
    )(got_z)
    got_face = lax.all_to_all(to_face, ("normal", "strike"), 0, 0, tiled=True)
    xa2, xb2 = swap_near(xa2, "normal"), swap_far(xb2, "normal")
    (share,) = call(final_kernel, "final", [(2, 3)], flops=10_000, moved=10_000)(got_face)
    (following,) = call(
        functools.partial(second_kernel, counts), "second", [flat], [flat, faces, faces, tile, tile],
        flops=10_000_000, moved=900_000,
    )(kept, now, rw, scale, xa2, xb2, got_z, zd2, mx, my, mz, xd, zd, y_low, y_high, r_high)
    return following.reshape(field_now.shape), mid.reshape(field_now.shape), share


def solution(mesh):
    field = P(None, "normal", "strike", "depth")
    cells = P("normal", "strike", "depth")
    pairs = P("strike", "depth", None)
    return jax.shard_map(
        local,
        mesh=mesh,
        in_specs=(field, field, cells, cells, pairs, pairs),
        out_specs=(field, field, P(("strike", "depth"), None)),
        check_vma=False,
    )
```

```python
import functools
import math

import jax
import jax.numpy as jnp
import numpy as np
from jax import lax
from jax.experimental import pallas as pl
from jax.experimental.pallas import tpu as pltpu
from jax.sharding import PartitionSpec as P

DT = 0.03
NXL, NYL, NZL = 8, 16, 128
ROWS = NXL * NYL
F32 = jnp.float32
HIGHEST = lax.Precision.HIGHEST


def gll_tables():
    spread = math.sqrt(3.0 / 7.0)
    points = np.array([-1.0, -spread, 0.0, spread, 1.0])
    weights = np.array([0.1, 49.0 / 90.0, 32.0 / 45.0, 49.0 / 90.0, 0.1]) * 0.5
    derivative = np.zeros((5, 5))
    for b in range(5):
        for a in range(5):
            if a == b:
                derivative[b, a] = sum(1.0 / (points[b] - points[o]) for o in range(5) if o != b)
            else:
                row = np.prod([points[b] - points[o] for o in range(5) if o != b and o != a])
                col = np.prod([points[a] - points[o] for o in range(5) if o != a and o != b])
                derivative[b, a] = row / (col * (points[a] - points[b]))
    return weights, 2.0 * derivative


WQ, D = gll_tables()
W0 = float(WQ[0])
NODE_W = np.array([2 * WQ[0], WQ[1], WQ[2], WQ[3], 2 * WQ[0]])
E = (WQ[:, None] * D).T / NODE_W[:, None]
KAPPA = float(E[4, 4])


def total(pairs):
    acc = None
    for const, arr in pairs:
        if abs(const) < 1e-12:
            continue
        term = arr * np.float32(const)
        acc = term if acc is None else acc + term
    return acc


def element(v, r):
    twice = v[2] + v[2]
    s0, s1 = v[0] + v[4] - twice, v[1] + v[3] - twice
    d0, d1 = v[0] - v[4], v[1] - v[3]
    ev = [total([((D[b, 0] + D[b, 4]) / 2, s0), ((D[b, 1] + D[b, 3]) / 2, s1)]) for b in (0, 1)]
    od = [total([((D[b, 0] - D[b, 4]) / 2, d0), ((D[b, 1] - D[b, 3]) / 2, d1)]) for b in (0, 1)]
    g2 = total([(D[2, 0], d0), (D[2, 1], d1)])
    q = [r[0] * (od[0] + ev[0]), r[1] * (od[1] + ev[1]), r[2] * g2, r[3] * (od[1] - ev[1]), r[4] * (od[0] - ev[0])]
    p0, m0, p1, m1 = q[0] + q[4], q[0] - q[4], q[1] + q[3], q[1] - q[3]
    ec = [total([((E[a, 0] + E[a, 4]) / 2, p0), ((E[a, 1] + E[a, 3]) / 2, p1), (E[a, 2], q[2])]) for a in (0, 1)]
    oc = [total([((E[a, 0] - E[a, 4]) / 2, m0), ((E[a, 1] - E[a, 3]) / 2, m1)]) for a in (0, 1)]
    c2 = total([(E[2, 0], m0), (E[2, 1], m1)])
    return [oc[0] + ec[0], oc[1] + ec[1], c2, oc[1] - ec[1], oc[0] - ec[0]]


def first_term(v, r):
    twice = v[2] + v[2]
    s0, s1 = v[0] + v[4] - twice, v[1] + v[3] - twice
    d0, d1 = v[0] - v[4], v[1] - v[3]
    ev = [total([((D[b, 0] + D[b, 4]) / 2, s0), ((D[b, 1] + D[b, 3]) / 2, s1)]) for b in (0, 1)]
    od = [total([((D[b, 0] - D[b, 4]) / 2, d0), ((D[b, 1] - D[b, 3]) / 2, d1)]) for b in (0, 1)]
    g2 = total([(D[2, 0], d0), (D[2, 1], d1)])
    q = [r[0] * (od[0] + ev[0]), r[1] * (od[1] + ev[1]), r[2] * g2, r[3] * (od[1] - ev[1]), r[4] * (od[0] - ev[0])]
    return total([(E[0, b], q[b]) for b in range(5)])


def open_terms(v, r):
    flux = [r[b] * total([(D[b, a], v[a]) for a in range(4)]) for b in range(4)]
    part = total([(E[4, b], flux[b]) for b in range(4)])
    grad = total([(D[4, a], v[a]) for a in range(4)])
    return part, grad


def open_scale(r):
    return total([(E[4, b] * D[b, 4], r[b]) for b in range(4)])


def rolled(x, shift):
    shift = shift % NZL
    return x if shift == 0 else pltpu.roll(x, shift, 1)


def lane_of():
    return lax.broadcasted_iota(jnp.int32, (8, NZL), 1)


def lane_table(phase, values):
    out = jnp.full((8, NZL), np.float32(values[0]), F32)
    for b in range(1, 4):
        out = jnp.where(phase == b, np.float32(values[b]), out)
    return out


def x_rows(x, half):
    return pl.ds(x * NYL + half * 8, 8)


def y_rows(y):
    return pl.ds(y, 8, stride=NYL)


def first_lanes(read, read_r, lane):
    out = jnp.zeros((8, NZL), F32)
    for k in range(16):
        rows = pl.ds(8 * k, 8)
        for c in range(3 if read_r is None else 4):
            src = read_r(rows) if c == 3 else read(c, rows)
            out = jnp.where(lane == 4 * k + c, rolled(src, 4 * k + c), out)
    return out


def last_lanes(read, lane):
    out = jnp.zeros((8, NZL), F32)
    for k in range(16):
        out = jnp.where((lane >> 2) == k, rolled(read(pl.ds(8 * k, 8)), 4 * k + 4), out)
    return out


def interleaved(parts, lane, base):
    out = jnp.zeros((8, NZL), F32)
    for j, part in enumerate(parts):
        if part is None:
            continue
        out = jnp.where((lane >= base) & (lane < base + 64) & ((lane & 3) == j), rolled(part, base + j - 3), out)
    return out


def widen(src, dst):
    for x in range(NXL):
        dst[pl.ds(x * NYL, NYL), :] = src[pl.ds(x * NYL, NYL), :].astype(F32)


X_UP, X_DOWN = 112, 64
Y_UP, Y_DOWN = 136, 64


def place():
    return tuple(lax.axis_index(axis) for axis in ("normal", "strike", "depth"))


def paired(index, up, down, near, far):
    even = (index & 1) == 0
    rows = pl.ds(0, down.shape[0])
    near[...] = up[...]
    far[...] = up[...]
    near[rows, :] = jnp.where(even, up[rows, :], down[...])
    far[rows, :] = jnp.where(even, down[...], up[rows, :])


def unpaired(index, near, far, low, high):
    even = (index & 1) == 0
    rows = pl.ds(0, high.shape[0])
    low[...] = jnp.where(even, far[...], near[...])
    high[...] = jnp.where(even, near[rows, :], far[rows, :])


def beside(index, count, got, group, low, high):
    below = pl.multiple_of((group * count + jnp.maximum(index - 1, 0)) * 8, 8)
    above = pl.multiple_of((group * count + jnp.minimum(index + 1, count - 1)) * 8, 8)
    low[...] = jnp.where(index > 0, got[pl.ds(below, low.shape[0]), :], 0.0)
    high[...] = jnp.where(index < count - 1, got[pl.ds(above, high.shape[0]), :], 0.0)


def pack_kernel(now_hbm, rig_hbm, xa, xb, za, zb, zd, now, rig, rw, xu, xd, zu, sems):
    copies = [pltpu.make_async_copy(rig_hbm, rig, sems.at[0]), pltpu.make_async_copy(now_hbm, now, sems.at[1])]
    for copy in copies:
        copy.start()
    for copy in copies:
        copy.wait()
    widen(rig, rw)
    lane = lane_of()
    for half in range(2):
        r = [rw[x_rows(4 + a, half), :] for a in range(4)]
        xu[pl.ds(96 + 8 * half, 8), :] = open_scale(r)
        xd[pl.ds(48 + 8 * half, 8), :] = rw[x_rows(0, half), :]
        for c in range(3):
            part, grad = open_terms([now[c, x_rows(4 + a, half), :] for a in range(4)], r)
            xu[pl.ds(16 * c + 8 * half, 8), :] = part
            xu[pl.ds(48 + 16 * c + 8 * half, 8), :] = grad
            xd[pl.ds(16 * c + 8 * half, 8), :] = now[c, x_rows(0, half), :]
    back = lambda t: [rolled(t, 3 - a) for a in range(4)]
    r = back(last_lanes(lambda rows: rw[rows, :], lane))
    parts, grads = [], []
    for c in range(3):
        part, grad = open_terms(back(last_lanes(lambda rows: now[c, rows, :], lane)), r)
        parts.append(part)
        grads.append(grad)
    zu[...] = jnp.where(
        lane < 64, interleaved(parts + [open_scale(r)], lane, 0), interleaved(grads + [None], lane, 64)
    )
    zd[...] = first_lanes(lambda c, rows: now[c, rows, :], lambda rows: rw[rows, :], lane)
    index = place()
    paired(index[0], xu, xd, xa, xb)
    paired(index[2], zu, zd, za, zb)


def from_fourth(tile, lane):
    phase = lane & 3
    out = tile
    for j in range(3):
        out = jnp.where(phase == j, rolled(tile, j - 3), out)
    return out


def advance(now, prev, rw, low, high_v, high_r, scale, ghost_z, ghost_rz, closing_z, index, store, acc, on_first):
    index_x, index_y, index_z = index
    at_x = jnp.where(index_x == 0, 2.0, 1.0).astype(F32)
    at_y = jnp.where(index_y == 0, 2.0, 1.0).astype(F32)
    at_z = jnp.where(index_z == 0, 2.0, 1.0).astype(F32)

    def along_y(c, carry):
        none = jnp.zeros((8, NZL), F32)
        v = [now[c, y_rows(y), :] for y in range(NYL)] + [high_v[1][pl.ds(8 * c, 8), :] if high_v[1] is not None else none]
        r = [rw[y_rows(y), :] for y in range(NYL)] + [high_r[1][...] if high_r[1] is not None else none]
        carried = low[1](c, v[0]) if low[1] is not None else none
        for e in range(4):
            terms = element(v[4 * e : 4 * e + 5], r[4 * e : 4 * e + 5])
            head = terms[0] * at_y if e == 0 else terms[0]
            acc[c, y_rows(4 * e), :] = head + carried
            for a in range(1, 4):
                acc[c, y_rows(4 * e + a), :] = terms[a]
            carried = terms[4]
        return carry

    lax.fori_loop(0, 3, along_y, 0)

    lane = lane_of()
    phase = lane & 3
    gm = [lane_table(phase, [D[b, b - k] if b >= k else 0 for b in range(4)]) for k in range(4)]
    gp = [None] + [lane_table(phase, [D[b, b + k] if b + k <= 4 else 0 for b in range(4)]) for k in range(1, 5)]
    cm = [lane_table(phase, [E[a, a - k] if a >= k else 0 for a in range(4)]) for k in range(4)]
    cp = [None] + [lane_table(phase, [E[a, a + k] if a + k <= 3 else 0 for a in range(4)]) for k in range(1, 4)]
    c_close = lane_table(phase, [E[a, 4] for a in range(4)])
    last = [lane_table(phase, [0, 0, 0, E[4, b]]) for b in range(5)]
    first = lane == 0
    edge = jnp.where(first, at_z, jnp.float32(1.0))

    def along_xz(n, carry):
        c, half = n >> 1, n & 1
        offset = half * 8
        rows = [pl.ds(pl.multiple_of(x * NYL + offset, 8), 8) for x in range(NXL)]
        plane = pl.ds(pl.multiple_of(16 * c + offset, 8), 8)
        v = [now[c, rows[x], :] for x in range(NXL)] + [high_v[0][plane, :]]
        r = [rw[rows[x], :] for x in range(NXL)] + [high_r[0][pl.ds(pl.multiple_of(offset, 8), 8), :]]
        carried = low[0](c, offset, plane, v[0])
        back = NZL - (4 * half + c)
        ghost_v = pltpu.roll(ghost_z, back, 1)
        ghost_r = pltpu.roll(ghost_rz, NZL - 4 * half, 1)
        closing = pltpu.roll(closing_z, back, 1)
        for e in range(2):
            terms = element(v[4 * e : 4 * e + 5], r[4 * e : 4 * e + 5])
            if e == 0:
                on_first(c, plane, carried, terms[0])
            for a in range(4):
                x = 4 * e + a
                force = terms[a] + acc[c, rows[x], :]
                if a == 0:
                    force = (terms[0] * at_x if e == 0 else terms[0]) + carried + acc[c, rows[x], :]
                vx = jnp.where(first, rolled(ghost_v, -8 * x), v[x])
                rx = jnp.where(first, rolled(ghost_r, -8 * x), r[x])
                vm = [v[x]] + [rolled(v[x], k) for k in range(1, 4)]
                vp = [None] + [rolled(vx, -k) for k in range(1, 5)]
                g = gm[0] * v[x]
                for k in range(1, 4):
                    g = g + gm[k] * vm[k]
                for k in range(1, 5):
                    g = g + gp[k] * vp[k]
                g4 = total([(D[4, 0], vm[3]), (D[4, 1], vm[2]), (D[4, 2], vm[1]), (D[4, 3], vm[0]), (D[4, 4], vp[1])])
                q = r[x] * g
                q4 = jnp.where(phase == 3, rolled(rx, -1) * g4, 0.0)
                qm = [q] + [rolled(q, k) for k in range(1, 4)]
                own = cm[0] * q
                for k in range(1, 4):
                    own = own + cm[k] * qm[k]
                for k in range(1, 4):
                    own = own + cp[k] * rolled(q, -k)
                pair = q4 + rolled(q4, -1)
                own = own + c_close * (pair + rolled(pair, -2))
                tail = last[3] * q + last[4] * q4
                for b in range(3):
                    tail = tail + last[b] * qm[3 - b]
                tail = jnp.where(first, rolled(closing, -8 * x), rolled(tail, 1))
                force = force + own * edge + tail
                after = (v[x] + v[x]) - prev[c, rows[x], :] - scale[rows[x], :] * force
                store(c, x, rows[x], plane, after)
            carried = terms[4]
        return carry

    lax.fori_loop(0, 6, along_xz, 0)


def step_scale(rho, scale):
    for x in range(NXL):
        rows = pl.ds(x * NYL, NYL)
        scale[rows, :] = np.float32(DT * DT) / rho[rows, :].astype(F32)


def axis_weight(pos, is_first):
    phase = pos & 3
    out = jnp.full(pos.shape, np.float32(2 * W0), F32)
    for b in range(1, 4):
        out = jnp.where(phase == b, np.float32(WQ[b]), out)
    return jnp.where((pos == 0) & is_first, np.float32(W0), out)


def half_kernel(
    counts, now, prev, rig, rho, xa, xb, za, zb, zd_own, nodes_in, ids_in,
    base, yb, ya, early, mx, mz, xd, zd, rw, scale, nodes, ids,
    acc, xu, zu, yu, yd,
):
    nodes[...] = nodes_in[...]
    ids[...] = ids_in[...]
    index = place()
    unpaired(index[0], xa, xb, xu, xd)
    unpaired(index[2], za, zb, zu, zd)
    widen(rig, rw)
    step_scale(rho, scale)
    lane = lane_of()
    has_x, has_z = (index[0] > 0).astype(F32), (index[2] > 0).astype(F32)
    kappa, diagonal = np.float32(KAPPA), np.float32(KAPPA * D[4, 4])
    for half in range(2):
        rows = pl.ds(8 * half, 8)
        mx[rows, :] = (xu[pl.ds(96 + 8 * half, 8), :] + diagonal * rw[x_rows(0, half), :]) * has_x
    own, above = zd_own[...], zu[...]
    r_first = from_fourth(own, lane)
    scale_z = (from_fourth(above, lane) + diagonal * r_first) * has_z
    mz[...] = scale_z
    closing_z = above + kappa * r_first * rolled(above, 64) + scale_z * own

    def low_x(c, offset, plane, v0):
        rows = pl.ds(pl.multiple_of(offset, 8), 8)
        grad = xu[pl.ds(pl.multiple_of(48 + 16 * c + offset, 8), 8), :]
        return xu[plane, :] + kappa * rw[rows, :] * grad + mx[rows, :] * v0

    def store(c, x, rows, plane, after):
        base[c, rows, :] = after

    def on_first(c, plane, carried, term):
        early[plane, :] = carried - term

    below = zd[...]
    advance(
        now, prev, rw, (low_x, None), (xd, None), (xd.at[pl.ds(48, 16)], None), scale,
        below, rolled(below, -3), closing_z, index, store, acc, on_first,
    )

    r = [rw[y_rows(12 + a), :] for a in range(4)]
    by_value, by_flux = open_response([scale[y_rows(12 + a), :] for a in range(4)], r)
    planes = [open_scale(r), *open_terms(by_value, r), *open_terms(by_flux, r)]
    for n, plane in enumerate(planes):
        yu[pl.ds(96 + 8 * n, 8), :] = plane
    for c in range(3):
        planes = open_terms([now[c, y_rows(12 + a), :] for a in range(4)], r)
        planes += open_terms([base[c, y_rows(12 + a), :] for a in range(4)], r)
        for n, plane in enumerate(planes):
            yu[pl.ds(24 * n + 8 * c, 8), :] = plane
        yd[pl.ds(8 * c, 8), :] = now[c, y_rows(0), :]
        yd[pl.ds(24 + 8 * c, 8), :] = base[c, y_rows(0), :]
    yd[pl.ds(48, 8), :] = rw[y_rows(0), :]
    yd[pl.ds(56, 8), :] = scale[y_rows(0), :]
    paired(index[1], yu, yd, ya, yb)


def open_response(scale, r):
    by_value = [scale[a] * total([(E[a, b] * D[b, 4], r[b]) for b in range(4)]) for a in range(4)]
    by_flux = [scale[a] * np.float32(E[a, 4]) for a in range(4)]
    return by_value, by_flux


def whole_kernel(
    counts, base, now, rw, scale, early, yb, ya, mx, xd, zd, nodes, ids,
    out, kept, to_depth, xa2, xb2, zd2, my, y_low, y_high, r_high,
    slip, yu, yd, xu2, xd2, zu2,
):
    middle = counts[0] // 2
    index = place()
    lane = lane_of()
    kappa, diagonal = np.float32(KAPPA), np.float32(KAPPA * D[4, 4])
    d44 = np.float32(D[4, 4])
    unpaired(index[1], ya, yb, yu, yd)
    for c in range(3):
        for k in range(16):
            rows = pl.ds(8 * k, 8)
            values = base[c, rows, :]
            out[c, rows, :] = values
            kept[c, rows, :] = values
    r = [rw[y_rows(12 + a), :] for a in range(4)]
    by_value, by_flux = open_response([scale[y_rows(12 + a), :] for a in range(4)], r)
    own_scale = open_scale(r)
    r0, s0 = rw[y_rows(0), :], scale[y_rows(0), :]
    r_above, s_above = yd[pl.ds(48, 8), :], yd[pl.ds(56, 8), :]
    r_high[...] = r_above
    gain, value_part, value_grad, flux_part, flux_grad = (yu[pl.ds(96 + 8 * n, 8), :] for n in range(5))
    gain = (gain + diagonal * r0) * (index[1] > 0).astype(F32)
    my[...] = gain
    for c in range(3):
        plane = pl.ds(8 * c, 8)
        part, grad, part2, grad2 = (yu[pl.ds(24 * n + 8 * c, 8), :] for n in range(4))
        v0 = now[c, y_rows(0), :]
        after = base[c, y_rows(0), :] - s0 * (part + kappa * r0 * grad + gain * v0)
        out[c, y_rows(0), :] = after
        kept[c, y_rows(0), :] = after
        flux = r0 * (grad + d44 * v0)
        y_low[plane, :] = (part2 - value_part * v0 - flux_part * flux) + kappa * r0 * (
            grad2 - value_grad * v0 - flux_grad * flux
        )
        above = yd[plane, :]
        part, grad = open_terms([now[c, y_rows(12 + a), :] for a in range(4)], r)
        flux = r_above * (grad + d44 * above)
        y_high[plane, :] = yd[pl.ds(24 + 8 * c, 8), :] - s_above * (part + own_scale * above + kappa * flux)
        for a in range(4):
            after = base[c, y_rows(12 + a), :] - by_value[a] * above - by_flux[a] * flux
            out[c, y_rows(12 + a), :] = after
            kept[c, y_rows(12 + a), :] = after

    on_one, on_two = index[0] == middle - 1, index[0] == middle
    for half in range(2):
        rows = pl.ds(8 * half, 8)
        r = [rw[x_rows(x, half), :] for x in range(8)] + [xd[pl.ds(48 + 8 * half, 8), :]]
        y_pos = lax.broadcasted_iota(jnp.int32, (8, NZL), 0) + 8 * half
        face = axis_weight(y_pos, index[1] == 0) * axis_weight(lane, index[2] == 0) * np.float32(W0)
        for c in range(3):
            plane = pl.ds(16 * c + 8 * half, 8)
            v = [out[c, x_rows(x, half), :] for x in range(8)]
            part, grad = open_terms(v[4:], r[4:8])
            sent = part + kappa * r[8] * grad
            xu2[plane, :] = sent
            xd2[plane, :] = v[0]
            here = early[plane, :] + mx[rows, :] * v[0] - first_term(v[:5], r[:5])
            slip[plane, :] = face * jnp.where(on_one, sent, jnp.where(on_two, here, 0.0))
    back = lambda t: [rolled(t, 3 - a) for a in range(4)]
    r = back(last_lanes(lambda rows: rw[rows, :], lane))
    sent = []
    for c in range(3):
        part, grad = open_terms(back(last_lanes(lambda rows: out[c, rows, :], lane)), r)
        sent.append(part + kappa * zd[...] * grad)
    zu2[...] = interleaved(sent + [None], lane, 0)
    zd2[...] = first_lanes(lambda c, rows: out[c, rows, :], None, lane)
    paired(index[0], xu2, xd2, xa2, xb2)
    tile = patch_tile(counts[2], slip[...], nodes[...], ids[...])
    for d in range(counts[2]):
        chunk = with_row(jnp.where(d > index[2], zu2[...], zd2[...]), tile[d : d + 1, :], lane)
        for n in range(counts[0]):
            to_depth[pl.ds(8 * (n * counts[2] + d), 8), :] = chunk


def with_row(halo, row, lane):
    sub = lax.broadcasted_iota(jnp.int32, (8, NZL), 0)
    row = jnp.broadcast_to(row, (8, NZL))
    spread = jnp.where(sub == 0, rolled(row, 64), jnp.where(sub == 1, row, 0.0))
    return jnp.where(lane < 64, halo, spread)


def sum_kernel(counts, got, to_strike):
    total_tile = got[pl.ds(0, 8), :]
    for n in range(1, counts[0] * counts[2]):
        total_tile = total_tile + got[pl.ds(8 * n, 8), :]
    lane = lane_of()
    low = jnp.broadcast_to(rolled(total_tile, 64)[0:1, :], (8, NZL))
    high = jnp.broadcast_to(total_tile[1:2, :], (8, NZL))
    row = jnp.where(lane < 64, low, high)
    for k in range((counts[1] + 7) // 8):
        to_strike[pl.ds(8 * k, min(8, counts[1])), :] = row[: min(8, counts[1]), :]


def second_kernel(
    counts, now, prev, rw, scale, xa2, xb2, got_z, zd2_own, mx, my, mz, xd, zd, y_low, y_high, r_high,
    out, acc, xu2, xd2, zu2, zd2,
):
    index = place()
    unpaired(index[0], xa2, xb2, xu2, xd2)
    beside(index[2], counts[2], got_z, index[0], zu2, zd2)
    closing_z = zu2[...] + mz[...] * zd2_own[...]

    def low_x(c, offset, plane, v0):
        return xu2[plane, :] + mx[pl.ds(pl.multiple_of(offset, 8), 8), :] * v0

    def low_y(c, v0):
        return y_low[pl.ds(pl.multiple_of(8 * c, 8), 8), :] + my[...] * v0

    def store(c, x, rows, plane, after):
        out[c, rows, :] = after

    advance(
        now, prev, rw, (low_x, low_y), (xd2, y_high), (xd.at[pl.ds(48, 16)], r_high), scale,
        zd2[...], rolled(zd[...], -3), closing_z, index, store, acc, lambda *args: None,
    )


def patch_tile(count_d, slip, node, patch):
    pairs = node.shape[-1]
    hot_z = (lax.broadcasted_iota(jnp.int32, (NZL, pairs), 0) == (node & (NZL - 1))).astype(F32)
    at_z = jnp.dot(slip, hot_z, precision=HIGHEST, preferred_element_type=F32)
    row_y = lax.broadcasted_iota(jnp.int32, (NYL, pairs), 0) == (node >> 7)
    owner = patch >> 1
    owner_d = owner & (count_d - 1)
    slot = ((owner >> (count_d.bit_length() - 1)) << 1) + (patch & 1)
    hot_slot = lax.broadcasted_iota(jnp.int32, (32, pairs), 0) == slot
    spread = []
    for c in range(3):
        picked = jnp.sum(jnp.where(row_y, at_z[NYL * c : NYL * (c + 1), :], 0.0), axis=0, keepdims=True)
        spread.append(jnp.where(hot_slot, picked, 0.0))
    spread.append(jnp.zeros((32, pairs), F32))
    hot_d = (lax.broadcasted_iota(jnp.int32, (8, pairs), 0) == owner_d).astype(F32)
    return lax.dot_general(
        hot_d, jnp.concatenate(spread, axis=0), (((1,), (1,)), ((), ())), precision=HIGHEST,
        preferred_element_type=F32,
    )


def final_kernel(tiles, out):
    mine = lax.axis_index("strike") * 2
    summed = jnp.sum(tiles[...], axis=0, keepdims=True)
    lane = lax.broadcasted_iota(jnp.int32, (2, NZL), 1)
    place = lax.broadcasted_iota(jnp.int32, (2, NZL), 0)
    for c in range(3):
        hit = lane == 32 * c + mine + place
        out[:, pl.ds(c, 1)] = jnp.sum(jnp.where(hit, summed, 0.0), axis=1, keepdims=True)


def call(kernel, name, outs, scratch=(), flops=0, moved=0, in_specs=None):
    specs = {} if in_specs is None else {"in_specs": in_specs}
    return pl.pallas_call(
        kernel,
        out_shape=[jax.ShapeDtypeStruct(o, F32) if isinstance(o, tuple) else jax.typeof(o) for o in outs],
        scratch_shapes=[pltpu.VMEM(shape, F32) if isinstance(shape, tuple) else shape for shape in scratch],
        compiler_params=pltpu.CompilerParams(vmem_limit_bytes=16 * 2**20),
        cost_estimate=pl.CostEstimate(flops=flops, bytes_accessed=moved, transcendentals=0),
        name=name,
        **specs,
    )


def swap_near(value, axis):
    return lax.ppermute(value, axis, [(i, i ^ 1) for i in range(lax.axis_size(axis))])


def swap_far(value, axis):
    lower = range(1, lax.axis_size(axis) - 1, 2)
    return lax.ppermute(value, axis, [(i, i + 1) for i in lower] + [(i + 1, i) for i in lower])


def local(field_now, field_prev, rigidity, density, fault_nodes, patch_ids):
    axes = ("normal", "strike", "depth")
    counts = tuple(lax.axis_size(a) for a in axes)
    flat, block, tile = (3, ROWS, NZL), (ROWS, NZL), (8, NZL)
    now, prev = field_now.reshape(flat), field_prev.reshape(flat)
    rig, rho = rigidity.reshape(block), density.reshape(block)
    nodes, ids = fault_nodes.reshape(1, -1), patch_ids.reshape(1, -1)
    x_up, x_down, y_up, y_down = ((n, NZL) for n in (X_UP, X_DOWN, Y_UP, Y_DOWN))
    faces, strip = (48, NZL), (24, NZL)
    xa, xb, za, zb, zd_own = call(
        pack_kernel, "pack", [x_up, x_up, tile, tile, tile],
        [pltpu.VMEM(flat, F32), pltpu.VMEM(block, jnp.bfloat16), block, x_up, x_down, tile,
         pltpu.SemaphoreType.DMA((2,))],
        flops=2_000_000, moved=400_000, in_specs=[pl.BlockSpec(memory_space=pltpu.HBM)] * 2,
    )(now, rig)
    xa, xb = swap_near(xa, "normal"), swap_far(xb, "normal")
    zb, za = swap_far(zb, "depth"), swap_near(za, "depth")
    base, yb, ya, early, mx, mz, xd, zd, rw, scale, nodes, ids = call(
        functools.partial(half_kernel, counts), "half",
        [flat, y_up, y_up, faces, (16, NZL), tile, x_down, tile, block, block, nodes, ids],
        [flat, x_up, tile, y_up, y_down], flops=10_000_000, moved=900_000,
    )(now, prev, rig, rho, xa, xb, za, zb, zd_own, nodes, ids)
    yb, ya = swap_far(yb, "strike"), swap_near(ya, "strike")
    mid, kept, to_depth, xa2, xb2, zd2, my, y_low, y_high, r_high = call(
        functools.partial(whole_kernel, counts), "whole",
        [flat, flat, (8 * counts[0] * counts[2], NZL), faces, faces, tile, tile, strip, strip, tile],
        [faces, y_up, y_down, faces, faces, tile], flops=2_000_000, moved=900_000,
    )(base, now, rw, scale, early, yb, ya, mx, xd, zd, nodes, ids)
    got_z = lax.all_to_all(to_depth, ("normal", "depth"), 0, 0, tiled=True)
    (to_strike,) = call(
        functools.partial(sum_kernel, counts), "add", [(counts[1], NZL)], flops=10_000, moved=150_000,
    )(got_z)
    got_face = lax.all_to_all(to_strike, "strike", 0, 0, tiled=True)
    xa2, xb2 = swap_near(xa2, "normal"), swap_far(xb2, "normal")
    (share,) = call(final_kernel, "final", [(2, 3)], flops=10_000, moved=10_000)(got_face)
    (following,) = call(
        functools.partial(second_kernel, counts), "second", [flat], [flat, faces, faces, tile, tile],
        flops=10_000_000, moved=900_000,
    )(kept, now, rw, scale, xa2, xb2, got_z, zd2, mx, my, mz, xd, zd, y_low, y_high, r_high)
    return following.reshape(field_now.shape), mid.reshape(field_now.shape), share


def solution(mesh):
    field = P(None, "normal", "strike", "depth")
    cells = P("normal", "strike", "depth")
    pairs = P("strike", "depth", None)
    return jax.shard_map(
        local,
        mesh=mesh,
        in_specs=(field, field, cells, cells, pairs, pairs),
        out_specs=(field, field, P(("strike", "depth"), None)),
        check_vma=False,
    )
```

```python
import functools
import math

import jax
import jax.numpy as jnp
import numpy as np
from jax import lax
from jax.experimental import pallas as pl
from jax.experimental.pallas import tpu as pltpu
from jax.sharding import PartitionSpec as P

DT = 0.03
NXL, NYL, NZL = 8, 16, 128
ROWS = NXL * NYL
F32 = jnp.float32
HIGHEST = lax.Precision.HIGHEST


def gll_tables():
    spread = math.sqrt(3.0 / 7.0)
    points = np.array([-1.0, -spread, 0.0, spread, 1.0])
    weights = np.array([0.1, 49.0 / 90.0, 32.0 / 45.0, 49.0 / 90.0, 0.1]) * 0.5
    derivative = np.zeros((5, 5))
    for b in range(5):
        for a in range(5):
            if a == b:
                derivative[b, a] = sum(1.0 / (points[b] - points[o]) for o in range(5) if o != b)
            else:
                row = np.prod([points[b] - points[o] for o in range(5) if o != b and o != a])
                col = np.prod([points[a] - points[o] for o in range(5) if o != a and o != b])
                derivative[b, a] = row / (col * (points[a] - points[b]))
    return weights, 2.0 * derivative


WQ, D = gll_tables()
W0 = float(WQ[0])
NODE_W = np.array([2 * WQ[0], WQ[1], WQ[2], WQ[3], 2 * WQ[0]])
E = (WQ[:, None] * D).T / NODE_W[:, None]
KAPPA = float(E[4, 4])


def total(pairs):
    acc = None
    for const, arr in pairs:
        if abs(const) < 1e-12:
            continue
        term = arr * np.float32(const)
        acc = term if acc is None else acc + term
    return acc


def element(v, r):
    twice = v[2] + v[2]
    s0, s1 = v[0] + v[4] - twice, v[1] + v[3] - twice
    d0, d1 = v[0] - v[4], v[1] - v[3]
    ev = [total([((D[b, 0] + D[b, 4]) / 2, s0), ((D[b, 1] + D[b, 3]) / 2, s1)]) for b in (0, 1)]
    od = [total([((D[b, 0] - D[b, 4]) / 2, d0), ((D[b, 1] - D[b, 3]) / 2, d1)]) for b in (0, 1)]
    g2 = total([(D[2, 0], d0), (D[2, 1], d1)])
    q = [r[0] * (od[0] + ev[0]), r[1] * (od[1] + ev[1]), r[2] * g2, r[3] * (od[1] - ev[1]), r[4] * (od[0] - ev[0])]
    p0, m0, p1, m1 = q[0] + q[4], q[0] - q[4], q[1] + q[3], q[1] - q[3]
    ec = [total([((E[a, 0] + E[a, 4]) / 2, p0), ((E[a, 1] + E[a, 3]) / 2, p1), (E[a, 2], q[2])]) for a in (0, 1)]
    oc = [total([((E[a, 0] - E[a, 4]) / 2, m0), ((E[a, 1] - E[a, 3]) / 2, m1)]) for a in (0, 1)]
    c2 = total([(E[2, 0], m0), (E[2, 1], m1)])
    return [oc[0] + ec[0], oc[1] + ec[1], c2, oc[1] - ec[1], oc[0] - ec[0]]


def first_term(v, r):
    twice = v[2] + v[2]
    s0, s1 = v[0] + v[4] - twice, v[1] + v[3] - twice
    d0, d1 = v[0] - v[4], v[1] - v[3]
    ev = [total([((D[b, 0] + D[b, 4]) / 2, s0), ((D[b, 1] + D[b, 3]) / 2, s1)]) for b in (0, 1)]
    od = [total([((D[b, 0] - D[b, 4]) / 2, d0), ((D[b, 1] - D[b, 3]) / 2, d1)]) for b in (0, 1)]
    g2 = total([(D[2, 0], d0), (D[2, 1], d1)])
    q = [r[0] * (od[0] + ev[0]), r[1] * (od[1] + ev[1]), r[2] * g2, r[3] * (od[1] - ev[1]), r[4] * (od[0] - ev[0])]
    return total([(E[0, b], q[b]) for b in range(5)])


def open_terms(v, r):
    flux = [r[b] * total([(D[b, a], v[a]) for a in range(4)]) for b in range(4)]
    part = total([(E[4, b], flux[b]) for b in range(4)])
    grad = total([(D[4, a], v[a]) for a in range(4)])
    return part, grad


def open_scale(r):
    return total([(E[4, b] * D[b, 4], r[b]) for b in range(4)])


def rolled(x, shift):
    shift = shift % NZL
    return x if shift == 0 else pltpu.roll(x, shift, 1)


def lane_of():
    return lax.broadcasted_iota(jnp.int32, (8, NZL), 1)


def lane_table(phase, values):
    out = jnp.full((8, NZL), np.float32(values[0]), F32)
    for b in range(1, 4):
        out = jnp.where(phase == b, np.float32(values[b]), out)
    return out


def x_rows(x, half):
    return pl.ds(x * NYL + half * 8, 8)


def y_rows(y):
    return pl.ds(y, 8, stride=NYL)


def first_lanes(read, read_r, lane):
    out = jnp.zeros((8, NZL), F32)
    for k in range(16):
        rows = pl.ds(8 * k, 8)
        for c in range(3 if read_r is None else 4):
            src = read_r(rows) if c == 3 else read(c, rows)
            out = jnp.where(lane == 4 * k + c, rolled(src, 4 * k + c), out)
    return out


def last_lanes(read, lane):
    out = jnp.zeros((8, NZL), F32)
    for k in range(16):
        out = jnp.where((lane >> 2) == k, rolled(read(pl.ds(8 * k, 8)), 4 * k + 4), out)
    return out


def interleaved(parts, lane, base):
    out = jnp.zeros((8, NZL), F32)
    for j, part in enumerate(parts):
        if part is None:
            continue
        out = jnp.where((lane >= base) & (lane < base + 64) & ((lane & 3) == j), rolled(part, base + j - 3), out)
    return out


def widen(src, dst):
    for x in range(NXL):
        dst[pl.ds(x * NYL, NYL), :] = src[pl.ds(x * NYL, NYL), :].astype(F32)


X_UP, X_DOWN = 112, 64
Y_UP, Y_DOWN = 136, 64


def place():
    return tuple(lax.axis_index(axis) for axis in ("normal", "strike", "depth"))


def paired(index, up, down, near, far):
    even = (index & 1) == 0
    rows = pl.ds(0, down.shape[0])
    near[...] = up[...]
    far[...] = up[...]
    near[rows, :] = jnp.where(even, up[rows, :], down[...])
    far[rows, :] = jnp.where(even, down[...], up[rows, :])


def unpaired(index, near, far, low, high):
    even = (index & 1) == 0
    rows = pl.ds(0, high.shape[0])
    low[...] = jnp.where(even, far[...], near[...])
    high[...] = jnp.where(even, near[rows, :], far[rows, :])


def beside(index, count, got, low, high):
    below = pl.multiple_of((jnp.maximum(index - 1, 0)) * 8, 8)
    above = pl.multiple_of((jnp.minimum(index + 1, count - 1)) * 8, 8)
    low[...] = jnp.where(index > 0, got[pl.ds(below, low.shape[0]), :], 0.0)
    high[...] = jnp.where(index < count - 1, got[pl.ds(above, high.shape[0]), :], 0.0)


def pack_kernel(now_hbm, rig_hbm, xa, xb, za, zb, zd, tails, now, rig, rw, xu, xd, zu, sems):
    copies = [pltpu.make_async_copy(rig_hbm, rig, sems.at[0]), pltpu.make_async_copy(now_hbm, now, sems.at[1])]
    for copy in copies:
        copy.start()
    for copy in copies:
        copy.wait()
    widen(rig, rw)
    lane = lane_of()
    for half in range(2):
        r = [rw[x_rows(4 + a, half), :] for a in range(4)]
        xu[pl.ds(96 + 8 * half, 8), :] = open_scale(r)
        xd[pl.ds(48 + 8 * half, 8), :] = rw[x_rows(0, half), :]
        for c in range(3):
            part, grad = open_terms([now[c, x_rows(4 + a, half), :] for a in range(4)], r)
            xu[pl.ds(16 * c + 8 * half, 8), :] = part
            xu[pl.ds(48 + 16 * c + 8 * half, 8), :] = grad
            xd[pl.ds(16 * c + 8 * half, 8), :] = now[c, x_rows(0, half), :]
    back = lambda t: [rolled(t, 3 - a) for a in range(4)]
    tails[pl.ds(24, 8), :] = last_lanes(lambda rows: rw[rows, :], lane)
    r = back(tails[pl.ds(24, 8), :])
    parts, grads = [], []
    for c in range(3):
        tails[pl.ds(8 * c, 8), :] = last_lanes(lambda rows: now[c, rows, :], lane)
        part, grad = open_terms(back(tails[pl.ds(8 * c, 8), :]), r)
        parts.append(part)
        grads.append(grad)
    zu[...] = jnp.where(
        lane < 64, interleaved(parts + [open_scale(r)], lane, 0), interleaved(grads + [None], lane, 64)
    )
    zd[...] = first_lanes(lambda c, rows: now[c, rows, :], lambda rows: rw[rows, :], lane)
    index = place()
    paired(index[0], xu, xd, xa, xb)
    paired(index[2], zu, zd, za, zb)


def advance(now, prev, rw, low, high_v, high_r, scale, ghost_z, ghost_rz, closing_z, index, store, acc, on_first):
    index_x, index_y, index_z = index
    at_x = jnp.where(index_x == 0, 2.0, 1.0).astype(F32)
    at_y = jnp.where(index_y == 0, 2.0, 1.0).astype(F32)
    at_z = jnp.where(index_z == 0, 2.0, 1.0).astype(F32)

    def along_y(c, carry):
        none = jnp.zeros((8, NZL), F32)
        v = [now[c, y_rows(y), :] for y in range(NYL)] + [high_v[1][pl.ds(8 * c, 8), :] if high_v[1] is not None else none]
        r = [rw[y_rows(y), :] for y in range(NYL)] + [high_r[1][...] if high_r[1] is not None else none]
        carried = low[1](c, v[0]) if low[1] is not None else none
        for e in range(4):
            terms = element(v[4 * e : 4 * e + 5], r[4 * e : 4 * e + 5])
            head = terms[0] * at_y if e == 0 else terms[0]
            acc[c, y_rows(4 * e), :] = head + carried
            for a in range(1, 4):
                acc[c, y_rows(4 * e + a), :] = terms[a]
            carried = terms[4]
        return carry

    lax.fori_loop(0, 3, along_y, 0)
    alone = ghost_z is None

    lane = lane_of()
    phase = lane & 3
    gm = [lane_table(phase, [D[b, b - k] if b >= k else 0 for b in range(4)]) for k in range(4)]
    gp = [None] + [lane_table(phase, [D[b, b + k] if b + k <= 4 else 0 for b in range(4)]) for k in range(1, 5)]
    cm = [lane_table(phase, [E[a, a - k] if a >= k else 0 for a in range(4)]) for k in range(4)]
    cp = [None] + [lane_table(phase, [E[a, a + k] if a + k <= 3 else 0 for a in range(4)]) for k in range(1, 4)]
    c_close = lane_table(phase, [E[a, 4] for a in range(4)])
    last = [lane_table(phase, [0, 0, 0, E[4, b]]) for b in range(5)]
    first = lane == 0
    edge = jnp.where(first, at_z, jnp.float32(1.0))

    def along_xz(n, carry):
        c, half = n >> 1, n & 1
        offset = half * 8
        rows = [pl.ds(pl.multiple_of(x * NYL + offset, 8), 8) for x in range(NXL)]
        plane = pl.ds(pl.multiple_of(16 * c + offset, 8), 8)
        none = jnp.zeros((8, NZL), F32)
        v = [now[c, rows[x], :] for x in range(NXL)] + [none if alone else high_v[0][plane, :]]
        r = [rw[rows[x], :] for x in range(NXL)]
        r.append(none if alone else high_r[0][pl.ds(pl.multiple_of(offset, 8), 8), :])
        carried = none if alone else low[0](c, offset, plane, v[0])
        back = NZL - (4 * half + c)
        ghost_v = 0.0 if alone else pltpu.roll(ghost_z, back, 1)
        ghost_r = 0.0 if alone else pltpu.roll(ghost_rz, NZL - 4 * half, 1)
        closing = 0.0 if alone else pltpu.roll(closing_z, back, 1)
        for e in range(2):
            terms = element(v[4 * e : 4 * e + 5], r[4 * e : 4 * e + 5])
            if e == 0:
                on_first(c, plane, carried, terms[0])
            for a in range(4):
                x = 4 * e + a
                force = terms[a] + acc[c, rows[x], :]
                if a == 0:
                    force = (terms[0] * at_x if e == 0 else terms[0]) + carried + acc[c, rows[x], :]
                vx = jnp.where(first, ghost_v if alone else rolled(ghost_v, -8 * x), v[x])
                rx = jnp.where(first, ghost_r if alone else rolled(ghost_r, -8 * x), r[x])
                vm = [v[x]] + [rolled(v[x], k) for k in range(1, 4)]
                vp = [None] + [rolled(vx, -k) for k in range(1, 5)]
                g = gm[0] * v[x]
                for k in range(1, 4):
                    g = g + gm[k] * vm[k]
                for k in range(1, 5):
                    g = g + gp[k] * vp[k]
                g4 = total([(D[4, 0], vm[3]), (D[4, 1], vm[2]), (D[4, 2], vm[1]), (D[4, 3], vm[0]), (D[4, 4], vp[1])])
                q = r[x] * g
                q4 = jnp.where(phase == 3, rolled(rx, -1) * g4, 0.0)
                qm = [q] + [rolled(q, k) for k in range(1, 4)]
                own = cm[0] * q
                for k in range(1, 4):
                    own = own + cm[k] * qm[k]
                for k in range(1, 4):
                    own = own + cp[k] * rolled(q, -k)
                pair = q4 + rolled(q4, -1)
                own = own + c_close * (pair + rolled(pair, -2))
                tail = last[3] * q + last[4] * q4
                for b in range(3):
                    tail = tail + last[b] * qm[3 - b]
                tail = jnp.where(first, closing if alone else rolled(closing, -8 * x), rolled(tail, 1))
                force = force + own * edge + tail
                after = (v[x] + v[x]) - prev[c, rows[x], :] - scale[rows[x], :] * force
                store(c, x, rows[x], plane, after)
            carried = terms[4]
        return carry

    lax.fori_loop(0, 6, along_xz, 0)


def step_scale(rho, scale):
    for x in range(NXL):
        rows = pl.ds(x * NYL, NYL)
        scale[rows, :] = np.float32(DT * DT) / rho[rows, :].astype(F32)


def axis_weight(pos, is_first):
    phase = pos & 3
    out = jnp.full(pos.shape, np.float32(2 * W0), F32)
    for b in range(1, 4):
        out = jnp.where(phase == b, np.float32(WQ[b]), out)
    return jnp.where((pos == 0) & is_first, np.float32(W0), out)


def inner_kernel(now, prev, rig, rho, nodes_in, ids_in, base, term, rw, scale, nodes, ids, acc):
    nodes[...] = nodes_in[...]
    ids[...] = ids_in[...]
    widen(rig, rw)
    step_scale(rho, scale)

    def store(c, x, rows, plane, after):
        base[c, rows, :] = after

    def on_first(c, plane, carried, own):
        term[plane, :] = own

    nothing = (None, None)
    advance(now, prev, rw, nothing, nothing, nothing, scale, None, None, None, place(), store, acc, on_first)


def spread_from(tile, lane, source):
    phase = lane & 3
    out = tile
    for j in range(4):
        if j != source:
            out = jnp.where(phase == j, rolled(tile, j - source), out)
    return out


def edge_kernel(
    counts, inner, now, rw, scale, term, tails, xa, xb, za, zb, zd_own,
    base, yb, ya, early, mx, mz, xd, zd,
    xu, zu, yu, yd,
):
    index = place()
    unpaired(index[0], xa, xb, xu, xd)
    unpaired(index[2], za, zb, zu, zd)
    lane = lane_of()
    phase = lane & 3
    has_x, has_z = (index[0] > 0).astype(F32), (index[2] > 0).astype(F32)
    kappa, diagonal, d44 = np.float32(KAPPA), np.float32(KAPPA * D[4, 4]), np.float32(D[4, 4])

    own, above, below = zd_own[...], zu[...], zd[...]
    r_first = spread_from(own, lane, 3)
    gain = (spread_from(above, lane, 3) + diagonal * r_first) * has_z
    mz[...] = gain
    s_first = jnp.zeros((8, NZL), F32)
    for k in range(16):
        s_first = jnp.where(lane == 4 * k, rolled(scale[pl.ds(8 * k, 8), :], 4 * k), s_first)
    closing = spread_from(s_first, lane, 0) * (above + kappa * r_first * rolled(above, 64) + gain * own)
    r_tail = tails[pl.ds(24, 8), :]
    s_tail = last_lanes(lambda rows: scale[rows, :], lane)
    weights = [
        lane_table(phase, [E[a, a + k] * D[a + k, 4] if 0 <= a + k <= 3 else 0 for a in range(4)]) for k in range(-3, 4)
    ]
    by_value = s_tail * sum(w * rolled(r_tail, -k) for w, k in zip(weights, range(-3, 4)))
    by_flux = s_tail * lane_table(phase, [E[a, 4] for a in range(4)])
    r_below = spread_from(below, lane, 3)
    last = lane >= NZL - 4
    for c in range(3):
        tail = tails[pl.ds(8 * c, 8), :]
        grad = spread_from(total([(D[4, a], rolled(tail, 3 - a)) for a in range(4)]), lane, 3)
        value = spread_from(below, lane, c)
        taken = by_value * value + by_flux * (r_below * (grad + d44 * value))
        for k in range(16):
            rows = pl.ds(8 * k, 8)
            off = jnp.where(lane == 0, rolled(closing, -(4 * k + c)), 0.0)
            base[c, rows, :] = inner[c, rows, :] - jnp.where(last, rolled(taken, NZL - 4 - 4 * k), off)

    for half in range(2):
        rows = pl.ds(8 * half, 8)
        r = [rw[x_rows(4 + a, half), :] for a in range(4)]
        by_value, by_flux = open_response([scale[x_rows(4 + a, half), :] for a in range(4)], r)
        r0, r8 = rw[x_rows(0, half), :], xd[pl.ds(48 + 8 * half, 8), :]
        gain = (xu[pl.ds(96 + 8 * half, 8), :] + diagonal * r0) * has_x
        mx[rows, :] = gain
        for c in range(3):
            plane = pl.ds(16 * c + 8 * half, 8)
            grad = xu[pl.ds(48 + 16 * c + 8 * half, 8), :]
            carried = xu[plane, :] + kappa * r0 * grad + gain * now[c, x_rows(0, half), :]
            early[plane, :] = carried - term[plane, :]
            base[c, x_rows(0, half), :] = base[c, x_rows(0, half), :] - scale[x_rows(0, half), :] * carried
            value = xd[plane, :]
            flux = r8 * (total([(D[4, a], now[c, x_rows(4 + a, half), :]) for a in range(4)]) + d44 * value)
            for a in range(4):
                at = x_rows(4 + a, half)
                base[c, at, :] = base[c, at, :] - by_value[a] * value - by_flux[a] * flux

    r = [rw[y_rows(12 + a), :] for a in range(4)]
    by_value, by_flux = open_response([scale[y_rows(12 + a), :] for a in range(4)], r)
    planes = [open_scale(r), *open_terms(by_value, r), *open_terms(by_flux, r)]
    for n, plane in enumerate(planes):
        yu[pl.ds(96 + 8 * n, 8), :] = plane
    for c in range(3):
        planes = open_terms([now[c, y_rows(12 + a), :] for a in range(4)], r)
        planes += open_terms([base[c, y_rows(12 + a), :] for a in range(4)], r)
        for n, plane in enumerate(planes):
            yu[pl.ds(24 * n + 8 * c, 8), :] = plane
        yd[pl.ds(8 * c, 8), :] = now[c, y_rows(0), :]
        yd[pl.ds(24 + 8 * c, 8), :] = base[c, y_rows(0), :]
    yd[pl.ds(48, 8), :] = rw[y_rows(0), :]
    yd[pl.ds(56, 8), :] = scale[y_rows(0), :]
    paired(index[1], yu, yd, ya, yb)


def open_response(scale, r):
    by_value = [scale[a] * total([(E[a, b] * D[b, 4], r[b]) for b in range(4)]) for a in range(4)]
    by_flux = [scale[a] * np.float32(E[a, 4]) for a in range(4)]
    return by_value, by_flux


def whole_kernel(
    counts, base, now, rw, scale, early, yb, ya, mx, xd, zd, nodes, ids,
    out, kept, to_depth, xa2, xb2, zd2, my, y_low, y_high, r_high,
    slip, yu, yd, xu2, xd2, zu2,
):
    middle = counts[0] // 2
    index = place()
    lane = lane_of()
    kappa, diagonal = np.float32(KAPPA), np.float32(KAPPA * D[4, 4])
    d44 = np.float32(D[4, 4])
    unpaired(index[1], ya, yb, yu, yd)
    for c in range(3):
        for k in range(16):
            rows = pl.ds(8 * k, 8)
            values = base[c, rows, :]
            out[c, rows, :] = values
            kept[c, rows, :] = values
    r = [rw[y_rows(12 + a), :] for a in range(4)]
    by_value, by_flux = open_response([scale[y_rows(12 + a), :] for a in range(4)], r)
    own_scale = open_scale(r)
    r0, s0 = rw[y_rows(0), :], scale[y_rows(0), :]
    r_above, s_above = yd[pl.ds(48, 8), :], yd[pl.ds(56, 8), :]
    r_high[...] = r_above
    gain, value_part, value_grad, flux_part, flux_grad = (yu[pl.ds(96 + 8 * n, 8), :] for n in range(5))
    gain = (gain + diagonal * r0) * (index[1] > 0).astype(F32)
    my[...] = gain
    for c in range(3):
        plane = pl.ds(8 * c, 8)
        part, grad, part2, grad2 = (yu[pl.ds(24 * n + 8 * c, 8), :] for n in range(4))
        v0 = now[c, y_rows(0), :]
        after = base[c, y_rows(0), :] - s0 * (part + kappa * r0 * grad + gain * v0)
        out[c, y_rows(0), :] = after
        kept[c, y_rows(0), :] = after
        flux = r0 * (grad + d44 * v0)
        y_low[plane, :] = (part2 - value_part * v0 - flux_part * flux) + kappa * r0 * (
            grad2 - value_grad * v0 - flux_grad * flux
        )
        above = yd[plane, :]
        part, grad = open_terms([now[c, y_rows(12 + a), :] for a in range(4)], r)
        flux = r_above * (grad + d44 * above)
        y_high[plane, :] = yd[pl.ds(24 + 8 * c, 8), :] - s_above * (part + own_scale * above + kappa * flux)
        for a in range(4):
            after = base[c, y_rows(12 + a), :] - by_value[a] * above - by_flux[a] * flux
            out[c, y_rows(12 + a), :] = after
            kept[c, y_rows(12 + a), :] = after

    on_one, on_two = index[0] == middle - 1, index[0] == middle
    for half in range(2):
        rows = pl.ds(8 * half, 8)
        r = [rw[x_rows(x, half), :] for x in range(8)] + [xd[pl.ds(48 + 8 * half, 8), :]]
        y_pos = lax.broadcasted_iota(jnp.int32, (8, NZL), 0) + 8 * half
        face = axis_weight(y_pos, index[1] == 0) * axis_weight(lane, index[2] == 0) * np.float32(W0)
        for c in range(3):
            plane = pl.ds(16 * c + 8 * half, 8)
            v = [out[c, x_rows(x, half), :] for x in range(8)]
            part, grad = open_terms(v[4:], r[4:8])
            sent = part + kappa * r[8] * grad
            xu2[plane, :] = sent
            xd2[plane, :] = v[0]
            here = early[plane, :] + mx[rows, :] * v[0] - first_term(v[:5], r[:5])
            slip[plane, :] = face * jnp.where(on_one, sent, jnp.where(on_two, here, 0.0))
    back = lambda t: [rolled(t, 3 - a) for a in range(4)]
    r = back(last_lanes(lambda rows: rw[rows, :], lane))
    sent = []
    for c in range(3):
        part, grad = open_terms(back(last_lanes(lambda rows: out[c, rows, :], lane)), r)
        sent.append(part + kappa * zd[...] * grad)
    zu2[...] = interleaved(sent + [None], lane, 0)
    zd2[...] = first_lanes(lambda c, rows: out[c, rows, :], None, lane)
    paired(index[0], xu2, xd2, xa2, xb2)
    tile = patch_tile(counts[2], slip[...], nodes[...], ids[...])
    for d in range(counts[2]):
        halo = jnp.where(d > index[2], zu2[...], zd2[...])
        to_depth[pl.ds(8 * d, 8), :] = with_row(halo, tile[d : d + 1, :], lane)


def with_row(halo, row, lane):
    sub = lax.broadcasted_iota(jnp.int32, (8, NZL), 0)
    row = jnp.broadcast_to(row, (8, NZL))
    spread = jnp.where(sub == 0, rolled(row, 64), jnp.where(sub == 1, row, 0.0))
    return jnp.where(lane < 64, halo, spread)


def sum_kernel(counts, got, to_face):
    summed = got[pl.ds(0, 8), :]
    for d in range(1, counts[2]):
        summed = summed + got[pl.ds(8 * d, 8), :]
    low = jnp.broadcast_to(rolled(summed, 64)[0:1, :], (8, NZL))
    high = jnp.broadcast_to(summed[1:2, :], (8, NZL))
    row = jnp.where(lane_of() < 64, low, high)
    for k in range(counts[0] * counts[1] // 8):
        to_face[pl.ds(8 * k, 8), :] = row


def second_kernel(
    counts, now, prev, rw, scale, xa2, xb2, got_z, zd2_own, mx, my, mz, xd, zd, y_low, y_high, r_high,
    out, acc, xu2, xd2, zu2, zd2,
):
    index = place()
    unpaired(index[0], xa2, xb2, xu2, xd2)
    beside(index[2], counts[2], got_z, zu2, zd2)
    closing_z = zu2[...] + mz[...] * zd2_own[...]

    def low_x(c, offset, plane, v0):
        return xu2[plane, :] + mx[pl.ds(pl.multiple_of(offset, 8), 8), :] * v0

    def low_y(c, v0):
        return y_low[pl.ds(pl.multiple_of(8 * c, 8), 8), :] + my[...] * v0

    def store(c, x, rows, plane, after):
        out[c, rows, :] = after

    advance(
        now, prev, rw, (low_x, low_y), (xd2, y_high), (xd.at[pl.ds(48, 16)], r_high), scale,
        zd2[...], rolled(zd[...], -3), closing_z, index, store, acc, lambda *args: None,
    )


def patch_tile(count_d, slip, node, patch):
    pairs = node.shape[-1]
    hot_z = (lax.broadcasted_iota(jnp.int32, (NZL, pairs), 0) == (node & (NZL - 1))).astype(F32)
    at_z = jnp.dot(slip, hot_z, precision=HIGHEST, preferred_element_type=F32)
    row_y = lax.broadcasted_iota(jnp.int32, (NYL, pairs), 0) == (node >> 7)
    owner = patch >> 1
    owner_d = owner & (count_d - 1)
    slot = ((owner >> (count_d.bit_length() - 1)) << 1) + (patch & 1)
    hot_slot = lax.broadcasted_iota(jnp.int32, (32, pairs), 0) == slot
    spread = []
    for c in range(3):
        picked = jnp.sum(jnp.where(row_y, at_z[NYL * c : NYL * (c + 1), :], 0.0), axis=0, keepdims=True)
        spread.append(jnp.where(hot_slot, picked, 0.0))
    spread.append(jnp.zeros((32, pairs), F32))
    hot_d = (lax.broadcasted_iota(jnp.int32, (8, pairs), 0) == owner_d).astype(F32)
    return lax.dot_general(
        hot_d, jnp.concatenate(spread, axis=0), (((1,), (1,)), ((), ())), precision=HIGHEST,
        preferred_element_type=F32,
    )


def final_kernel(tiles, out):
    mine = lax.axis_index("strike") * 2
    summed = jnp.sum(tiles[...], axis=0, keepdims=True)
    lane = lax.broadcasted_iota(jnp.int32, (2, NZL), 1)
    place = lax.broadcasted_iota(jnp.int32, (2, NZL), 0)
    for c in range(3):
        hit = lane == 32 * c + mine + place
        out[:, pl.ds(c, 1)] = jnp.sum(jnp.where(hit, summed, 0.0), axis=1, keepdims=True)


def call(kernel, name, outs, scratch=(), flops=0, moved=0, in_specs=None):
    specs = {} if in_specs is None else {"in_specs": in_specs}
    return pl.pallas_call(
        kernel,
        out_shape=[jax.ShapeDtypeStruct(o, F32) if isinstance(o, tuple) else jax.typeof(o) for o in outs],
        scratch_shapes=[pltpu.VMEM(shape, F32) if isinstance(shape, tuple) else shape for shape in scratch],
        compiler_params=pltpu.CompilerParams(vmem_limit_bytes=16 * 2**20),
        cost_estimate=pl.CostEstimate(flops=flops, bytes_accessed=moved, transcendentals=0),
        name=name,
        **specs,
    )


def swap_near(value, axis):
    return lax.ppermute(value, axis, [(i, i ^ 1) for i in range(lax.axis_size(axis))])


def swap_far(value, axis):
    lower = range(1, lax.axis_size(axis) - 1, 2)
    return lax.ppermute(value, axis, [(i, i + 1) for i in lower] + [(i + 1, i) for i in lower])


def local(field_now, field_prev, rigidity, density, fault_nodes, patch_ids):
    axes = ("normal", "strike", "depth")
    counts = tuple(lax.axis_size(a) for a in axes)
    flat, block, tile = (3, ROWS, NZL), (ROWS, NZL), (8, NZL)
    now, prev = field_now.reshape(flat), field_prev.reshape(flat)
    rig, rho = rigidity.reshape(block), density.reshape(block)
    nodes, ids = fault_nodes.reshape(1, -1), patch_ids.reshape(1, -1)
    x_up, x_down, y_up, y_down = ((n, NZL) for n in (X_UP, X_DOWN, Y_UP, Y_DOWN))
    faces, strip = (48, NZL), (24, NZL)
    xa, xb, za, zb, zd_own, tails = call(
        pack_kernel, "pack", [x_up, x_up, tile, tile, tile, (32, NZL)],
        [pltpu.VMEM(flat, F32), pltpu.VMEM(block, jnp.bfloat16), block, x_up, x_down, tile,
         pltpu.SemaphoreType.DMA((2,))],
        flops=2_000_000, moved=400_000, in_specs=[pl.BlockSpec(memory_space=pltpu.HBM)] * 2,
    )(now, rig)
    xa, xb = swap_near(xa, "normal"), swap_far(xb, "normal")
    zb, za = swap_far(zb, "depth"), swap_near(za, "depth")
    inner, term, rw, scale, nodes, ids = call(
        inner_kernel, "inner", [flat, faces, block, block, nodes, ids], [flat], flops=10_000_000, moved=900_000,
    )(now, prev, rig, rho, nodes, ids)
    base, yb, ya, early, mx, mz, xd, zd = call(
        functools.partial(edge_kernel, counts), "edge",
        [flat, y_up, y_up, faces, (16, NZL), tile, x_down, tile],
        [x_up, tile, y_up, y_down], flops=2_000_000, moved=900_000,
    )(inner, now, rw, scale, term, tails, xa, xb, za, zb, zd_own)
    yb, ya = swap_far(yb, "strike"), swap_near(ya, "strike")
    mid, kept, to_depth, xa2, xb2, zd2, my, y_low, y_high, r_high = call(
        functools.partial(whole_kernel, counts), "whole",
        [flat, flat, (8 * counts[2], NZL), faces, faces, tile, tile, strip, strip, tile],
        [faces, y_up, y_down, faces, faces, tile], flops=2_000_000, moved=900_000,
    )(base, now, rw, scale, early, yb, ya, mx, xd, zd, nodes, ids)
    got_z = lax.all_to_all(to_depth, "depth", 0, 0, tiled=True)
    (to_face,) = call(
        functools.partial(sum_kernel, counts), "add", [(counts[0] * counts[1], NZL)], flops=10_000, moved=80_000,
    )(got_z)
    got_face = lax.all_to_all(to_face, ("normal", "strike"), 0, 0, tiled=True)
    xa2, xb2 = swap_near(xa2, "normal"), swap_far(xb2, "normal")
    (share,) = call(final_kernel, "final", [(2, 3)], flops=10_000, moved=10_000)(got_face)
    (following,) = call(
        functools.partial(second_kernel, counts), "second", [flat], [flat, faces, faces, tile, tile],
        flops=10_000_000, moved=900_000,
    )(kept, now, rw, scale, xa2, xb2, got_z, zd2, mx, my, mz, xd, zd, y_low, y_high, r_high)
    return following.reshape(field_now.shape), mid.reshape(field_now.shape), share


def solution(mesh):
    field = P(None, "normal", "strike", "depth")
    cells = P("normal", "strike", "depth")
    pairs = P("strike", "depth", None)
    return jax.shard_map(
        local,
        mesh=mesh,
        in_specs=(field, field, cells, cells, pairs, pairs),
        out_specs=(field, field, P(("strike", "depth"), None)),
        check_vma=False,
    )
```

```python
import functools
import math

import jax
import jax.numpy as jnp
import numpy as np
from jax import lax
from jax.experimental import pallas as pl
from jax.experimental.pallas import tpu as pltpu
from jax.sharding import PartitionSpec as P

DT = 0.03
NXL, NYL, NZL = 8, 16, 128
ROWS = NXL * NYL
F32 = jnp.float32
HIGHEST = lax.Precision.HIGHEST


def gll_tables():
    spread = math.sqrt(3.0 / 7.0)
    points = np.array([-1.0, -spread, 0.0, spread, 1.0])
    weights = np.array([0.1, 49.0 / 90.0, 32.0 / 45.0, 49.0 / 90.0, 0.1]) * 0.5
    derivative = np.zeros((5, 5))
    for b in range(5):
        for a in range(5):
            if a == b:
                derivative[b, a] = sum(1.0 / (points[b] - points[o]) for o in range(5) if o != b)
            else:
                row = np.prod([points[b] - points[o] for o in range(5) if o != b and o != a])
                col = np.prod([points[a] - points[o] for o in range(5) if o != a and o != b])
                derivative[b, a] = row / (col * (points[a] - points[b]))
    return weights, 2.0 * derivative


WQ, D = gll_tables()
W0 = float(WQ[0])
NODE_W = np.array([2 * WQ[0], WQ[1], WQ[2], WQ[3], 2 * WQ[0]])
E = (WQ[:, None] * D).T / NODE_W[:, None]
KAPPA = float(E[4, 4])


def total(pairs):
    acc = None
    for const, arr in pairs:
        if abs(const) < 1e-12:
            continue
        term = arr * np.float32(const)
        acc = term if acc is None else acc + term
    return acc


def element(v, r):
    twice = v[2] + v[2]
    s0, s1 = v[0] + v[4] - twice, v[1] + v[3] - twice
    d0, d1 = v[0] - v[4], v[1] - v[3]
    ev = [total([((D[b, 0] + D[b, 4]) / 2, s0), ((D[b, 1] + D[b, 3]) / 2, s1)]) for b in (0, 1)]
    od = [total([((D[b, 0] - D[b, 4]) / 2, d0), ((D[b, 1] - D[b, 3]) / 2, d1)]) for b in (0, 1)]
    g2 = total([(D[2, 0], d0), (D[2, 1], d1)])
    q = [r[0] * (od[0] + ev[0]), r[1] * (od[1] + ev[1]), r[2] * g2, r[3] * (od[1] - ev[1]), r[4] * (od[0] - ev[0])]
    p0, m0, p1, m1 = q[0] + q[4], q[0] - q[4], q[1] + q[3], q[1] - q[3]
    ec = [total([((E[a, 0] + E[a, 4]) / 2, p0), ((E[a, 1] + E[a, 3]) / 2, p1), (E[a, 2], q[2])]) for a in (0, 1)]
    oc = [total([((E[a, 0] - E[a, 4]) / 2, m0), ((E[a, 1] - E[a, 3]) / 2, m1)]) for a in (0, 1)]
    c2 = total([(E[2, 0], m0), (E[2, 1], m1)])
    return [oc[0] + ec[0], oc[1] + ec[1], c2, oc[1] - ec[1], oc[0] - ec[0]]


def first_term(v, r):
    twice = v[2] + v[2]
    s0, s1 = v[0] + v[4] - twice, v[1] + v[3] - twice
    d0, d1 = v[0] - v[4], v[1] - v[3]
    ev = [total([((D[b, 0] + D[b, 4]) / 2, s0), ((D[b, 1] + D[b, 3]) / 2, s1)]) for b in (0, 1)]
    od = [total([((D[b, 0] - D[b, 4]) / 2, d0), ((D[b, 1] - D[b, 3]) / 2, d1)]) for b in (0, 1)]
    g2 = total([(D[2, 0], d0), (D[2, 1], d1)])
    q = [r[0] * (od[0] + ev[0]), r[1] * (od[1] + ev[1]), r[2] * g2, r[3] * (od[1] - ev[1]), r[4] * (od[0] - ev[0])]
    return total([(E[0, b], q[b]) for b in range(5)])


def open_terms(v, r):
    flux = [r[b] * total([(D[b, a], v[a]) for a in range(4)]) for b in range(4)]
    part = total([(E[4, b], flux[b]) for b in range(4)])
    grad = total([(D[4, a], v[a]) for a in range(4)])
    return part, grad


def open_scale(r):
    return total([(E[4, b] * D[b, 4], r[b]) for b in range(4)])


def rolled(x, shift):
    shift = shift % NZL
    return x if shift == 0 else pltpu.roll(x, shift, 1)


def lane_of():
    return lax.broadcasted_iota(jnp.int32, (8, NZL), 1)


def lane_table(phase, values):
    out = jnp.full((8, NZL), np.float32(values[0]), F32)
    for b in range(1, 4):
        out = jnp.where(phase == b, np.float32(values[b]), out)
    return out


def x_rows(x, half):
    return pl.ds(x * NYL + half * 8, 8)


def y_rows(y):
    return pl.ds(y, 8, stride=NYL)


def first_lanes(read, read_r, lane):
    out = jnp.zeros((8, NZL), F32)
    for k in range(16):
        rows = pl.ds(8 * k, 8)
        for c in range(3 if read_r is None else 4):
            src = read_r(rows) if c == 3 else read(c, rows)
            out = jnp.where(lane == 4 * k + c, rolled(src, 4 * k + c), out)
    return out


def last_lanes(read, lane):
    out = jnp.zeros((8, NZL), F32)
    for k in range(16):
        out = jnp.where((lane >> 2) == k, rolled(read(pl.ds(8 * k, 8)), 4 * k + 4), out)
    return out


def interleaved(parts, lane, base):
    out = jnp.zeros((8, NZL), F32)
    for j, part in enumerate(parts):
        if part is None:
            continue
        out = jnp.where((lane >= base) & (lane < base + 64) & ((lane & 3) == j), rolled(part, base + j - 3), out)
    return out


def widen(src, dst):
    for x in range(NXL):
        dst[pl.ds(x * NYL, NYL), :] = src[pl.ds(x * NYL, NYL), :].astype(F32)


X_UP, X_DOWN = 112, 64
Y_UP, Y_DOWN = 136, 64


def place():
    return tuple(lax.axis_index(axis) for axis in ("normal", "strike", "depth"))


def paired(index, up, down, near, far):
    even = (index & 1) == 0
    rows = pl.ds(0, down.shape[0])
    near[...] = up[...]
    far[...] = up[...]
    near[rows, :] = jnp.where(even, up[rows, :], down[...])
    far[rows, :] = jnp.where(even, down[...], up[rows, :])


def unpaired(index, near, far, low, high):
    even = (index & 1) == 0
    rows = pl.ds(0, high.shape[0])
    low[...] = jnp.where(even, far[...], near[...])
    high[...] = jnp.where(even, near[rows, :], far[rows, :])


def beside(index, count, got, low, high):
    below = pl.multiple_of((jnp.maximum(index - 1, 0)) * 8, 8)
    above = pl.multiple_of((jnp.minimum(index + 1, count - 1)) * 8, 8)
    low[...] = jnp.where(index > 0, got[pl.ds(below, low.shape[0]), :], 0.0)
    high[...] = jnp.where(index < count - 1, got[pl.ds(above, high.shape[0]), :], 0.0)


def pack_kernel(
    now_hbm, prev_hbm, rig_hbm, rho_hbm, nodes_hbm, ids_hbm,
    xa, xb, za, zb, zd, tails, rw, now, prev, rho, nodes, ids,
    rig, xu, xd, zu, sems,
):
    pairs = (
        (rig_hbm, rig), (now_hbm, now), (prev_hbm, prev), (rho_hbm, rho), (nodes_hbm, nodes), (ids_hbm, ids),
    )
    copies = [pltpu.make_async_copy(src, dst, sems.at[i]) for i, (src, dst) in enumerate(pairs)]
    for copy in copies:
        copy.start()
    for copy in copies[:2]:
        copy.wait()
    widen(rig, rw)
    lane = lane_of()
    for half in range(2):
        r = [rw[x_rows(4 + a, half), :] for a in range(4)]
        xu[pl.ds(96 + 8 * half, 8), :] = open_scale(r)
        xd[pl.ds(48 + 8 * half, 8), :] = rw[x_rows(0, half), :]
        for c in range(3):
            part, grad = open_terms([now[c, x_rows(4 + a, half), :] for a in range(4)], r)
            xu[pl.ds(16 * c + 8 * half, 8), :] = part
            xu[pl.ds(48 + 16 * c + 8 * half, 8), :] = grad
            xd[pl.ds(16 * c + 8 * half, 8), :] = now[c, x_rows(0, half), :]
    back = lambda t: [rolled(t, 3 - a) for a in range(4)]
    tails[pl.ds(24, 8), :] = last_lanes(lambda rows: rw[rows, :], lane)
    r = back(tails[pl.ds(24, 8), :])
    parts, grads = [], []
    for c in range(3):
        tails[pl.ds(8 * c, 8), :] = last_lanes(lambda rows: now[c, rows, :], lane)
        part, grad = open_terms(back(tails[pl.ds(8 * c, 8), :]), r)
        parts.append(part)
        grads.append(grad)
    zu[...] = jnp.where(
        lane < 64, interleaved(parts + [open_scale(r)], lane, 0), interleaved(grads + [None], lane, 64)
    )
    zd[...] = first_lanes(lambda c, rows: now[c, rows, :], lambda rows: rw[rows, :], lane)
    index = place()
    paired(index[0], xu, xd, xa, xb)
    paired(index[2], zu, zd, za, zb)
    for copy in copies[2:]:
        copy.wait()


def advance(now, prev, rw, low, high_v, high_r, scale, ghost_z, ghost_rz, closing_z, index, store, acc, on_first):
    index_x, index_y, index_z = index
    at_x = jnp.where(index_x == 0, 2.0, 1.0).astype(F32)
    at_y = jnp.where(index_y == 0, 2.0, 1.0).astype(F32)
    at_z = jnp.where(index_z == 0, 2.0, 1.0).astype(F32)

    def along_y(c, carry):
        none = jnp.zeros((8, NZL), F32)
        v = [now[c, y_rows(y), :] for y in range(NYL)] + [high_v[1][pl.ds(8 * c, 8), :] if high_v[1] is not None else none]
        r = [rw[y_rows(y), :] for y in range(NYL)] + [high_r[1][...] if high_r[1] is not None else none]
        carried = low[1](c, v[0]) if low[1] is not None else none
        for e in range(4):
            terms = element(v[4 * e : 4 * e + 5], r[4 * e : 4 * e + 5])
            head = terms[0] * at_y if e == 0 else terms[0]
            acc[c, y_rows(4 * e), :] = head + carried
            for a in range(1, 4):
                acc[c, y_rows(4 * e + a), :] = terms[a]
            carried = terms[4]
        return carry

    lax.fori_loop(0, 3, along_y, 0)
    alone = ghost_z is None

    lane = lane_of()
    phase = lane & 3
    gm = [lane_table(phase, [D[b, b - k] if b >= k else 0 for b in range(4)]) for k in range(4)]
    gp = [None] + [lane_table(phase, [D[b, b + k] if b + k <= 4 else 0 for b in range(4)]) for k in range(1, 5)]
    cm = [lane_table(phase, [E[a, a - k] if a >= k else 0 for a in range(4)]) for k in range(4)]
    cp = [None] + [lane_table(phase, [E[a, a + k] if a + k <= 3 else 0 for a in range(4)]) for k in range(1, 4)]
    c_close = lane_table(phase, [E[a, 4] for a in range(4)])
    last = [lane_table(phase, [0, 0, 0, E[4, b]]) for b in range(5)]
    first = lane == 0
    edge = jnp.where(first, at_z, jnp.float32(1.0))

    def along_xz(n, carry):
        c, half = n >> 1, n & 1
        offset = half * 8
        rows = [pl.ds(pl.multiple_of(x * NYL + offset, 8), 8) for x in range(NXL)]
        plane = pl.ds(pl.multiple_of(16 * c + offset, 8), 8)
        none = jnp.zeros((8, NZL), F32)
        v = [now[c, rows[x], :] for x in range(NXL)] + [none if alone else high_v[0][plane, :]]
        r = [rw[rows[x], :] for x in range(NXL)]
        r.append(none if alone else high_r[0][pl.ds(pl.multiple_of(offset, 8), 8), :])
        carried = none if alone else low[0](c, offset, plane, v[0])
        back = NZL - (4 * half + c)
        ghost_v = 0.0 if alone else pltpu.roll(ghost_z, back, 1)
        ghost_r = 0.0 if alone else pltpu.roll(ghost_rz, NZL - 4 * half, 1)
        closing = 0.0 if alone else pltpu.roll(closing_z, back, 1)
        for e in range(2):
            terms = element(v[4 * e : 4 * e + 5], r[4 * e : 4 * e + 5])
            if e == 0:
                on_first(c, plane, carried, terms[0])
            for a in range(4):
                x = 4 * e + a
                force = terms[a] + acc[c, rows[x], :]
                if a == 0:
                    force = (terms[0] * at_x if e == 0 else terms[0]) + carried + acc[c, rows[x], :]
                vx = jnp.where(first, ghost_v if alone else rolled(ghost_v, -8 * x), v[x])
                rx = jnp.where(first, ghost_r if alone else rolled(ghost_r, -8 * x), r[x])
                vm = [v[x]] + [rolled(v[x], k) for k in range(1, 4)]
                vp = [None] + [rolled(vx, -k) for k in range(1, 5)]
                g = gm[0] * v[x]
                for k in range(1, 4):
                    g = g + gm[k] * vm[k]
                for k in range(1, 5):
                    g = g + gp[k] * vp[k]
                g4 = total([(D[4, 0], vm[3]), (D[4, 1], vm[2]), (D[4, 2], vm[1]), (D[4, 3], vm[0]), (D[4, 4], vp[1])])
                q = r[x] * g
                q4 = jnp.where(phase == 3, rolled(rx, -1) * g4, 0.0)
                qm = [q] + [rolled(q, k) for k in range(1, 4)]
                own = cm[0] * q
                for k in range(1, 4):
                    own = own + cm[k] * qm[k]
                for k in range(1, 4):
                    own = own + cp[k] * rolled(q, -k)
                pair = q4 + rolled(q4, -1)
                own = own + c_close * (pair + rolled(pair, -2))
                tail = last[3] * q + last[4] * q4
                for b in range(3):
                    tail = tail + last[b] * qm[3 - b]
                tail = jnp.where(first, closing if alone else rolled(closing, -8 * x), rolled(tail, 1))
                force = force + own * edge + tail
                after = (v[x] + v[x]) - prev[c, rows[x], :] - scale[rows[x], :] * force
                store(c, x, rows[x], plane, after)
            carried = terms[4]
        return carry

    lax.fori_loop(0, 6, along_xz, 0)


def step_scale(rho, scale):
    for x in range(NXL):
        rows = pl.ds(x * NYL, NYL)
        scale[rows, :] = np.float32(DT * DT) / rho[rows, :].astype(F32)


def axis_weight(pos, is_first):
    phase = pos & 3
    out = jnp.full(pos.shape, np.float32(2 * W0), F32)
    for b in range(1, 4):
        out = jnp.where(phase == b, np.float32(WQ[b]), out)
    return jnp.where((pos == 0) & is_first, np.float32(W0), out)


def inner_kernel(now, prev, rw, rho, base, term, scale, acc):
    step_scale(rho, scale)

    def store(c, x, rows, plane, after):
        base[c, rows, :] = after

    def on_first(c, plane, carried, own):
        term[plane, :] = own

    nothing = (None, None)
    advance(now, prev, rw, nothing, nothing, nothing, scale, None, None, None, place(), store, acc, on_first)


def spread_from(tile, lane, source):
    phase = lane & 3
    out = tile
    for j in range(4):
        if j != source:
            out = jnp.where(phase == j, rolled(tile, j - source), out)
    return out


def edge_kernel(
    counts, inner, now, rw, scale, term, tails, xa, xb, za, zb, zd_own,
    base, yb, ya, early, mx, mz, xd, zd,
    xu, zu, yu, yd,
):
    index = place()
    unpaired(index[0], xa, xb, xu, xd)
    unpaired(index[2], za, zb, zu, zd)
    lane = lane_of()
    phase = lane & 3
    has_x, has_z = (index[0] > 0).astype(F32), (index[2] > 0).astype(F32)
    kappa, diagonal, d44 = np.float32(KAPPA), np.float32(KAPPA * D[4, 4]), np.float32(D[4, 4])

    own, above, below = zd_own[...], zu[...], zd[...]
    r_first = spread_from(own, lane, 3)
    gain = (spread_from(above, lane, 3) + diagonal * r_first) * has_z
    mz[...] = gain
    s_first = jnp.zeros((8, NZL), F32)
    for k in range(16):
        s_first = jnp.where(lane == 4 * k, rolled(scale[pl.ds(8 * k, 8), :], 4 * k), s_first)
    closing = spread_from(s_first, lane, 0) * (above + kappa * r_first * rolled(above, 64) + gain * own)
    r_tail = tails[pl.ds(24, 8), :]
    s_tail = last_lanes(lambda rows: scale[rows, :], lane)
    weights = [
        lane_table(phase, [E[a, a + k] * D[a + k, 4] if 0 <= a + k <= 3 else 0 for a in range(4)]) for k in range(-3, 4)
    ]
    by_value = s_tail * sum(w * rolled(r_tail, -k) for w, k in zip(weights, range(-3, 4)))
    by_flux = s_tail * lane_table(phase, [E[a, 4] for a in range(4)])
    r_below = spread_from(below, lane, 3)
    last = lane >= NZL - 4
    for c in range(3):
        tail = tails[pl.ds(8 * c, 8), :]
        grad = spread_from(total([(D[4, a], rolled(tail, 3 - a)) for a in range(4)]), lane, 3)
        value = spread_from(below, lane, c)
        taken = by_value * value + by_flux * (r_below * (grad + d44 * value))
        for k in range(16):
            rows = pl.ds(8 * k, 8)
            off = jnp.where(lane == 0, rolled(closing, -(4 * k + c)), 0.0)
            base[c, rows, :] = inner[c, rows, :] - jnp.where(last, rolled(taken, NZL - 4 - 4 * k), off)

    for half in range(2):
        rows = pl.ds(8 * half, 8)
        r = [rw[x_rows(4 + a, half), :] for a in range(4)]
        by_value, by_flux = open_response([scale[x_rows(4 + a, half), :] for a in range(4)], r)
        r0, r8 = rw[x_rows(0, half), :], xd[pl.ds(48 + 8 * half, 8), :]
        gain = (xu[pl.ds(96 + 8 * half, 8), :] + diagonal * r0) * has_x
        mx[rows, :] = gain
        for c in range(3):
            plane = pl.ds(16 * c + 8 * half, 8)
            grad = xu[pl.ds(48 + 16 * c + 8 * half, 8), :]
            carried = xu[plane, :] + kappa * r0 * grad + gain * now[c, x_rows(0, half), :]
            early[plane, :] = carried - term[plane, :]
            base[c, x_rows(0, half), :] = base[c, x_rows(0, half), :] - scale[x_rows(0, half), :] * carried
            value = xd[plane, :]
            flux = r8 * (total([(D[4, a], now[c, x_rows(4 + a, half), :]) for a in range(4)]) + d44 * value)
            for a in range(4):
                at = x_rows(4 + a, half)
                base[c, at, :] = base[c, at, :] - by_value[a] * value - by_flux[a] * flux

    r = [rw[y_rows(12 + a), :] for a in range(4)]
    by_value, by_flux = open_response([scale[y_rows(12 + a), :] for a in range(4)], r)
    planes = [open_scale(r), *open_terms(by_value, r), *open_terms(by_flux, r)]
    for n, plane in enumerate(planes):
        yu[pl.ds(96 + 8 * n, 8), :] = plane
    for c in range(3):
        planes = open_terms([now[c, y_rows(12 + a), :] for a in range(4)], r)
        planes += open_terms([base[c, y_rows(12 + a), :] for a in range(4)], r)
        for n, plane in enumerate(planes):
            yu[pl.ds(24 * n + 8 * c, 8), :] = plane
        yd[pl.ds(8 * c, 8), :] = now[c, y_rows(0), :]
        yd[pl.ds(24 + 8 * c, 8), :] = base[c, y_rows(0), :]
    yd[pl.ds(48, 8), :] = rw[y_rows(0), :]
    yd[pl.ds(56, 8), :] = scale[y_rows(0), :]
    paired(index[1], yu, yd, ya, yb)


def open_response(scale, r):
    by_value = [scale[a] * total([(E[a, b] * D[b, 4], r[b]) for b in range(4)]) for a in range(4)]
    by_flux = [scale[a] * np.float32(E[a, 4]) for a in range(4)]
    return by_value, by_flux


def whole_kernel(
    counts, base, now, rw, scale, early, yb, ya, mx, xd, zd, nodes, ids,
    out, kept, to_depth, xa2, xb2, zd2, my, y_low, y_high, r_high,
    slip, yu, yd, xu2, xd2, zu2,
):
    middle = counts[0] // 2
    index = place()
    lane = lane_of()
    kappa, diagonal = np.float32(KAPPA), np.float32(KAPPA * D[4, 4])
    d44 = np.float32(D[4, 4])
    unpaired(index[1], ya, yb, yu, yd)
    for c in range(3):
        for k in range(16):
            rows = pl.ds(8 * k, 8)
            values = base[c, rows, :]
            out[c, rows, :] = values
            kept[c, rows, :] = values
    r = [rw[y_rows(12 + a), :] for a in range(4)]
    by_value, by_flux = open_response([scale[y_rows(12 + a), :] for a in range(4)], r)
    own_scale = open_scale(r)
    r0, s0 = rw[y_rows(0), :], scale[y_rows(0), :]
    r_above, s_above = yd[pl.ds(48, 8), :], yd[pl.ds(56, 8), :]
    r_high[...] = r_above
    gain, value_part, value_grad, flux_part, flux_grad = (yu[pl.ds(96 + 8 * n, 8), :] for n in range(5))
    gain = (gain + diagonal * r0) * (index[1] > 0).astype(F32)
    my[...] = gain
    for c in range(3):
        plane = pl.ds(8 * c, 8)
        part, grad, part2, grad2 = (yu[pl.ds(24 * n + 8 * c, 8), :] for n in range(4))
        v0 = now[c, y_rows(0), :]
        after = base[c, y_rows(0), :] - s0 * (part + kappa * r0 * grad + gain * v0)
        out[c, y_rows(0), :] = after
        kept[c, y_rows(0), :] = after
        flux = r0 * (grad + d44 * v0)
        y_low[plane, :] = (part2 - value_part * v0 - flux_part * flux) + kappa * r0 * (
            grad2 - value_grad * v0 - flux_grad * flux
        )
        above = yd[plane, :]
        part, grad = open_terms([now[c, y_rows(12 + a), :] for a in range(4)], r)
        flux = r_above * (grad + d44 * above)
        y_high[plane, :] = yd[pl.ds(24 + 8 * c, 8), :] - s_above * (part + own_scale * above + kappa * flux)
        for a in range(4):
            after = base[c, y_rows(12 + a), :] - by_value[a] * above - by_flux[a] * flux
            out[c, y_rows(12 + a), :] = after
            kept[c, y_rows(12 + a), :] = after

    on_one, on_two = index[0] == middle - 1, index[0] == middle
    for half in range(2):
        rows = pl.ds(8 * half, 8)
        r = [rw[x_rows(x, half), :] for x in range(8)] + [xd[pl.ds(48 + 8 * half, 8), :]]
        y_pos = lax.broadcasted_iota(jnp.int32, (8, NZL), 0) + 8 * half
        face = axis_weight(y_pos, index[1] == 0) * axis_weight(lane, index[2] == 0) * np.float32(W0)
        for c in range(3):
            plane = pl.ds(16 * c + 8 * half, 8)
            v = [out[c, x_rows(x, half), :] for x in range(8)]
            part, grad = open_terms(v[4:], r[4:8])
            sent = part + kappa * r[8] * grad
            xu2[plane, :] = sent
            xd2[plane, :] = v[0]
            here = early[plane, :] + mx[rows, :] * v[0] - first_term(v[:5], r[:5])
            slip[plane, :] = face * jnp.where(on_one, sent, jnp.where(on_two, here, 0.0))
    back = lambda t: [rolled(t, 3 - a) for a in range(4)]
    r = back(last_lanes(lambda rows: rw[rows, :], lane))
    sent = []
    for c in range(3):
        part, grad = open_terms(back(last_lanes(lambda rows: out[c, rows, :], lane)), r)
        sent.append(part + kappa * zd[...] * grad)
    zu2[...] = interleaved(sent + [None], lane, 0)
    zd2[...] = first_lanes(lambda c, rows: out[c, rows, :], None, lane)
    paired(index[0], xu2, xd2, xa2, xb2)
    tile = patch_tile(counts[2], slip[...], nodes[...], ids[...])
    for d in range(counts[2]):
        halo = jnp.where(d > index[2], zu2[...], zd2[...])
        to_depth[pl.ds(8 * d, 8), :] = with_row(halo, tile[d : d + 1, :], lane)


def with_row(halo, row, lane):
    sub = lax.broadcasted_iota(jnp.int32, (8, NZL), 0)
    row = jnp.broadcast_to(row, (8, NZL))
    spread = jnp.where(sub == 0, rolled(row, 64), jnp.where(sub == 1, row, 0.0))
    return jnp.where(lane < 64, halo, spread)


def sum_kernel(counts, got, to_face):
    summed = got[pl.ds(0, 8), :]
    for d in range(1, counts[2]):
        summed = summed + got[pl.ds(8 * d, 8), :]
    low = jnp.broadcast_to(rolled(summed, 64)[0:1, :], (8, NZL))
    high = jnp.broadcast_to(summed[1:2, :], (8, NZL))
    row = jnp.where(lane_of() < 64, low, high)
    for k in range(counts[0] * counts[1] // 8):
        to_face[pl.ds(8 * k, 8), :] = row


def second_kernel(
    counts, now, prev, rw, scale, xa2, xb2, got_z, zd2_own, mx, my, mz, xd, zd, y_low, y_high, r_high,
    out, acc, xu2, xd2, zu2, zd2,
):
    index = place()
    unpaired(index[0], xa2, xb2, xu2, xd2)
    beside(index[2], counts[2], got_z, zu2, zd2)
    closing_z = zu2[...] + mz[...] * zd2_own[...]

    def low_x(c, offset, plane, v0):
        return xu2[plane, :] + mx[pl.ds(pl.multiple_of(offset, 8), 8), :] * v0

    def low_y(c, v0):
        return y_low[pl.ds(pl.multiple_of(8 * c, 8), 8), :] + my[...] * v0

    def store(c, x, rows, plane, after):
        out[c, rows, :] = after

    advance(
        now, prev, rw, (low_x, low_y), (xd2, y_high), (xd.at[pl.ds(48, 16)], r_high), scale,
        zd2[...], rolled(zd[...], -3), closing_z, index, store, acc, lambda *args: None,
    )


def patch_tile(count_d, slip, node, patch):
    pairs = node.shape[-1]
    hot_z = (lax.broadcasted_iota(jnp.int32, (NZL, pairs), 0) == (node & (NZL - 1))).astype(F32)
    at_z = jnp.dot(slip, hot_z, precision=HIGHEST, preferred_element_type=F32)
    row_y = lax.broadcasted_iota(jnp.int32, (NYL, pairs), 0) == (node >> 7)
    owner = patch >> 1
    owner_d = owner & (count_d - 1)
    slot = ((owner >> (count_d.bit_length() - 1)) << 1) + (patch & 1)
    hot_slot = lax.broadcasted_iota(jnp.int32, (32, pairs), 0) == slot
    spread = []
    for c in range(3):
        picked = jnp.sum(jnp.where(row_y, at_z[NYL * c : NYL * (c + 1), :], 0.0), axis=0, keepdims=True)
        spread.append(jnp.where(hot_slot, picked, 0.0))
    spread.append(jnp.zeros((32, pairs), F32))
    hot_d = (lax.broadcasted_iota(jnp.int32, (8, pairs), 0) == owner_d).astype(F32)
    return lax.dot_general(
        hot_d, jnp.concatenate(spread, axis=0), (((1,), (1,)), ((), ())), precision=HIGHEST,
        preferred_element_type=F32,
    )


def final_kernel(tiles, out):
    mine = lax.axis_index("strike") * 2
    summed = jnp.sum(tiles[...], axis=0, keepdims=True)
    lane = lax.broadcasted_iota(jnp.int32, (2, NZL), 1)
    place = lax.broadcasted_iota(jnp.int32, (2, NZL), 0)
    for c in range(3):
        hit = lane == 32 * c + mine + place
        out[:, pl.ds(c, 1)] = jnp.sum(jnp.where(hit, summed, 0.0), axis=1, keepdims=True)


def call(kernel, name, outs, scratch=(), flops=0, moved=0, in_specs=None):
    specs = {} if in_specs is None else {"in_specs": in_specs}
    return pl.pallas_call(
        kernel,
        out_shape=[jax.ShapeDtypeStruct(o, F32) if isinstance(o, tuple) else jax.typeof(o) for o in outs],
        scratch_shapes=[pltpu.VMEM(shape, F32) if isinstance(shape, tuple) else shape for shape in scratch],
        compiler_params=pltpu.CompilerParams(vmem_limit_bytes=16 * 2**20),
        cost_estimate=pl.CostEstimate(flops=flops, bytes_accessed=moved, transcendentals=0),
        name=name,
        **specs,
    )


def swap_near(value, axis):
    return lax.ppermute(value, axis, [(i, i ^ 1) for i in range(lax.axis_size(axis))])


def swap_far(value, axis):
    lower = range(1, lax.axis_size(axis) - 1, 2)
    return lax.ppermute(value, axis, [(i, i + 1) for i in lower] + [(i + 1, i) for i in lower])


def local(field_now, field_prev, rigidity, density, fault_nodes, patch_ids):
    axes = ("normal", "strike", "depth")
    counts = tuple(lax.axis_size(a) for a in axes)
    flat, block, tile = (3, ROWS, NZL), (ROWS, NZL), (8, NZL)
    now, prev = field_now.reshape(flat), field_prev.reshape(flat)
    rig, rho = rigidity.reshape(block), density.reshape(block)
    nodes, ids = fault_nodes.reshape(1, -1), patch_ids.reshape(1, -1)
    x_up, x_down, y_up, y_down = ((n, NZL) for n in (X_UP, X_DOWN, Y_UP, Y_DOWN))
    faces, strip = (48, NZL), (24, NZL)
    xa, xb, za, zb, zd_own, tails, rw, now, prev, rho, nodes, ids = call(
        pack_kernel, "pack",
        [x_up, x_up, tile, tile, tile, (32, NZL), block, flat, flat, rho, nodes, ids],
        [pltpu.VMEM(block, jnp.bfloat16), x_up, x_down, tile, pltpu.SemaphoreType.DMA((6,))],
        flops=2_000_000, moved=900_000, in_specs=[pl.BlockSpec(memory_space=pltpu.HBM)] * 6,
    )(*(pltpu.with_memory_space_constraint(x, pltpu.HBM) for x in (now, prev, rig, rho, nodes, ids)))
    xa, xb = swap_near(xa, "normal"), swap_far(xb, "normal")
    zb, za = swap_far(zb, "depth"), swap_near(za, "depth")
    inner, term, scale = call(
        inner_kernel, "inner", [flat, faces, block], [flat], flops=10_000_000, moved=900_000,
    )(now, prev, rw, rho)
    base, yb, ya, early, mx, mz, xd, zd = call(
        functools.partial(edge_kernel, counts), "edge",
        [flat, y_up, y_up, faces, (16, NZL), tile, x_down, tile],
        [x_up, tile, y_up, y_down], flops=2_000_000, moved=900_000,
    )(inner, now, rw, scale, term, tails, xa, xb, za, zb, zd_own)
    yb, ya = swap_far(yb, "strike"), swap_near(ya, "strike")
    mid, kept, to_depth, xa2, xb2, zd2, my, y_low, y_high, r_high = call(
        functools.partial(whole_kernel, counts), "whole",
        [flat, flat, (8 * counts[2], NZL), faces, faces, tile, tile, strip, strip, tile],
        [faces, y_up, y_down, faces, faces, tile], flops=2_000_000, moved=900_000,
    )(base, now, rw, scale, early, yb, ya, mx, xd, zd, nodes, ids)
    got_z = lax.all_to_all(to_depth, "depth", 0, 0, tiled=True)
    (to_face,) = call(
        functools.partial(sum_kernel, counts), "add", [(counts[0] * counts[1], NZL)], flops=10_000, moved=80_000,
    )(got_z)
    got_face = lax.all_to_all(to_face, ("normal", "strike"), 0, 0, tiled=True)
    xa2, xb2 = swap_near(xa2, "normal"), swap_far(xb2, "normal")
    (share,) = call(final_kernel, "final", [(2, 3)], flops=10_000, moved=10_000)(got_face)
    (following,) = call(
        functools.partial(second_kernel, counts), "second", [flat], [flat, faces, faces, tile, tile],
        flops=10_000_000, moved=900_000,
    )(kept, now, rw, scale, xa2, xb2, got_z, zd2, mx, my, mz, xd, zd, y_low, y_high, r_high)
    return following.reshape(field_now.shape), mid.reshape(field_now.shape), share


def solution(mesh):
    field = P(None, "normal", "strike", "depth")
    cells = P("normal", "strike", "depth")
    pairs = P("strike", "depth", None)
    return jax.shard_map(
        local,
        mesh=mesh,
        in_specs=(field, field, cells, cells, pairs, pairs),
        out_specs=(field, field, P(("strike", "depth"), None)),
        check_vma=False,
    )
```

```python
import functools
import math

import jax
import jax.numpy as jnp
import numpy as np
from jax import lax
from jax.experimental import pallas as pl
from jax.experimental.pallas import tpu as pltpu
from jax.sharding import PartitionSpec as P

DT = 0.03
NXL, NYL, NZL = 8, 16, 128
ROWS = NXL * NYL
F32 = jnp.float32
HIGHEST = lax.Precision.HIGHEST


def gll_tables():
    spread = math.sqrt(3.0 / 7.0)
    points = np.array([-1.0, -spread, 0.0, spread, 1.0])
    weights = np.array([0.1, 49.0 / 90.0, 32.0 / 45.0, 49.0 / 90.0, 0.1]) * 0.5
    derivative = np.zeros((5, 5))
    for b in range(5):
        for a in range(5):
            if a == b:
                derivative[b, a] = sum(1.0 / (points[b] - points[o]) for o in range(5) if o != b)
            else:
                row = np.prod([points[b] - points[o] for o in range(5) if o != b and o != a])
                col = np.prod([points[a] - points[o] for o in range(5) if o != a and o != b])
                derivative[b, a] = row / (col * (points[a] - points[b]))
    return weights, 2.0 * derivative


WQ, D = gll_tables()
W0 = float(WQ[0])
NODE_W = np.array([2 * WQ[0], WQ[1], WQ[2], WQ[3], 2 * WQ[0]])
E = (WQ[:, None] * D).T / NODE_W[:, None]
KAPPA = float(E[4, 4])


def total(pairs):
    acc = None
    for const, arr in pairs:
        if abs(const) < 1e-12:
            continue
        term = arr * np.float32(const)
        acc = term if acc is None else acc + term
    return acc


def element(v, r):
    twice = v[2] + v[2]
    s0, s1 = v[0] + v[4] - twice, v[1] + v[3] - twice
    d0, d1 = v[0] - v[4], v[1] - v[3]
    ev = [total([((D[b, 0] + D[b, 4]) / 2, s0), ((D[b, 1] + D[b, 3]) / 2, s1)]) for b in (0, 1)]
    od = [total([((D[b, 0] - D[b, 4]) / 2, d0), ((D[b, 1] - D[b, 3]) / 2, d1)]) for b in (0, 1)]
    g2 = total([(D[2, 0], d0), (D[2, 1], d1)])
    q = [r[0] * (od[0] + ev[0]), r[1] * (od[1] + ev[1]), r[2] * g2, r[3] * (od[1] - ev[1]), r[4] * (od[0] - ev[0])]
    p0, m0, p1, m1 = q[0] + q[4], q[0] - q[4], q[1] + q[3], q[1] - q[3]
    ec = [total([((E[a, 0] + E[a, 4]) / 2, p0), ((E[a, 1] + E[a, 3]) / 2, p1), (E[a, 2], q[2])]) for a in (0, 1)]
    oc = [total([((E[a, 0] - E[a, 4]) / 2, m0), ((E[a, 1] - E[a, 3]) / 2, m1)]) for a in (0, 1)]
    c2 = total([(E[2, 0], m0), (E[2, 1], m1)])
    return [oc[0] + ec[0], oc[1] + ec[1], c2, oc[1] - ec[1], oc[0] - ec[0]]


def first_term(v, r):
    twice = v[2] + v[2]
    s0, s1 = v[0] + v[4] - twice, v[1] + v[3] - twice
    d0, d1 = v[0] - v[4], v[1] - v[3]
    ev = [total([((D[b, 0] + D[b, 4]) / 2, s0), ((D[b, 1] + D[b, 3]) / 2, s1)]) for b in (0, 1)]
    od = [total([((D[b, 0] - D[b, 4]) / 2, d0), ((D[b, 1] - D[b, 3]) / 2, d1)]) for b in (0, 1)]
    g2 = total([(D[2, 0], d0), (D[2, 1], d1)])
    q = [r[0] * (od[0] + ev[0]), r[1] * (od[1] + ev[1]), r[2] * g2, r[3] * (od[1] - ev[1]), r[4] * (od[0] - ev[0])]
    return total([(E[0, b], q[b]) for b in range(5)])


def open_terms(v, r):
    flux = [r[b] * total([(D[b, a], v[a]) for a in range(4)]) for b in range(4)]
    part = total([(E[4, b], flux[b]) for b in range(4)])
    grad = total([(D[4, a], v[a]) for a in range(4)])
    return part, grad


def open_scale(r):
    return total([(E[4, b] * D[b, 4], r[b]) for b in range(4)])


def rolled(x, shift):
    shift = shift % NZL
    return x if shift == 0 else pltpu.roll(x, shift, 1)


def lane_of():
    return lax.broadcasted_iota(jnp.int32, (8, NZL), 1)


def lane_table(phase, values):
    out = jnp.full((8, NZL), np.float32(values[0]), F32)
    for b in range(1, 4):
        out = jnp.where(phase == b, np.float32(values[b]), out)
    return out


def x_rows(x, half):
    return pl.ds(x * NYL + half * 8, 8)


def y_rows(y):
    return pl.ds(y, 8, stride=NYL)


def first_lanes(read, read_r, lane):
    out = jnp.zeros((8, NZL), F32)
    for k in range(16):
        rows = pl.ds(8 * k, 8)
        for c in range(3 if read_r is None else 4):
            src = read_r(rows) if c == 3 else read(c, rows)
            out = jnp.where(lane == 4 * k + c, rolled(src, 4 * k + c), out)
    return out


def last_lanes(read, lane):
    out = jnp.zeros((8, NZL), F32)
    for k in range(16):
        out = jnp.where((lane >> 2) == k, rolled(read(pl.ds(8 * k, 8)), 4 * k + 4), out)
    return out


def interleaved(parts, lane, base):
    out = jnp.zeros((8, NZL), F32)
    for j, part in enumerate(parts):
        if part is None:
            continue
        out = jnp.where((lane >= base) & (lane < base + 64) & ((lane & 3) == j), rolled(part, base + j - 3), out)
    return out


def widen(src, dst):
    for x in range(NXL):
        dst[pl.ds(x * NYL, NYL), :] = src[pl.ds(x * NYL, NYL), :].astype(F32)


X_UP, X_DOWN = 112, 64
Y_UP, Y_DOWN = 136, 64


def place():
    return tuple(lax.axis_index(axis) for axis in ("normal", "strike", "depth"))


def paired(index, up, down, near, far):
    even = (index & 1) == 0
    rows = pl.ds(0, down.shape[0])
    near[...] = up[...]
    far[...] = up[...]
    near[rows, :] = jnp.where(even, up[rows, :], down[...])
    far[rows, :] = jnp.where(even, down[...], up[rows, :])


def unpaired(index, near, far, low, high):
    even = (index & 1) == 0
    rows = pl.ds(0, high.shape[0])
    low[...] = jnp.where(even, far[...], near[...])
    high[...] = jnp.where(even, near[rows, :], far[rows, :])


def beside(index, count, got, low, high):
    below = pl.multiple_of((jnp.maximum(index - 1, 0)) * 8, 8)
    above = pl.multiple_of((jnp.minimum(index + 1, count - 1)) * 8, 8)
    low[...] = jnp.where(index > 0, got[pl.ds(below, low.shape[0]), :], 0.0)
    high[...] = jnp.where(index < count - 1, got[pl.ds(above, high.shape[0]), :], 0.0)


Y_SPLIT, Y_PAIRS = (0, 1, 2, 3, 4, 5, 12), ((6, 7), (8, 9), (10, 11), (13, 14), (15, 16))
Y_TILES = len(Y_SPLIT) + len(Y_PAIRS)


def plane_of(ref, n):
    return ref[pl.ds(8 * n, 8), :]


def in_parts(value):
    return jnp.concatenate([value, value - value.astype(jnp.bfloat16).astype(F32)], axis=0)


def y_pack(index, up, down, near, far):
    even = (index & 1) == 0
    ups = [in_parts(plane_of(up, n)) for n in Y_SPLIT]
    ups += [jnp.concatenate([plane_of(up, a), plane_of(up, b)], axis=0) for a, b in Y_PAIRS]
    for t, above in enumerate(ups):
        below = in_parts(plane_of(down, t)) if t < Y_DOWN // 8 else above
        rows = pl.ds(16 * t, 16)
        near[rows, :] = jnp.where(even, above, below).astype(jnp.bfloat16)
        far[rows, :] = jnp.where(even, below, above).astype(jnp.bfloat16)


def y_unpack(index, near, far, low, high):
    even = (index & 1) == 0
    for t in range(Y_TILES):
        rows = pl.ds(16 * t, 16)
        from_near, from_far = near[rows, :].astype(F32), far[rows, :].astype(F32)
        below, above = jnp.where(even, from_far, from_near), jnp.where(even, from_near, from_far)
        if t < Y_DOWN // 8:
            high[pl.ds(8 * t, 8), :] = above[:8, :] + above[8:, :]
        if t < len(Y_SPLIT):
            low[pl.ds(8 * Y_SPLIT[t], 8), :] = below[:8, :] + below[8:, :]
        else:
            for part, n in enumerate(Y_PAIRS[t - len(Y_SPLIT)]):
                low[pl.ds(8 * n, 8), :] = below[8 * part : 8 * part + 8, :]


def pack_kernel(
    now_hbm, prev_hbm, rig_hbm, rho_hbm, nodes_hbm, ids_hbm,
    xa, xb, za, zb, zd, tails, rw, now, prev, rho, nodes, ids,
    rig, xu, xd, zu, sems,
):
    pairs = (
        (rig_hbm, rig), (now_hbm, now), (prev_hbm, prev), (rho_hbm, rho), (nodes_hbm, nodes), (ids_hbm, ids),
    )
    copies = [pltpu.make_async_copy(src, dst, sems.at[i]) for i, (src, dst) in enumerate(pairs)]
    for copy in copies:
        copy.start()
    for copy in copies[:2]:
        copy.wait()
    widen(rig, rw)
    lane = lane_of()
    for half in range(2):
        r = [rw[x_rows(4 + a, half), :] for a in range(4)]
        xu[pl.ds(96 + 8 * half, 8), :] = open_scale(r)
        xd[pl.ds(48 + 8 * half, 8), :] = rw[x_rows(0, half), :]
        for c in range(3):
            part, grad = open_terms([now[c, x_rows(4 + a, half), :] for a in range(4)], r)
            xu[pl.ds(16 * c + 8 * half, 8), :] = part
            xu[pl.ds(48 + 16 * c + 8 * half, 8), :] = grad
            xd[pl.ds(16 * c + 8 * half, 8), :] = now[c, x_rows(0, half), :]
    back = lambda t: [rolled(t, 3 - a) for a in range(4)]
    tails[pl.ds(24, 8), :] = last_lanes(lambda rows: rw[rows, :], lane)
    r = back(tails[pl.ds(24, 8), :])
    parts, grads = [], []
    for c in range(3):
        tails[pl.ds(8 * c, 8), :] = last_lanes(lambda rows: now[c, rows, :], lane)
        part, grad = open_terms(back(tails[pl.ds(8 * c, 8), :]), r)
        parts.append(part)
        grads.append(grad)
    zu[...] = jnp.where(
        lane < 64, interleaved(parts + [open_scale(r)], lane, 0), interleaved(grads + [None], lane, 64)
    )
    zd[...] = first_lanes(lambda c, rows: now[c, rows, :], lambda rows: rw[rows, :], lane)
    index = place()
    paired(index[0], xu, xd, xa, xb)
    paired(index[2], zu, zd, za, zb)
    for copy in copies[2:]:
        copy.wait()


def advance(now, prev, rw, low, high_v, high_r, scale, ghost_z, ghost_rz, closing_z, index, store, acc, on_first):
    index_x, index_y, index_z = index
    at_x = jnp.where(index_x == 0, 2.0, 1.0).astype(F32)
    at_y = jnp.where(index_y == 0, 2.0, 1.0).astype(F32)
    at_z = jnp.where(index_z == 0, 2.0, 1.0).astype(F32)

    def along_y(c, carry):
        none = jnp.zeros((8, NZL), F32)
        v = [now[c, y_rows(y), :] for y in range(NYL)] + [high_v[1][pl.ds(8 * c, 8), :] if high_v[1] is not None else none]
        r = [rw[y_rows(y), :] for y in range(NYL)] + [high_r[1][...] if high_r[1] is not None else none]
        carried = low[1](c, v[0]) if low[1] is not None else none
        for e in range(4):
            terms = element(v[4 * e : 4 * e + 5], r[4 * e : 4 * e + 5])
            head = terms[0] * at_y if e == 0 else terms[0]
            acc[c, y_rows(4 * e), :] = head + carried
            for a in range(1, 4):
                acc[c, y_rows(4 * e + a), :] = terms[a]
            carried = terms[4]
        return carry

    lax.fori_loop(0, 3, along_y, 0)
    alone = ghost_z is None

    lane = lane_of()
    phase = lane & 3
    gm = [lane_table(phase, [D[b, b - k] if b >= k else 0 for b in range(4)]) for k in range(4)]
    gp = [None] + [lane_table(phase, [D[b, b + k] if b + k <= 4 else 0 for b in range(4)]) for k in range(1, 5)]
    cm = [lane_table(phase, [E[a, a - k] if a >= k else 0 for a in range(4)]) for k in range(4)]
    cp = [None] + [lane_table(phase, [E[a, a + k] if a + k <= 3 else 0 for a in range(4)]) for k in range(1, 4)]
    c_close = lane_table(phase, [E[a, 4] for a in range(4)])
    last = [lane_table(phase, [0, 0, 0, E[4, b]]) for b in range(5)]
    first = lane == 0
    edge = jnp.where(first, at_z, jnp.float32(1.0))

    def along_xz(n, carry):
        c, half = n >> 1, n & 1
        offset = half * 8
        rows = [pl.ds(pl.multiple_of(x * NYL + offset, 8), 8) for x in range(NXL)]
        plane = pl.ds(pl.multiple_of(16 * c + offset, 8), 8)
        none = jnp.zeros((8, NZL), F32)
        v = [now[c, rows[x], :] for x in range(NXL)] + [none if alone else high_v[0][plane, :]]
        r = [rw[rows[x], :] for x in range(NXL)]
        r.append(none if alone else high_r[0][pl.ds(pl.multiple_of(offset, 8), 8), :])
        carried = none if alone else low[0](c, offset, plane, v[0])
        back = NZL - (4 * half + c)
        ghost_v = 0.0 if alone else pltpu.roll(ghost_z, back, 1)
        ghost_r = 0.0 if alone else pltpu.roll(ghost_rz, NZL - 4 * half, 1)
        closing = 0.0 if alone else pltpu.roll(closing_z, back, 1)
        for e in range(2):
            terms = element(v[4 * e : 4 * e + 5], r[4 * e : 4 * e + 5])
            if e == 0:
                on_first(c, plane, carried, terms[0])
            for a in range(4):
                x = 4 * e + a
                force = terms[a] + acc[c, rows[x], :]
                if a == 0:
                    force = (terms[0] * at_x if e == 0 else terms[0]) + carried + acc[c, rows[x], :]
                vx = jnp.where(first, ghost_v if alone else rolled(ghost_v, -8 * x), v[x])
                rx = jnp.where(first, ghost_r if alone else rolled(ghost_r, -8 * x), r[x])
                vm = [v[x]] + [rolled(v[x], k) for k in range(1, 4)]
                vp = [None] + [rolled(vx, -k) for k in range(1, 5)]
                g = gm[0] * v[x]
                for k in range(1, 4):
                    g = g + gm[k] * vm[k]
                for k in range(1, 5):
                    g = g + gp[k] * vp[k]
                g4 = total([(D[4, 0], vm[3]), (D[4, 1], vm[2]), (D[4, 2], vm[1]), (D[4, 3], vm[0]), (D[4, 4], vp[1])])
                q = r[x] * g
                q4 = jnp.where(phase == 3, rolled(rx, -1) * g4, 0.0)
                qm = [q] + [rolled(q, k) for k in range(1, 4)]
                own = cm[0] * q
                for k in range(1, 4):
                    own = own + cm[k] * qm[k]
                for k in range(1, 4):
                    own = own + cp[k] * rolled(q, -k)
                pair = q4 + rolled(q4, -1)
                own = own + c_close * (pair + rolled(pair, -2))
                tail = last[3] * q + last[4] * q4
                for b in range(3):
                    tail = tail + last[b] * qm[3 - b]
                tail = jnp.where(first, closing if alone else rolled(closing, -8 * x), rolled(tail, 1))
                force = force + own * edge + tail
                after = (v[x] + v[x]) - prev[c, rows[x], :] - scale[rows[x], :] * force
                store(c, x, rows[x], plane, after)
            carried = terms[4]
        return carry

    lax.fori_loop(0, 6, along_xz, 0)


def step_scale(rho, scale):
    for x in range(NXL):
        rows = pl.ds(x * NYL, NYL)
        scale[rows, :] = np.float32(DT * DT) / rho[rows, :].astype(F32)


def axis_weight(pos, is_first):
    phase = pos & 3
    out = jnp.full(pos.shape, np.float32(2 * W0), F32)
    for b in range(1, 4):
        out = jnp.where(phase == b, np.float32(WQ[b]), out)
    return jnp.where((pos == 0) & is_first, np.float32(W0), out)


def inner_kernel(now, prev, rw, rho, base, term, scale, acc):
    step_scale(rho, scale)

    def store(c, x, rows, plane, after):
        base[c, rows, :] = after

    def on_first(c, plane, carried, own):
        term[plane, :] = own

    nothing = (None, None)
    advance(now, prev, rw, nothing, nothing, nothing, scale, None, None, None, place(), store, acc, on_first)


def spread_from(tile, lane, source):
    phase = lane & 3
    out = tile
    for j in range(4):
        if j != source:
            out = jnp.where(phase == j, rolled(tile, j - source), out)
    return out


def edge_kernel(
    counts, inner, now, rw, scale, term, tails, xa, xb, za, zb, zd_own,
    base, yb, ya, early, mx, mz, xd, zd,
    xu, zu, yu, yd,
):
    index = place()
    unpaired(index[0], xa, xb, xu, xd)
    unpaired(index[2], za, zb, zu, zd)
    lane = lane_of()
    phase = lane & 3
    has_x, has_z = (index[0] > 0).astype(F32), (index[2] > 0).astype(F32)
    kappa, diagonal, d44 = np.float32(KAPPA), np.float32(KAPPA * D[4, 4]), np.float32(D[4, 4])

    own, above, below = zd_own[...], zu[...], zd[...]
    r_first = spread_from(own, lane, 3)
    gain = (spread_from(above, lane, 3) + diagonal * r_first) * has_z
    mz[...] = gain
    s_first = jnp.zeros((8, NZL), F32)
    for k in range(16):
        s_first = jnp.where(lane == 4 * k, rolled(scale[pl.ds(8 * k, 8), :], 4 * k), s_first)
    closing = spread_from(s_first, lane, 0) * (above + kappa * r_first * rolled(above, 64) + gain * own)
    r_tail = tails[pl.ds(24, 8), :]
    s_tail = last_lanes(lambda rows: scale[rows, :], lane)
    weights = [
        lane_table(phase, [E[a, a + k] * D[a + k, 4] if 0 <= a + k <= 3 else 0 for a in range(4)]) for k in range(-3, 4)
    ]
    by_value = s_tail * sum(w * rolled(r_tail, -k) for w, k in zip(weights, range(-3, 4)))
    by_flux = s_tail * lane_table(phase, [E[a, 4] for a in range(4)])
    r_below = spread_from(below, lane, 3)
    last = lane >= NZL - 4
    for c in range(3):
        tail = tails[pl.ds(8 * c, 8), :]
        grad = spread_from(total([(D[4, a], rolled(tail, 3 - a)) for a in range(4)]), lane, 3)
        value = spread_from(below, lane, c)
        taken = by_value * value + by_flux * (r_below * (grad + d44 * value))
        for k in range(16):
            rows = pl.ds(8 * k, 8)
            off = jnp.where(lane == 0, rolled(closing, -(4 * k + c)), 0.0)
            base[c, rows, :] = inner[c, rows, :] - jnp.where(last, rolled(taken, NZL - 4 - 4 * k), off)

    for half in range(2):
        rows = pl.ds(8 * half, 8)
        r = [rw[x_rows(4 + a, half), :] for a in range(4)]
        by_value, by_flux = open_response([scale[x_rows(4 + a, half), :] for a in range(4)], r)
        r0, r8 = rw[x_rows(0, half), :], xd[pl.ds(48 + 8 * half, 8), :]
        gain = (xu[pl.ds(96 + 8 * half, 8), :] + diagonal * r0) * has_x
        mx[rows, :] = gain
        for c in range(3):
            plane = pl.ds(16 * c + 8 * half, 8)
            grad = xu[pl.ds(48 + 16 * c + 8 * half, 8), :]
            carried = xu[plane, :] + kappa * r0 * grad + gain * now[c, x_rows(0, half), :]
            early[plane, :] = carried - term[plane, :]
            base[c, x_rows(0, half), :] = base[c, x_rows(0, half), :] - scale[x_rows(0, half), :] * carried
            value = xd[plane, :]
            flux = r8 * (total([(D[4, a], now[c, x_rows(4 + a, half), :]) for a in range(4)]) + d44 * value)
            for a in range(4):
                at = x_rows(4 + a, half)
                base[c, at, :] = base[c, at, :] - by_value[a] * value - by_flux[a] * flux

    r = [rw[y_rows(12 + a), :] for a in range(4)]
    by_value, by_flux = open_response([scale[y_rows(12 + a), :] for a in range(4)], r)
    planes = [open_scale(r), *open_terms(by_value, r), *open_terms(by_flux, r)]
    for n, plane in enumerate(planes):
        yu[pl.ds(96 + 8 * n, 8), :] = plane
    for c in range(3):
        planes = open_terms([now[c, y_rows(12 + a), :] for a in range(4)], r)
        planes += open_terms([base[c, y_rows(12 + a), :] for a in range(4)], r)
        for n, plane in enumerate(planes):
            yu[pl.ds(24 * n + 8 * c, 8), :] = plane
        yd[pl.ds(8 * c, 8), :] = now[c, y_rows(0), :]
        yd[pl.ds(24 + 8 * c, 8), :] = base[c, y_rows(0), :]
    yd[pl.ds(48, 8), :] = rw[y_rows(0), :]
    yd[pl.ds(56, 8), :] = scale[y_rows(0), :]
    y_pack(index[1], yu, yd, ya, yb)


def open_response(scale, r):
    by_value = [scale[a] * total([(E[a, b] * D[b, 4], r[b]) for b in range(4)]) for a in range(4)]
    by_flux = [scale[a] * np.float32(E[a, 4]) for a in range(4)]
    return by_value, by_flux


def whole_kernel(
    counts, base, now, rw, scale, early, yb, ya, mx, xd, zd, nodes, ids,
    out, kept, to_depth, xa2, xb2, zd2, my, y_low, y_high, r_high,
    slip, yu, yd, xu2, xd2, zu2,
):
    middle = counts[0] // 2
    index = place()
    lane = lane_of()
    kappa, diagonal = np.float32(KAPPA), np.float32(KAPPA * D[4, 4])
    d44 = np.float32(D[4, 4])
    y_unpack(index[1], ya, yb, yu, yd)
    for c in range(3):
        for k in range(16):
            rows = pl.ds(8 * k, 8)
            values = base[c, rows, :]
            out[c, rows, :] = values
            kept[c, rows, :] = values
    r = [rw[y_rows(12 + a), :] for a in range(4)]
    by_value, by_flux = open_response([scale[y_rows(12 + a), :] for a in range(4)], r)
    own_scale = open_scale(r)
    r0, s0 = rw[y_rows(0), :], scale[y_rows(0), :]
    r_above, s_above = yd[pl.ds(48, 8), :], yd[pl.ds(56, 8), :]
    r_high[...] = r_above
    gain, value_part, value_grad, flux_part, flux_grad = (yu[pl.ds(96 + 8 * n, 8), :] for n in range(5))
    gain = (gain + diagonal * r0) * (index[1] > 0).astype(F32)
    my[...] = gain
    for c in range(3):
        plane = pl.ds(8 * c, 8)
        part, grad, part2, grad2 = (yu[pl.ds(24 * n + 8 * c, 8), :] for n in range(4))
        v0 = now[c, y_rows(0), :]
        after = base[c, y_rows(0), :] - s0 * (part + kappa * r0 * grad + gain * v0)
        out[c, y_rows(0), :] = after
        kept[c, y_rows(0), :] = after
        flux = r0 * (grad + d44 * v0)
        y_low[plane, :] = (part2 - value_part * v0 - flux_part * flux) + kappa * r0 * (
            grad2 - value_grad * v0 - flux_grad * flux
        )
        above = yd[plane, :]
        part, grad = open_terms([now[c, y_rows(12 + a), :] for a in range(4)], r)
        flux = r_above * (grad + d44 * above)
        y_high[plane, :] = yd[pl.ds(24 + 8 * c, 8), :] - s_above * (part + own_scale * above + kappa * flux)
        for a in range(4):
            after = base[c, y_rows(12 + a), :] - by_value[a] * above - by_flux[a] * flux
            out[c, y_rows(12 + a), :] = after
            kept[c, y_rows(12 + a), :] = after

    on_one, on_two = index[0] == middle - 1, index[0] == middle
    for half in range(2):
        rows = pl.ds(8 * half, 8)
        r = [rw[x_rows(x, half), :] for x in range(8)] + [xd[pl.ds(48 + 8 * half, 8), :]]
        y_pos = lax.broadcasted_iota(jnp.int32, (8, NZL), 0) + 8 * half
        face = axis_weight(y_pos, index[1] == 0) * axis_weight(lane, index[2] == 0) * np.float32(W0)
        for c in range(3):
            plane = pl.ds(16 * c + 8 * half, 8)
            v = [out[c, x_rows(x, half), :] for x in range(8)]
            part, grad = open_terms(v[4:], r[4:8])
            sent = part + kappa * r[8] * grad
            xu2[plane, :] = sent
            xd2[plane, :] = v[0]
            here = early[plane, :] + mx[rows, :] * v[0] - first_term(v[:5], r[:5])
            slip[plane, :] = face * jnp.where(on_one, sent, jnp.where(on_two, here, 0.0))
    back = lambda t: [rolled(t, 3 - a) for a in range(4)]
    r = back(last_lanes(lambda rows: rw[rows, :], lane))
    sent = []
    for c in range(3):
        part, grad = open_terms(back(last_lanes(lambda rows: out[c, rows, :], lane)), r)
        sent.append(part + kappa * zd[...] * grad)
    zu2[...] = interleaved(sent + [None], lane, 0)
    zd2[...] = first_lanes(lambda c, rows: out[c, rows, :], None, lane)
    paired(index[0], xu2, xd2, xa2, xb2)
    tile = patch_tile(counts[2], slip[...], nodes[...], ids[...])
    for d in range(counts[2]):
        halo = jnp.where(d > index[2], zu2[...], zd2[...])
        to_depth[pl.ds(8 * d, 8), :] = with_row(halo, tile[d : d + 1, :], lane)


def with_row(halo, row, lane):
    sub = lax.broadcasted_iota(jnp.int32, (8, NZL), 0)
    row = jnp.broadcast_to(row, (8, NZL))
    spread = jnp.where(sub == 0, rolled(row, 64), jnp.where(sub == 1, row, 0.0))
    return jnp.where(lane < 64, halo, spread)


def sum_kernel(counts, got, to_face):
    summed = got[pl.ds(0, 8), :]
    for d in range(1, counts[2]):
        summed = summed + got[pl.ds(8 * d, 8), :]
    low = jnp.broadcast_to(rolled(summed, 64)[0:1, :], (8, NZL))
    high = jnp.broadcast_to(summed[1:2, :], (8, NZL))
    row = jnp.where(lane_of() < 64, low, high)
    for k in range(counts[0] * counts[1] // 8):
        to_face[pl.ds(8 * k, 8), :] = row


def second_kernel(
    counts, now, prev, rw, scale, xa2, xb2, got_z, zd2_own, mx, my, mz, xd, zd, y_low, y_high, r_high,
    out, acc, xu2, xd2, zu2, zd2,
):
    index = place()
    unpaired(index[0], xa2, xb2, xu2, xd2)
    beside(index[2], counts[2], got_z, zu2, zd2)
    closing_z = zu2[...] + mz[...] * zd2_own[...]

    def low_x(c, offset, plane, v0):
        return xu2[plane, :] + mx[pl.ds(pl.multiple_of(offset, 8), 8), :] * v0

    def low_y(c, v0):
        return y_low[pl.ds(pl.multiple_of(8 * c, 8), 8), :] + my[...] * v0

    def store(c, x, rows, plane, after):
        out[c, rows, :] = after

    advance(
        now, prev, rw, (low_x, low_y), (xd2, y_high), (xd.at[pl.ds(48, 16)], r_high), scale,
        zd2[...], rolled(zd[...], -3), closing_z, index, store, acc, lambda *args: None,
    )


def patch_tile(count_d, slip, node, patch):
    pairs = node.shape[-1]
    hot_z = (lax.broadcasted_iota(jnp.int32, (NZL, pairs), 0) == (node & (NZL - 1))).astype(F32)
    at_z = jnp.dot(slip, hot_z, precision=HIGHEST, preferred_element_type=F32)
    row_y = lax.broadcasted_iota(jnp.int32, (NYL, pairs), 0) == (node >> 7)
    owner = patch >> 1
    owner_d = owner & (count_d - 1)
    slot = ((owner >> (count_d.bit_length() - 1)) << 1) + (patch & 1)
    hot_slot = lax.broadcasted_iota(jnp.int32, (32, pairs), 0) == slot
    spread = []
    for c in range(3):
        picked = jnp.sum(jnp.where(row_y, at_z[NYL * c : NYL * (c + 1), :], 0.0), axis=0, keepdims=True)
        spread.append(jnp.where(hot_slot, picked, 0.0))
    spread.append(jnp.zeros((32, pairs), F32))
    hot_d = (lax.broadcasted_iota(jnp.int32, (8, pairs), 0) == owner_d).astype(F32)
    return lax.dot_general(
        hot_d, jnp.concatenate(spread, axis=0), (((1,), (1,)), ((), ())), precision=HIGHEST,
        preferred_element_type=F32,
    )


def final_kernel(tiles, out):
    mine = lax.axis_index("strike") * 2
    summed = jnp.sum(tiles[...], axis=0, keepdims=True)
    lane = lax.broadcasted_iota(jnp.int32, (2, NZL), 1)
    place = lax.broadcasted_iota(jnp.int32, (2, NZL), 0)
    for c in range(3):
        hit = lane == 32 * c + mine + place
        out[:, pl.ds(c, 1)] = jnp.sum(jnp.where(hit, summed, 0.0), axis=1, keepdims=True)


def call(kernel, name, outs, scratch=(), flops=0, moved=0, in_specs=None):
    specs = {} if in_specs is None else {"in_specs": in_specs}
    return pl.pallas_call(
        kernel,
        out_shape=[jax.ShapeDtypeStruct(o, F32) if isinstance(o, tuple) else jax.ShapeDtypeStruct(o.shape, o.dtype) for o in outs],
        scratch_shapes=[pltpu.VMEM(shape, F32) if isinstance(shape, tuple) else shape for shape in scratch],
        compiler_params=pltpu.CompilerParams(vmem_limit_bytes=16 * 2**20),
        cost_estimate=pl.CostEstimate(flops=flops, bytes_accessed=moved, transcendentals=0),
        name=name,
        **specs,
    )


def swap_near(value, axis):
    return lax.ppermute(value, axis, [(i, i ^ 1) for i in range(lax.axis_size(axis))])


def swap_far(value, axis):
    lower = range(1, lax.axis_size(axis) - 1, 2)
    return lax.ppermute(value, axis, [(i, i + 1) for i in lower] + [(i + 1, i) for i in lower])


def local(field_now, field_prev, rigidity, density, fault_nodes, patch_ids):
    axes = ("normal", "strike", "depth")
    counts = tuple(lax.axis_size(a) for a in axes)
    flat, block, tile = (3, ROWS, NZL), (ROWS, NZL), (8, NZL)
    now, prev = field_now.reshape(flat), field_prev.reshape(flat)
    rig, rho = rigidity.reshape(block), density.reshape(block)
    nodes, ids = fault_nodes.reshape(1, -1), patch_ids.reshape(1, -1)
    x_up, x_down, y_up, y_down = ((n, NZL) for n in (X_UP, X_DOWN, Y_UP, Y_DOWN))
    faces, strip = (48, NZL), (24, NZL)
    y_sent = jax.ShapeDtypeStruct((16 * Y_TILES, NZL), jnp.bfloat16)
    xa, xb, za, zb, zd_own, tails, rw, now, prev, rho, nodes, ids = call(
        pack_kernel, "pack",
        [x_up, x_up, tile, tile, tile, (32, NZL), block, flat, flat, rho, nodes, ids],
        [pltpu.VMEM(block, jnp.bfloat16), x_up, x_down, tile, pltpu.SemaphoreType.DMA((6,))],
        flops=2_000_000, moved=900_000, in_specs=[pl.BlockSpec(memory_space=pltpu.HBM)] * 6,
    )(*(pltpu.with_memory_space_constraint(x, pltpu.HBM) for x in (now, prev, rig, rho, nodes, ids)))
    xa, xb = swap_near(xa, "normal"), swap_far(xb, "normal")
    zb, za = swap_far(zb, "depth"), swap_near(za, "depth")
    inner, term, scale = call(
        inner_kernel, "inner", [flat, faces, block], [flat], flops=10_000_000, moved=900_000,
    )(now, prev, rw, rho)
    base, yb, ya, early, mx, mz, xd, zd = call(
        functools.partial(edge_kernel, counts), "edge",
        [flat, y_sent, y_sent, faces, (16, NZL), tile, x_down, tile],
        [x_up, tile, y_up, y_down], flops=2_000_000, moved=900_000,
    )(inner, now, rw, scale, term, tails, xa, xb, za, zb, zd_own)
    yb, ya = swap_far(yb, "strike"), swap_near(ya, "strike")
    mid, kept, to_depth, xa2, xb2, zd2, my, y_low, y_high, r_high = call(
        functools.partial(whole_kernel, counts), "whole",
        [flat, flat, (8 * counts[2], NZL), faces, faces, tile, tile, strip, strip, tile],
        [faces, y_up, y_down, faces, faces, tile], flops=2_000_000, moved=900_000,
    )(base, now, rw, scale, early, yb, ya, mx, xd, zd, nodes, ids)
    got_z = lax.all_to_all(to_depth, "depth", 0, 0, tiled=True)
    (to_face,) = call(
        functools.partial(sum_kernel, counts), "add", [(counts[0] * counts[1], NZL)], flops=10_000, moved=80_000,
    )(got_z)
    got_face = lax.all_to_all(to_face, ("normal", "strike"), 0, 0, tiled=True)
    xa2, xb2 = swap_near(xa2, "normal"), swap_far(xb2, "normal")
    (share,) = call(final_kernel, "final", [(2, 3)], flops=10_000, moved=10_000)(got_face)
    (following,) = call(
        functools.partial(second_kernel, counts), "second", [flat], [flat, faces, faces, tile, tile],
        flops=10_000_000, moved=900_000,
    )(kept, now, rw, scale, xa2, xb2, got_z, zd2, mx, my, mz, xd, zd, y_low, y_high, r_high)
    return following.reshape(field_now.shape), mid.reshape(field_now.shape), share


def solution(mesh):
    field = P(None, "normal", "strike", "depth")
    cells = P("normal", "strike", "depth")
    pairs = P("strike", "depth", None)
    return jax.shard_map(
        local,
        mesh=mesh,
        in_specs=(field, field, cells, cells, pairs, pairs),
        out_specs=(field, field, P(("strike", "depth"), None)),
        check_vma=False,
    )
```

```python
import functools
import math

import jax
import jax.numpy as jnp
import numpy as np
from jax import lax
from jax.experimental import pallas as pl
from jax.experimental.pallas import tpu as pltpu
from jax.sharding import PartitionSpec as P

DT = 0.03
NXL, NYL, NZL = 8, 16, 128
ROWS = NXL * NYL
F32 = jnp.float32
HIGHEST = lax.Precision.HIGHEST


def gll_tables():
    spread = math.sqrt(3.0 / 7.0)
    points = np.array([-1.0, -spread, 0.0, spread, 1.0])
    weights = np.array([0.1, 49.0 / 90.0, 32.0 / 45.0, 49.0 / 90.0, 0.1]) * 0.5
    derivative = np.zeros((5, 5))
    for b in range(5):
        for a in range(5):
            if a == b:
                derivative[b, a] = sum(1.0 / (points[b] - points[o]) for o in range(5) if o != b)
            else:
                row = np.prod([points[b] - points[o] for o in range(5) if o != b and o != a])
                col = np.prod([points[a] - points[o] for o in range(5) if o != a and o != b])
                derivative[b, a] = row / (col * (points[a] - points[b]))
    return weights, 2.0 * derivative


WQ, D = gll_tables()
W0 = float(WQ[0])
NODE_W = np.array([2 * WQ[0], WQ[1], WQ[2], WQ[3], 2 * WQ[0]])
E = (WQ[:, None] * D).T / NODE_W[:, None]
KAPPA = float(E[4, 4])


def total(pairs):
    acc = None
    for const, arr in pairs:
        if abs(const) < 1e-12:
            continue
        term = arr * np.float32(const)
        acc = term if acc is None else acc + term
    return acc


def element(v, r):
    twice = v[2] + v[2]
    s0, s1 = v[0] + v[4] - twice, v[1] + v[3] - twice
    d0, d1 = v[0] - v[4], v[1] - v[3]
    ev = [total([((D[b, 0] + D[b, 4]) / 2, s0), ((D[b, 1] + D[b, 3]) / 2, s1)]) for b in (0, 1)]
    od = [total([((D[b, 0] - D[b, 4]) / 2, d0), ((D[b, 1] - D[b, 3]) / 2, d1)]) for b in (0, 1)]
    g2 = total([(D[2, 0], d0), (D[2, 1], d1)])
    q = [r[0] * (od[0] + ev[0]), r[1] * (od[1] + ev[1]), r[2] * g2, r[3] * (od[1] - ev[1]), r[4] * (od[0] - ev[0])]
    p0, m0, p1, m1 = q[0] + q[4], q[0] - q[4], q[1] + q[3], q[1] - q[3]
    ec = [total([((E[a, 0] + E[a, 4]) / 2, p0), ((E[a, 1] + E[a, 3]) / 2, p1), (E[a, 2], q[2])]) for a in (0, 1)]
    oc = [total([((E[a, 0] - E[a, 4]) / 2, m0), ((E[a, 1] - E[a, 3]) / 2, m1)]) for a in (0, 1)]
    c2 = total([(E[2, 0], m0), (E[2, 1], m1)])
    return [oc[0] + ec[0], oc[1] + ec[1], c2, oc[1] - ec[1], oc[0] - ec[0]]


def first_term(v, r):
    twice = v[2] + v[2]
    s0, s1 = v[0] + v[4] - twice, v[1] + v[3] - twice
    d0, d1 = v[0] - v[4], v[1] - v[3]
    ev = [total([((D[b, 0] + D[b, 4]) / 2, s0), ((D[b, 1] + D[b, 3]) / 2, s1)]) for b in (0, 1)]
    od = [total([((D[b, 0] - D[b, 4]) / 2, d0), ((D[b, 1] - D[b, 3]) / 2, d1)]) for b in (0, 1)]
    g2 = total([(D[2, 0], d0), (D[2, 1], d1)])
    q = [r[0] * (od[0] + ev[0]), r[1] * (od[1] + ev[1]), r[2] * g2, r[3] * (od[1] - ev[1]), r[4] * (od[0] - ev[0])]
    return total([(E[0, b], q[b]) for b in range(5)])


def open_terms(v, r):
    flux = [r[b] * total([(D[b, a], v[a]) for a in range(4)]) for b in range(4)]
    part = total([(E[4, b], flux[b]) for b in range(4)])
    grad = total([(D[4, a], v[a]) for a in range(4)])
    return part, grad


def open_scale(r):
    return total([(E[4, b] * D[b, 4], r[b]) for b in range(4)])


def rolled(x, shift):
    shift = shift % NZL
    return x if shift == 0 else pltpu.roll(x, shift, 1)


def lane_of():
    return lax.broadcasted_iota(jnp.int32, (8, NZL), 1)


def lane_table(phase, values):
    out = jnp.full((8, NZL), np.float32(values[0]), F32)
    for b in range(1, 4):
        out = jnp.where(phase == b, np.float32(values[b]), out)
    return out


def x_rows(x, half):
    return pl.ds(x * NYL + half * 8, 8)


def y_rows(y):
    return pl.ds(y, 8, stride=NYL)


def first_lanes(read, read_r, lane):
    out = jnp.zeros((8, NZL), F32)
    for k in range(16):
        rows = pl.ds(8 * k, 8)
        for c in range(3 if read_r is None else 4):
            src = read_r(rows) if c == 3 else read(c, rows)
            out = jnp.where(lane == 4 * k + c, rolled(src, 4 * k + c), out)
    return out


def last_lanes(read, lane):
    out = jnp.zeros((8, NZL), F32)
    for k in range(16):
        out = jnp.where((lane >> 2) == k, rolled(read(pl.ds(8 * k, 8)), 4 * k + 4), out)
    return out


def interleaved(parts, lane, base):
    out = jnp.zeros((8, NZL), F32)
    for j, part in enumerate(parts):
        if part is None:
            continue
        out = jnp.where((lane >= base) & (lane < base + 64) & ((lane & 3) == j), rolled(part, base + j - 3), out)
    return out


def widen(src, dst):
    for x in range(NXL):
        dst[pl.ds(x * NYL, NYL), :] = src[pl.ds(x * NYL, NYL), :].astype(F32)


X_UP, X_DOWN = 112, 64
Y_UP, Y_DOWN = 136, 64


def place():
    return tuple(lax.axis_index(axis) for axis in ("normal", "strike", "depth"))


def paired(index, up, down, near, far):
    even = (index & 1) == 0
    rows = pl.ds(0, down.shape[0])
    near[...] = up[...]
    far[...] = up[...]
    near[rows, :] = jnp.where(even, up[rows, :], down[...])
    far[rows, :] = jnp.where(even, down[...], up[rows, :])


def unpaired(index, near, far, low, high):
    even = (index & 1) == 0
    rows = pl.ds(0, high.shape[0])
    low[...] = jnp.where(even, far[...], near[...])
    high[...] = jnp.where(even, near[rows, :], far[rows, :])


def beside(index, count, got, low, high):
    below = pl.multiple_of((jnp.maximum(index - 1, 0)) * 8, 8)
    above = pl.multiple_of((jnp.minimum(index + 1, count - 1)) * 8, 8)
    low[...] = jnp.where(index > 0, got[pl.ds(below, low.shape[0]), :], 0.0)
    high[...] = jnp.where(index < count - 1, got[pl.ds(above, high.shape[0]), :], 0.0)


Y_SPLIT, Y_PAIRS = (0, 1, 2, 3, 4, 5, 12), ((6, 7), (8, 9), (10, 11), (13, 14), (15, 16))
Y_TILES = len(Y_SPLIT) + len(Y_PAIRS)


def plane_of(ref, n):
    return ref[pl.ds(8 * n, 8), :]


def in_parts(value):
    return jnp.concatenate([value, value - value.astype(jnp.bfloat16).astype(F32)], axis=0)


def y_pack(index, up, down, near, far):
    even = (index & 1) == 0
    ups = [in_parts(plane_of(up, n)) for n in Y_SPLIT]
    ups += [jnp.concatenate([plane_of(up, a), plane_of(up, b)], axis=0) for a, b in Y_PAIRS]
    for t, above in enumerate(ups):
        below = in_parts(plane_of(down, t)) if t < Y_DOWN // 8 else above
        rows = pl.ds(16 * t, 16)
        near[rows, :] = jnp.where(even, above, below).astype(jnp.bfloat16)
        far[rows, :] = jnp.where(even, below, above).astype(jnp.bfloat16)


def y_unpack(index, near, far, low, high):
    even = (index & 1) == 0
    for t in range(Y_TILES):
        rows = pl.ds(16 * t, 16)
        from_near, from_far = near[rows, :].astype(F32), far[rows, :].astype(F32)
        below, above = jnp.where(even, from_far, from_near), jnp.where(even, from_near, from_far)
        if t < Y_DOWN // 8:
            high[pl.ds(8 * t, 8), :] = above[:8, :] + above[8:, :]
        if t < len(Y_SPLIT):
            low[pl.ds(8 * Y_SPLIT[t], 8), :] = below[:8, :] + below[8:, :]
        else:
            for part, n in enumerate(Y_PAIRS[t - len(Y_SPLIT)]):
                low[pl.ds(8 * n, 8), :] = below[8 * part : 8 * part + 8, :]


def pack_kernel(
    now_hbm, prev_hbm, rig_hbm, rho_hbm, nodes_hbm, ids_hbm,
    xa, xb, za, zb, zd, tails, rw, now, prev, rho, nodes, ids,
    rig, xu, xd, zu, sems,
):
    pairs = (
        (rig_hbm, rig), (now_hbm, now), (prev_hbm, prev), (rho_hbm, rho), (nodes_hbm, nodes), (ids_hbm, ids),
    )
    copies = [pltpu.make_async_copy(src, dst, sems.at[i]) for i, (src, dst) in enumerate(pairs)]
    for copy in copies:
        copy.start()
    for copy in copies[:2]:
        copy.wait()
    widen(rig, rw)
    lane = lane_of()
    for half in range(2):
        r = [rw[x_rows(4 + a, half), :] for a in range(4)]
        xu[pl.ds(96 + 8 * half, 8), :] = open_scale(r)
        xd[pl.ds(48 + 8 * half, 8), :] = rw[x_rows(0, half), :]
        for c in range(3):
            part, grad = open_terms([now[c, x_rows(4 + a, half), :] for a in range(4)], r)
            xu[pl.ds(16 * c + 8 * half, 8), :] = part
            xu[pl.ds(48 + 16 * c + 8 * half, 8), :] = grad
            xd[pl.ds(16 * c + 8 * half, 8), :] = now[c, x_rows(0, half), :]
    back = lambda t: [rolled(t, 3 - a) for a in range(4)]
    tails[pl.ds(24, 8), :] = last_lanes(lambda rows: rw[rows, :], lane)
    r = back(tails[pl.ds(24, 8), :])
    parts, grads = [], []
    for c in range(3):
        tails[pl.ds(8 * c, 8), :] = last_lanes(lambda rows: now[c, rows, :], lane)
        part, grad = open_terms(back(tails[pl.ds(8 * c, 8), :]), r)
        parts.append(part)
        grads.append(grad)
    zu[...] = jnp.where(
        lane < 64, interleaved(parts + [open_scale(r)], lane, 0), interleaved(grads + [None], lane, 64)
    )
    zd[...] = first_lanes(lambda c, rows: now[c, rows, :], lambda rows: rw[rows, :], lane)
    index = place()
    paired(index[0], xu, xd, xa, xb)
    paired(index[2], zu, zd, za, zb)
    for copy in copies[2:]:
        copy.wait()


def advance(now, prev, rw, low, high_v, high_r, scale, ghost_z, ghost_rz, closing_z, index, store, acc, on_first, on_end=None):
    index_x, index_y, index_z = index
    at_x = jnp.where(index_x == 0, 2.0, 1.0).astype(F32)
    at_y = jnp.where(index_y == 0, 2.0, 1.0).astype(F32)
    at_z = jnp.where(index_z == 0, 2.0, 1.0).astype(F32)

    def along_y(c, carry):
        none = jnp.zeros((8, NZL), F32)
        v = [now[c, y_rows(y), :] for y in range(NYL)] + [high_v[1][pl.ds(8 * c, 8), :] if high_v[1] is not None else none]
        r = [rw[y_rows(y), :] for y in range(NYL)] + [high_r[1][...] if high_r[1] is not None else none]
        carried = low[1](c, v[0]) if low[1] is not None else none
        for e in range(4):
            terms = element(v[4 * e : 4 * e + 5], r[4 * e : 4 * e + 5])
            head = terms[0] * at_y if e == 0 else terms[0]
            acc[c, y_rows(4 * e), :] = head + carried
            for a in range(1, 4):
                acc[c, y_rows(4 * e + a), :] = terms[a]
            carried = terms[4]
        return carry

    lax.fori_loop(0, 3, along_y, 0)
    alone = ghost_z is None

    lane = lane_of()
    phase = lane & 3
    gm = [lane_table(phase, [D[b, b - k] if b >= k else 0 for b in range(4)]) for k in range(4)]
    gp = [None] + [lane_table(phase, [D[b, b + k] if b + k <= 4 else 0 for b in range(4)]) for k in range(1, 5)]
    cm = [lane_table(phase, [E[a, a - k] if a >= k else 0 for a in range(4)]) for k in range(4)]
    cp = [None] + [lane_table(phase, [E[a, a + k] if a + k <= 3 else 0 for a in range(4)]) for k in range(1, 4)]
    c_close = lane_table(phase, [E[a, 4] for a in range(4)])
    last = [lane_table(phase, [0, 0, 0, E[4, b]]) for b in range(5)]
    first = lane == 0
    edge = jnp.where(first, at_z, jnp.float32(1.0))

    def along_xz(n, carry):
        c, half = n >> 1, n & 1
        offset = half * 8
        rows = [pl.ds(pl.multiple_of(x * NYL + offset, 8), 8) for x in range(NXL)]
        plane = pl.ds(pl.multiple_of(16 * c + offset, 8), 8)
        none = jnp.zeros((8, NZL), F32)
        v = [now[c, rows[x], :] for x in range(NXL)] + [none if alone else high_v[0][plane, :]]
        r = [rw[rows[x], :] for x in range(NXL)]
        r.append(none if alone else high_r[0][pl.ds(pl.multiple_of(offset, 8), 8), :])
        carried = none if alone else low[0](c, offset, plane, v[0])
        back = NZL - (4 * half + c)
        ghost_v = 0.0 if alone else pltpu.roll(ghost_z, back, 1)
        ghost_r = 0.0 if alone else pltpu.roll(ghost_rz, NZL - 4 * half, 1)
        closing = 0.0 if alone else pltpu.roll(closing_z, back, 1)
        for e in range(2):
            terms = element(v[4 * e : 4 * e + 5], r[4 * e : 4 * e + 5])
            if e == 0:
                on_first(c, plane, carried, terms[0])
            for a in range(4):
                x = 4 * e + a
                force = terms[a] + acc[c, rows[x], :]
                if a == 0:
                    force = (terms[0] * at_x if e == 0 else terms[0]) + carried + acc[c, rows[x], :]
                vx = jnp.where(first, ghost_v if alone else rolled(ghost_v, -8 * x), v[x])
                rx = jnp.where(first, ghost_r if alone else rolled(ghost_r, -8 * x), r[x])
                vm = [v[x]] + [rolled(v[x], k) for k in range(1, 4)]
                vp = [None] + [rolled(vx, -k) for k in range(1, 5)]
                g = gm[0] * v[x]
                for k in range(1, 4):
                    g = g + gm[k] * vm[k]
                for k in range(1, 5):
                    g = g + gp[k] * vp[k]
                g4 = total([(D[4, 0], vm[3]), (D[4, 1], vm[2]), (D[4, 2], vm[1]), (D[4, 3], vm[0]), (D[4, 4], vp[1])])
                q = r[x] * g
                q4 = jnp.where(phase == 3, rolled(rx, -1) * g4, 0.0)
                qm = [q] + [rolled(q, k) for k in range(1, 4)]
                own = cm[0] * q
                for k in range(1, 4):
                    own = own + cm[k] * qm[k]
                for k in range(1, 4):
                    own = own + cp[k] * rolled(q, -k)
                pair = q4 + rolled(q4, -1)
                own = own + c_close * (pair + rolled(pair, -2))
                tail = last[3] * q + last[4] * q4
                for b in range(3):
                    tail = tail + last[b] * qm[3 - b]
                tail = jnp.where(first, closing if alone else rolled(closing, -8 * x), rolled(tail, 1))
                force = force + own * edge + tail
                after = (v[x] + v[x]) - prev[c, rows[x], :] - scale[rows[x], :] * force
                store(c, x, rows[x], plane, after)
            carried = terms[4]
        if on_end is not None:
            on_end(c, half)
        return carry

    lax.fori_loop(0, 6, along_xz, 0)


def step_scale(rho, scale):
    for x in range(NXL):
        rows = pl.ds(x * NYL, NYL)
        scale[rows, :] = np.float32(DT * DT) / rho[rows, :].astype(F32)


def axis_weight(pos, is_first):
    phase = pos & 3
    out = jnp.full(pos.shape, np.float32(2 * W0), F32)
    for b in range(1, 4):
        out = jnp.where(phase == b, np.float32(WQ[b]), out)
    return jnp.where((pos == 0) & is_first, np.float32(W0), out)


def inner_kernel(now, prev, rw, rho, base, term, scale, acc):
    step_scale(rho, scale)

    def store(c, x, rows, plane, after):
        base[c, rows, :] = after

    def on_first(c, plane, carried, own):
        term[plane, :] = own

    nothing = (None, None)
    advance(now, prev, rw, nothing, nothing, nothing, scale, None, None, None, place(), store, acc, on_first)


def spread_from(tile, lane, source):
    phase = lane & 3
    out = tile
    for j in range(4):
        if j != source:
            out = jnp.where(phase == j, rolled(tile, j - source), out)
    return out


def edge_kernel(
    counts, inner, now, rw, scale, term, tails, xa, xb, za, zb, zd_own,
    base, yb, ya, early, mx, mz, xd, zd,
    xu, zu, yu, yd,
):
    index = place()
    unpaired(index[0], xa, xb, xu, xd)
    unpaired(index[2], za, zb, zu, zd)
    lane = lane_of()
    phase = lane & 3
    has_x, has_z = (index[0] > 0).astype(F32), (index[2] > 0).astype(F32)
    kappa, diagonal, d44 = np.float32(KAPPA), np.float32(KAPPA * D[4, 4]), np.float32(D[4, 4])

    own, above, below = zd_own[...], zu[...], zd[...]
    r_first = spread_from(own, lane, 3)
    gain = (spread_from(above, lane, 3) + diagonal * r_first) * has_z
    mz[...] = gain
    s_first = jnp.zeros((8, NZL), F32)
    for k in range(16):
        s_first = jnp.where(lane == 4 * k, rolled(scale[pl.ds(8 * k, 8), :], 4 * k), s_first)
    closing = spread_from(s_first, lane, 0) * (above + kappa * r_first * rolled(above, 64) + gain * own)
    r_tail = tails[pl.ds(24, 8), :]
    s_tail = last_lanes(lambda rows: scale[rows, :], lane)
    weights = [
        lane_table(phase, [E[a, a + k] * D[a + k, 4] if 0 <= a + k <= 3 else 0 for a in range(4)]) for k in range(-3, 4)
    ]
    by_value = s_tail * sum(w * rolled(r_tail, -k) for w, k in zip(weights, range(-3, 4)))
    by_flux = s_tail * lane_table(phase, [E[a, 4] for a in range(4)])
    r_below = spread_from(below, lane, 3)
    last = lane >= NZL - 4
    for c in range(3):
        tail = tails[pl.ds(8 * c, 8), :]
        grad = spread_from(total([(D[4, a], rolled(tail, 3 - a)) for a in range(4)]), lane, 3)
        value = spread_from(below, lane, c)
        taken = by_value * value + by_flux * (r_below * (grad + d44 * value))
        for k in range(16):
            rows = pl.ds(8 * k, 8)
            off = jnp.where(lane == 0, rolled(closing, -(4 * k + c)), 0.0)
            base[c, rows, :] = inner[c, rows, :] - jnp.where(last, rolled(taken, NZL - 4 - 4 * k), off)

    for half in range(2):
        rows = pl.ds(8 * half, 8)
        r = [rw[x_rows(4 + a, half), :] for a in range(4)]
        by_value, by_flux = open_response([scale[x_rows(4 + a, half), :] for a in range(4)], r)
        r0, r8 = rw[x_rows(0, half), :], xd[pl.ds(48 + 8 * half, 8), :]
        gain = (xu[pl.ds(96 + 8 * half, 8), :] + diagonal * r0) * has_x
        mx[rows, :] = gain
        for c in range(3):
            plane = pl.ds(16 * c + 8 * half, 8)
            grad = xu[pl.ds(48 + 16 * c + 8 * half, 8), :]
            carried = xu[plane, :] + kappa * r0 * grad + gain * now[c, x_rows(0, half), :]
            early[plane, :] = carried - term[plane, :]
            base[c, x_rows(0, half), :] = base[c, x_rows(0, half), :] - scale[x_rows(0, half), :] * carried
            value = xd[plane, :]
            flux = r8 * (total([(D[4, a], now[c, x_rows(4 + a, half), :]) for a in range(4)]) + d44 * value)
            for a in range(4):
                at = x_rows(4 + a, half)
                base[c, at, :] = base[c, at, :] - by_value[a] * value - by_flux[a] * flux

    r = [rw[y_rows(12 + a), :] for a in range(4)]
    by_value, by_flux = open_response([scale[y_rows(12 + a), :] for a in range(4)], r)
    planes = [open_scale(r), *open_terms(by_value, r), *open_terms(by_flux, r)]
    for n, plane in enumerate(planes):
        yu[pl.ds(96 + 8 * n, 8), :] = plane
    for c in range(3):
        planes = open_terms([now[c, y_rows(12 + a), :] for a in range(4)], r)
        planes += open_terms([base[c, y_rows(12 + a), :] for a in range(4)], r)
        for n, plane in enumerate(planes):
            yu[pl.ds(24 * n + 8 * c, 8), :] = plane
        yd[pl.ds(8 * c, 8), :] = now[c, y_rows(0), :]
        yd[pl.ds(24 + 8 * c, 8), :] = base[c, y_rows(0), :]
    yd[pl.ds(48, 8), :] = rw[y_rows(0), :]
    yd[pl.ds(56, 8), :] = scale[y_rows(0), :]
    y_pack(index[1], yu, yd, ya, yb)


def open_response(scale, r):
    by_value = [scale[a] * total([(E[a, b] * D[b, 4], r[b]) for b in range(4)]) for a in range(4)]
    by_flux = [scale[a] * np.float32(E[a, 4]) for a in range(4)]
    return by_value, by_flux


def whole_kernel(
    counts, base, now, rw, scale, early, yb, ya, mx, xd, zd, nodes, ids,
    out, to_depth, xa2, xb2, zd2, my, y_low, y_high, r_high,
    slip, yu, yd, xu2, xd2, zu2,
):
    middle = counts[0] // 2
    index = place()
    lane = lane_of()
    kappa, diagonal = np.float32(KAPPA), np.float32(KAPPA * D[4, 4])
    d44 = np.float32(D[4, 4])
    y_unpack(index[1], ya, yb, yu, yd)
    for c in range(3):
        for k in range(16):
            rows = pl.ds(8 * k, 8)
            out[c, rows, :] = base[c, rows, :]
    r = [rw[y_rows(12 + a), :] for a in range(4)]
    by_value, by_flux = open_response([scale[y_rows(12 + a), :] for a in range(4)], r)
    own_scale = open_scale(r)
    r0, s0 = rw[y_rows(0), :], scale[y_rows(0), :]
    r_above, s_above = yd[pl.ds(48, 8), :], yd[pl.ds(56, 8), :]
    r_high[...] = r_above
    gain, value_part, value_grad, flux_part, flux_grad = (yu[pl.ds(96 + 8 * n, 8), :] for n in range(5))
    gain = (gain + diagonal * r0) * (index[1] > 0).astype(F32)
    my[...] = gain
    for c in range(3):
        plane = pl.ds(8 * c, 8)
        part, grad, part2, grad2 = (yu[pl.ds(24 * n + 8 * c, 8), :] for n in range(4))
        v0 = now[c, y_rows(0), :]
        after = base[c, y_rows(0), :] - s0 * (part + kappa * r0 * grad + gain * v0)
        out[c, y_rows(0), :] = after
        flux = r0 * (grad + d44 * v0)
        y_low[plane, :] = (part2 - value_part * v0 - flux_part * flux) + kappa * r0 * (
            grad2 - value_grad * v0 - flux_grad * flux
        )
        above = yd[plane, :]
        part, grad = open_terms([now[c, y_rows(12 + a), :] for a in range(4)], r)
        flux = r_above * (grad + d44 * above)
        y_high[plane, :] = yd[pl.ds(24 + 8 * c, 8), :] - s_above * (part + own_scale * above + kappa * flux)
        for a in range(4):
            after = base[c, y_rows(12 + a), :] - by_value[a] * above - by_flux[a] * flux
            out[c, y_rows(12 + a), :] = after

    on_one, on_two = index[0] == middle - 1, index[0] == middle
    for half in range(2):
        rows = pl.ds(8 * half, 8)
        r = [rw[x_rows(x, half), :] for x in range(8)] + [xd[pl.ds(48 + 8 * half, 8), :]]
        y_pos = lax.broadcasted_iota(jnp.int32, (8, NZL), 0) + 8 * half
        face = axis_weight(y_pos, index[1] == 0) * axis_weight(lane, index[2] == 0) * np.float32(W0)
        for c in range(3):
            plane = pl.ds(16 * c + 8 * half, 8)
            v = [out[c, x_rows(x, half), :] for x in range(8)]
            part, grad = open_terms(v[4:], r[4:8])
            sent = part + kappa * r[8] * grad
            xu2[plane, :] = sent
            xd2[plane, :] = v[0]
            here = early[plane, :] + mx[rows, :] * v[0] - first_term(v[:5], r[:5])
            slip[plane, :] = face * jnp.where(on_one, sent, jnp.where(on_two, here, 0.0))
    back = lambda t: [rolled(t, 3 - a) for a in range(4)]
    r = back(last_lanes(lambda rows: rw[rows, :], lane))
    sent = []
    for c in range(3):
        part, grad = open_terms(back(last_lanes(lambda rows: out[c, rows, :], lane)), r)
        sent.append(part + kappa * zd[...] * grad)
    zu2[...] = interleaved(sent + [None], lane, 0)
    zd2[...] = first_lanes(lambda c, rows: out[c, rows, :], None, lane)
    paired(index[0], xu2, xd2, xa2, xb2)
    tile = patch_tile(counts[2], slip[...], nodes[...], ids[...])
    for d in range(counts[2]):
        halo = jnp.where(d > index[2], zu2[...], zd2[...])
        to_depth[pl.ds(8 * d, 8), :] = with_row(halo, tile[d : d + 1, :], lane)


def with_row(halo, row, lane):
    sub = lax.broadcasted_iota(jnp.int32, (8, NZL), 0)
    row = jnp.broadcast_to(row, (8, NZL))
    spread = jnp.where(sub == 0, rolled(row, 64), jnp.where(sub == 1, row, 0.0))
    return jnp.where(lane < 64, halo, spread)


def sum_kernel(counts, got, to_face):
    summed = got[pl.ds(0, 8), :]
    for d in range(1, counts[2]):
        summed = summed + got[pl.ds(8 * d, 8), :]
    low = jnp.broadcast_to(rolled(summed, 64)[0:1, :], (8, NZL))
    high = jnp.broadcast_to(summed[1:2, :], (8, NZL))
    row = jnp.where(lane_of() < 64, low, high)
    for k in range(counts[0] * counts[1] // 8):
        to_face[pl.ds(8 * k, 8), :] = row


def second_kernel(
    counts, now, prev, rw, scale, xa2, xb2, got_z, zd2_own, mx, my, mz, xd, zd, y_low, y_high, r_high,
    out_hbm, mid_hbm, out, acc, xu2, xd2, zu2, zd2, sems,
):
    index = place()
    copies = [pltpu.make_async_copy(out.at[c], out_hbm.at[c], sems.at[c]) for c in range(3)]
    copies.append(pltpu.make_async_copy(now, mid_hbm, sems.at[3]))
    copies[3].start()
    unpaired(index[0], xa2, xb2, xu2, xd2)
    beside(index[2], counts[2], got_z, zu2, zd2)
    closing_z = zu2[...] + mz[...] * zd2_own[...]

    def low_x(c, offset, plane, v0):
        return xu2[plane, :] + mx[pl.ds(pl.multiple_of(offset, 8), 8), :] * v0

    def low_y(c, v0):
        return y_low[pl.ds(pl.multiple_of(8 * c, 8), 8), :] + my[...] * v0

    def store(c, x, rows, plane, after):
        out[c, rows, :] = after

    def sent(c, half):
        @pl.when(half == 1)
        def _():
            pltpu.make_async_copy(out.at[c], out_hbm.at[c], sems.at[c]).start()

    advance(
        now, prev, rw, (low_x, low_y), (xd2, y_high), (xd.at[pl.ds(48, 16)], r_high), scale,
        zd2[...], rolled(zd[...], -3), closing_z, index, store, acc, lambda *args: None, sent,
    )
    for copy in copies:
        copy.wait()


def patch_tile(count_d, slip, node, patch):
    pairs = node.shape[-1]
    hot_z = (lax.broadcasted_iota(jnp.int32, (NZL, pairs), 0) == (node & (NZL - 1))).astype(F32)
    at_z = jnp.dot(slip, hot_z, precision=HIGHEST, preferred_element_type=F32)
    row_y = lax.broadcasted_iota(jnp.int32, (NYL, pairs), 0) == (node >> 7)
    owner = patch >> 1
    owner_d = owner & (count_d - 1)
    slot = ((owner >> (count_d.bit_length() - 1)) << 1) + (patch & 1)
    hot_slot = lax.broadcasted_iota(jnp.int32, (32, pairs), 0) == slot
    spread = []
    for c in range(3):
        picked = jnp.sum(jnp.where(row_y, at_z[NYL * c : NYL * (c + 1), :], 0.0), axis=0, keepdims=True)
        spread.append(jnp.where(hot_slot, picked, 0.0))
    spread.append(jnp.zeros((32, pairs), F32))
    hot_d = (lax.broadcasted_iota(jnp.int32, (8, pairs), 0) == owner_d).astype(F32)
    return lax.dot_general(
        hot_d, jnp.concatenate(spread, axis=0), (((1,), (1,)), ((), ())), precision=HIGHEST,
        preferred_element_type=F32,
    )


def final_kernel(tiles, out):
    mine = lax.axis_index("strike") * 2
    summed = jnp.sum(tiles[...], axis=0, keepdims=True)
    lane = lax.broadcasted_iota(jnp.int32, (2, NZL), 1)
    place = lax.broadcasted_iota(jnp.int32, (2, NZL), 0)
    for c in range(3):
        hit = lane == 32 * c + mine + place
        out[:, pl.ds(c, 1)] = jnp.sum(jnp.where(hit, summed, 0.0), axis=1, keepdims=True)


def call(kernel, name, outs, scratch=(), flops=0, moved=0, **specs):
    return pl.pallas_call(
        kernel,
        out_shape=[jax.ShapeDtypeStruct(o, F32) if isinstance(o, tuple) else jax.ShapeDtypeStruct(o.shape, o.dtype) for o in outs],
        scratch_shapes=[pltpu.VMEM(shape, F32) if isinstance(shape, tuple) else shape for shape in scratch],
        compiler_params=pltpu.CompilerParams(vmem_limit_bytes=16 * 2**20),
        cost_estimate=pl.CostEstimate(flops=flops, bytes_accessed=moved, transcendentals=0),
        name=name,
        **specs,
    )


def swap_near(value, axis):
    return lax.ppermute(value, axis, [(i, i ^ 1) for i in range(lax.axis_size(axis))])


def swap_far(value, axis):
    lower = range(1, lax.axis_size(axis) - 1, 2)
    return lax.ppermute(value, axis, [(i, i + 1) for i in lower] + [(i + 1, i) for i in lower])


def local(field_now, field_prev, rigidity, density, fault_nodes, patch_ids):
    axes = ("normal", "strike", "depth")
    counts = tuple(lax.axis_size(a) for a in axes)
    flat, block, tile = (3, ROWS, NZL), (ROWS, NZL), (8, NZL)
    now, prev = field_now.reshape(flat), field_prev.reshape(flat)
    rig, rho = rigidity.reshape(block), density.reshape(block)
    nodes, ids = fault_nodes.reshape(1, -1), patch_ids.reshape(1, -1)
    x_up, x_down, y_up, y_down = ((n, NZL) for n in (X_UP, X_DOWN, Y_UP, Y_DOWN))
    faces, strip = (48, NZL), (24, NZL)
    y_sent = jax.ShapeDtypeStruct((16 * Y_TILES, NZL), jnp.bfloat16)
    xa, xb, za, zb, zd_own, tails, rw, now, prev, rho, nodes, ids = call(
        pack_kernel, "pack",
        [x_up, x_up, tile, tile, tile, (32, NZL), block, flat, flat, rho, nodes, ids],
        [pltpu.VMEM(block, jnp.bfloat16), x_up, x_down, tile, pltpu.SemaphoreType.DMA((6,))],
        flops=2_000_000, moved=900_000, in_specs=[pl.BlockSpec(memory_space=pltpu.HBM)] * 6,
    )(*(pltpu.with_memory_space_constraint(x, pltpu.HBM) for x in (now, prev, rig, rho, nodes, ids)))
    xa, xb = swap_near(xa, "normal"), swap_far(xb, "normal")
    zb, za = swap_far(zb, "depth"), swap_near(za, "depth")
    inner, term, scale = call(
        inner_kernel, "inner", [flat, faces, block], [flat], flops=10_000_000, moved=900_000,
    )(now, prev, rw, rho)
    base, yb, ya, early, mx, mz, xd, zd = call(
        functools.partial(edge_kernel, counts), "edge",
        [flat, y_sent, y_sent, faces, (16, NZL), tile, x_down, tile],
        [x_up, tile, y_up, y_down], flops=2_000_000, moved=900_000,
    )(inner, now, rw, scale, term, tails, xa, xb, za, zb, zd_own)
    yb, ya = swap_far(yb, "strike"), swap_near(ya, "strike")
    kept, to_depth, xa2, xb2, zd2, my, y_low, y_high, r_high = call(
        functools.partial(whole_kernel, counts), "whole",
        [flat, (8 * counts[2], NZL), faces, faces, tile, tile, strip, strip, tile],
        [faces, y_up, y_down, faces, faces, tile], flops=2_000_000, moved=900_000,
    )(base, now, rw, scale, early, yb, ya, mx, xd, zd, nodes, ids)
    got_z = lax.all_to_all(to_depth, "depth", 0, 0, tiled=True)
    (to_face,) = call(
        functools.partial(sum_kernel, counts), "add", [(counts[0] * counts[1], NZL)], flops=10_000, moved=80_000,
    )(got_z)
    got_face = lax.all_to_all(to_face, ("normal", "strike"), 0, 0, tiled=True)
    xa2, xb2 = swap_near(xa2, "normal"), swap_far(xb2, "normal")
    (share,) = call(final_kernel, "final", [(2, 3)], flops=10_000, moved=10_000)(got_face)
    following, mid = call(
        functools.partial(second_kernel, counts), "second", [flat, flat],
        [flat, flat, faces, faces, tile, tile, pltpu.SemaphoreType.DMA((4,))],
        flops=10_000_000, moved=900_000, out_specs=[pl.BlockSpec(memory_space=pltpu.HBM)] * 2,
    )(kept, now, rw, scale, xa2, xb2, got_z, zd2, mx, my, mz, xd, zd, y_low, y_high, r_high)
    return following.reshape(field_now.shape), mid.reshape(field_now.shape), share


def solution(mesh):
    field = P(None, "normal", "strike", "depth")
    cells = P("normal", "strike", "depth")
    pairs = P("strike", "depth", None)
    return jax.shard_map(
        local,
        mesh=mesh,
        in_specs=(field, field, cells, cells, pairs, pairs),
        out_specs=(field, field, P(("strike", "depth"), None)),
        check_vma=False,
    )
```

```python
import functools
import math

import jax
import jax.numpy as jnp
import numpy as np
from jax import lax
from jax.experimental import pallas as pl
from jax.experimental.pallas import tpu as pltpu
from jax.sharding import PartitionSpec as P

DT = 0.03
NXL, NYL, NZL = 8, 16, 128
ROWS = NXL * NYL
F32 = jnp.float32
HIGHEST = lax.Precision.HIGHEST


def gll_tables():
    spread = math.sqrt(3.0 / 7.0)
    points = np.array([-1.0, -spread, 0.0, spread, 1.0])
    weights = np.array([0.1, 49.0 / 90.0, 32.0 / 45.0, 49.0 / 90.0, 0.1]) * 0.5
    derivative = np.zeros((5, 5))
    for b in range(5):
        for a in range(5):
            if a == b:
                derivative[b, a] = sum(1.0 / (points[b] - points[o]) for o in range(5) if o != b)
            else:
                row = np.prod([points[b] - points[o] for o in range(5) if o != b and o != a])
                col = np.prod([points[a] - points[o] for o in range(5) if o != a and o != b])
                derivative[b, a] = row / (col * (points[a] - points[b]))
    return weights, 2.0 * derivative


WQ, D = gll_tables()
W0 = float(WQ[0])
NODE_W = np.array([2 * WQ[0], WQ[1], WQ[2], WQ[3], 2 * WQ[0]])
E = (WQ[:, None] * D).T / NODE_W[:, None]
KAPPA = float(E[4, 4])


def total(pairs):
    acc = None
    for const, arr in pairs:
        if abs(const) < 1e-12:
            continue
        term = arr * np.float32(const)
        acc = term if acc is None else acc + term
    return acc


def element(v, r):
    twice = v[2] + v[2]
    s0, s1 = v[0] + v[4] - twice, v[1] + v[3] - twice
    d0, d1 = v[0] - v[4], v[1] - v[3]
    ev = [total([((D[b, 0] + D[b, 4]) / 2, s0), ((D[b, 1] + D[b, 3]) / 2, s1)]) for b in (0, 1)]
    od = [total([((D[b, 0] - D[b, 4]) / 2, d0), ((D[b, 1] - D[b, 3]) / 2, d1)]) for b in (0, 1)]
    g2 = total([(D[2, 0], d0), (D[2, 1], d1)])
    q = [r[0] * (od[0] + ev[0]), r[1] * (od[1] + ev[1]), r[2] * g2, r[3] * (od[1] - ev[1]), r[4] * (od[0] - ev[0])]
    p0, m0, p1, m1 = q[0] + q[4], q[0] - q[4], q[1] + q[3], q[1] - q[3]
    ec = [total([((E[a, 0] + E[a, 4]) / 2, p0), ((E[a, 1] + E[a, 3]) / 2, p1), (E[a, 2], q[2])]) for a in (0, 1)]
    oc = [total([((E[a, 0] - E[a, 4]) / 2, m0), ((E[a, 1] - E[a, 3]) / 2, m1)]) for a in (0, 1)]
    c2 = total([(E[2, 0], m0), (E[2, 1], m1)])
    return [oc[0] + ec[0], oc[1] + ec[1], c2, oc[1] - ec[1], oc[0] - ec[0]]


def first_term(v, r):
    twice = v[2] + v[2]
    s0, s1 = v[0] + v[4] - twice, v[1] + v[3] - twice
    d0, d1 = v[0] - v[4], v[1] - v[3]
    ev = [total([((D[b, 0] + D[b, 4]) / 2, s0), ((D[b, 1] + D[b, 3]) / 2, s1)]) for b in (0, 1)]
    od = [total([((D[b, 0] - D[b, 4]) / 2, d0), ((D[b, 1] - D[b, 3]) / 2, d1)]) for b in (0, 1)]
    g2 = total([(D[2, 0], d0), (D[2, 1], d1)])
    q = [r[0] * (od[0] + ev[0]), r[1] * (od[1] + ev[1]), r[2] * g2, r[3] * (od[1] - ev[1]), r[4] * (od[0] - ev[0])]
    return total([(E[0, b], q[b]) for b in range(5)])


def open_terms(v, r):
    flux = [r[b] * total([(D[b, a], v[a]) for a in range(4)]) for b in range(4)]
    part = total([(E[4, b], flux[b]) for b in range(4)])
    grad = total([(D[4, a], v[a]) for a in range(4)])
    return part, grad


def open_scale(r):
    return total([(E[4, b] * D[b, 4], r[b]) for b in range(4)])


def rolled(x, shift):
    shift = shift % NZL
    return x if shift == 0 else pltpu.roll(x, shift, 1)


def lane_of():
    return lax.broadcasted_iota(jnp.int32, (8, NZL), 1)


def lane_table(phase, values):
    out = jnp.full((8, NZL), np.float32(values[0]), F32)
    for b in range(1, 4):
        out = jnp.where(phase == b, np.float32(values[b]), out)
    return out


def x_rows(x, half):
    return pl.ds(x * NYL + half * 8, 8)


def y_rows(y):
    return pl.ds(y, 8, stride=NYL)


def first_lanes(read, read_r, lane):
    out = jnp.zeros((8, NZL), F32)
    for k in range(16):
        rows = pl.ds(8 * k, 8)
        for c in range(3 if read_r is None else 4):
            src = read_r(rows) if c == 3 else read(c, rows)
            out = jnp.where(lane == 4 * k + c, rolled(src, 4 * k + c), out)
    return out


def last_lanes(read, lane):
    out = jnp.zeros((8, NZL), F32)
    for k in range(16):
        out = jnp.where((lane >> 2) == k, rolled(read(pl.ds(8 * k, 8)), 4 * k + 4), out)
    return out


def interleaved(parts, lane, base):
    out = jnp.zeros((8, NZL), F32)
    for j, part in enumerate(parts):
        if part is None:
            continue
        out = jnp.where((lane >= base) & (lane < base + 64) & ((lane & 3) == j), rolled(part, base + j - 3), out)
    return out


def widen(src, dst):
    for x in range(NXL):
        dst[pl.ds(x * NYL, NYL), :] = src[pl.ds(x * NYL, NYL), :].astype(F32)


X_UP, X_DOWN = 112, 64
Y_UP, Y_DOWN = 136, 64


def place():
    return tuple(lax.axis_index(axis) for axis in ("normal", "strike", "depth"))


def paired(index, up, down, near, far):
    even = (index & 1) == 0
    rows = pl.ds(0, down.shape[0])
    near[...] = up[...]
    far[...] = up[...]
    near[rows, :] = jnp.where(even, up[rows, :], down[...])
    far[rows, :] = jnp.where(even, down[...], up[rows, :])


def unpaired(index, near, far, low, high):
    even = (index & 1) == 0
    rows = pl.ds(0, high.shape[0])
    low[...] = jnp.where(even, far[...], near[...])
    high[...] = jnp.where(even, near[rows, :], far[rows, :])


def beside(index, count, got, low, high):
    below = pl.multiple_of((jnp.maximum(index - 1, 0)) * 8, 8)
    above = pl.multiple_of((jnp.minimum(index + 1, count - 1)) * 8, 8)
    low[...] = jnp.where(index > 0, got[pl.ds(below, low.shape[0]), :], 0.0)
    high[...] = jnp.where(index < count - 1, got[pl.ds(above, high.shape[0]), :], 0.0)


Y_SPLIT, Y_PAIRS = (0, 1, 2, 3, 4, 5, 12), ((6, 7), (8, 9), (10, 11), (13, 14), (15, 16))
Y_TILES = len(Y_SPLIT) + len(Y_PAIRS)


def plane_of(ref, n):
    return ref[pl.ds(8 * n, 8), :]


def in_parts(value):
    return jnp.concatenate([value, value - value.astype(jnp.bfloat16).astype(F32)], axis=0)


def y_pack(index, up, down, near, far):
    even = (index & 1) == 0
    ups = [in_parts(plane_of(up, n)) for n in Y_SPLIT]
    ups += [jnp.concatenate([plane_of(up, a), plane_of(up, b)], axis=0) for a, b in Y_PAIRS]
    for t, above in enumerate(ups):
        below = in_parts(plane_of(down, t)) if t < Y_DOWN // 8 else above
        rows = pl.ds(16 * t, 16)
        near[rows, :] = jnp.where(even, above, below).astype(jnp.bfloat16)
        far[rows, :] = jnp.where(even, below, above).astype(jnp.bfloat16)


def y_unpack(index, near, far, low, high):
    even = (index & 1) == 0
    for t in range(Y_TILES):
        rows = pl.ds(16 * t, 16)
        from_near, from_far = near[rows, :].astype(F32), far[rows, :].astype(F32)
        below, above = jnp.where(even, from_far, from_near), jnp.where(even, from_near, from_far)
        if t < Y_DOWN // 8:
            high[pl.ds(8 * t, 8), :] = above[:8, :] + above[8:, :]
        if t < len(Y_SPLIT):
            low[pl.ds(8 * Y_SPLIT[t], 8), :] = below[:8, :] + below[8:, :]
        else:
            for part, n in enumerate(Y_PAIRS[t - len(Y_SPLIT)]):
                low[pl.ds(8 * n, 8), :] = below[8 * part : 8 * part + 8, :]


def pack_kernel(
    now_hbm, prev_hbm, rig_hbm, rho_hbm, nodes_hbm, ids_hbm,
    xa, xb, za, zb, zd, tails, rw, now, prev, rho, nodes, ids,
    rig, xu, xd, zu, sems,
):
    pairs = (
        (rig_hbm, rig), (now_hbm, now), (prev_hbm, prev), (rho_hbm, rho), (nodes_hbm, nodes), (ids_hbm, ids),
    )
    copies = [pltpu.make_async_copy(src, dst, sems.at[i]) for i, (src, dst) in enumerate(pairs)]
    for copy in copies:
        copy.start()
    for copy in copies[:2]:
        copy.wait()
    widen(rig, rw)
    lane = lane_of()
    for half in range(2):
        r = [rw[x_rows(4 + a, half), :] for a in range(4)]
        xu[pl.ds(96 + 8 * half, 8), :] = open_scale(r)
        xd[pl.ds(48 + 8 * half, 8), :] = rw[x_rows(0, half), :]
        for c in range(3):
            part, grad = open_terms([now[c, x_rows(4 + a, half), :] for a in range(4)], r)
            xu[pl.ds(16 * c + 8 * half, 8), :] = part
            xu[pl.ds(48 + 16 * c + 8 * half, 8), :] = grad
            xd[pl.ds(16 * c + 8 * half, 8), :] = now[c, x_rows(0, half), :]
    back = lambda t: [rolled(t, 3 - a) for a in range(4)]
    tails[pl.ds(24, 8), :] = last_lanes(lambda rows: rw[rows, :], lane)
    r = back(tails[pl.ds(24, 8), :])
    parts, grads = [], []
    for c in range(3):
        tails[pl.ds(8 * c, 8), :] = last_lanes(lambda rows: now[c, rows, :], lane)
        part, grad = open_terms(back(tails[pl.ds(8 * c, 8), :]), r)
        parts.append(part)
        grads.append(grad)
    zu[...] = jnp.where(
        lane < 64, interleaved(parts + [open_scale(r)], lane, 0), interleaved(grads + [None], lane, 64)
    )
    zd[...] = first_lanes(lambda c, rows: now[c, rows, :], lambda rows: rw[rows, :], lane)
    index = place()
    paired(index[0], xu, xd, xa, xb)
    paired(index[2], zu, zd, za, zb)
    for copy in copies[2:]:
        copy.wait()


def advance(now, prev, rw, low, high_v, high_r, scale, ghost_z, ghost_rz, closing_z, index, store, acc, on_first, on_end=None):
    index_x, index_y, index_z = index
    at_x = jnp.where(index_x == 0, 2.0, 1.0).astype(F32)
    at_y = jnp.where(index_y == 0, 2.0, 1.0).astype(F32)
    at_z = jnp.where(index_z == 0, 2.0, 1.0).astype(F32)

    def along_y(c, carry):
        none = jnp.zeros((8, NZL), F32)
        v = [now[c, y_rows(y), :] for y in range(NYL)] + [high_v[1][pl.ds(8 * c, 8), :] if high_v[1] is not None else none]
        r = [rw[y_rows(y), :] for y in range(NYL)] + [high_r[1][...] if high_r[1] is not None else none]
        carried = low[1](c, v[0]) if low[1] is not None else none
        for e in range(4):
            terms = element(v[4 * e : 4 * e + 5], r[4 * e : 4 * e + 5])
            head = terms[0] * at_y if e == 0 else terms[0]
            acc[c, y_rows(4 * e), :] = head + carried
            for a in range(1, 4):
                acc[c, y_rows(4 * e + a), :] = terms[a]
            carried = terms[4]
        return carry

    lax.fori_loop(0, 3, along_y, 0)
    alone = ghost_z is None

    lane = lane_of()
    phase = lane & 3
    gm = [lane_table(phase, [D[b, b - k] if b >= k else 0 for b in range(4)]) for k in range(4)]
    gp = [None] + [lane_table(phase, [D[b, b + k] if b + k <= 4 else 0 for b in range(4)]) for k in range(1, 5)]
    cm = [lane_table(phase, [E[a, a - k] if a >= k else 0 for a in range(4)]) for k in range(4)]
    cp = [None] + [lane_table(phase, [E[a, a + k] if a + k <= 3 else 0 for a in range(4)]) for k in range(1, 4)]
    c_close = lane_table(phase, [E[a, 4] for a in range(4)])
    last = [lane_table(phase, [0, 0, 0, E[4, b]]) for b in range(5)]
    first = lane == 0
    edge = jnp.where(first, at_z, jnp.float32(1.0))

    def along_xz(n, carry):
        c, half = n >> 1, n & 1
        offset = half * 8
        rows = [pl.ds(pl.multiple_of(x * NYL + offset, 8), 8) for x in range(NXL)]
        plane = pl.ds(pl.multiple_of(16 * c + offset, 8), 8)
        none = jnp.zeros((8, NZL), F32)
        v = [now[c, rows[x], :] for x in range(NXL)] + [none if alone else high_v[0][plane, :]]
        r = [rw[rows[x], :] for x in range(NXL)]
        r.append(none if alone else high_r[0][pl.ds(pl.multiple_of(offset, 8), 8), :])
        carried = none if alone else low[0](c, offset, plane, v[0])
        back = NZL - (4 * half + c)
        ghost_v = 0.0 if alone else pltpu.roll(ghost_z, back, 1)
        ghost_r = 0.0 if alone else pltpu.roll(ghost_rz, NZL - 4 * half, 1)
        closing = 0.0 if alone else pltpu.roll(closing_z, back, 1)
        for e in range(2):
            terms = element(v[4 * e : 4 * e + 5], r[4 * e : 4 * e + 5])
            if e == 0:
                on_first(c, plane, carried, terms[0])
            for a in range(4):
                x = 4 * e + a
                force = terms[a] + acc[c, rows[x], :]
                if a == 0:
                    force = (terms[0] * at_x if e == 0 else terms[0]) + carried + acc[c, rows[x], :]
                vx = jnp.where(first, ghost_v if alone else rolled(ghost_v, -8 * x), v[x])
                rx = jnp.where(first, ghost_r if alone else rolled(ghost_r, -8 * x), r[x])
                vm = [v[x]] + [rolled(v[x], k) for k in range(1, 4)]
                vp = [None] + [rolled(vx, -k) for k in range(1, 5)]
                g = gm[0] * v[x]
                for k in range(1, 4):
                    g = g + gm[k] * vm[k]
                for k in range(1, 5):
                    g = g + gp[k] * vp[k]
                g4 = total([(D[4, 0], vm[3]), (D[4, 1], vm[2]), (D[4, 2], vm[1]), (D[4, 3], vm[0]), (D[4, 4], vp[1])])
                q = r[x] * g
                q4 = jnp.where(phase == 3, rolled(rx, -1) * g4, 0.0)
                qm = [q] + [rolled(q, k) for k in range(1, 4)]
                own = cm[0] * q
                for k in range(1, 4):
                    own = own + cm[k] * qm[k]
                for k in range(1, 4):
                    own = own + cp[k] * rolled(q, -k)
                pair = q4 + rolled(q4, -1)
                own = own + c_close * (pair + rolled(pair, -2))
                tail = last[3] * q + last[4] * q4
                for b in range(3):
                    tail = tail + last[b] * qm[3 - b]
                tail = jnp.where(first, closing if alone else rolled(closing, -8 * x), rolled(tail, 1))
                force = force + own * edge + tail
                after = (v[x] + v[x]) - prev[c, rows[x], :] - scale[rows[x], :] * force
                store(c, x, rows[x], plane, after)
            carried = terms[4]
        if on_end is not None:
            on_end(c, half)
        return carry

    lax.fori_loop(0, 6, along_xz, 0)


def step_scale(rho, scale):
    for x in range(NXL):
        rows = pl.ds(x * NYL, NYL)
        scale[rows, :] = np.float32(DT * DT) / rho[rows, :].astype(F32)


def axis_weight(pos, is_first):
    phase = pos & 3
    out = jnp.full(pos.shape, np.float32(2 * W0), F32)
    for b in range(1, 4):
        out = jnp.where(phase == b, np.float32(WQ[b]), out)
    return jnp.where((pos == 0) & is_first, np.float32(W0), out)


def inner_kernel(now, prev, rw, rho, base, term, scale, acc):
    step_scale(rho, scale)

    def store(c, x, rows, plane, after):
        base[c, rows, :] = after

    def on_first(c, plane, carried, own):
        term[plane, :] = own

    nothing = (None, None)
    advance(now, prev, rw, nothing, nothing, nothing, scale, None, None, None, place(), store, acc, on_first)


def spread_from(tile, lane, source):
    phase = lane & 3
    out = tile
    for j in range(4):
        if j != source:
            out = jnp.where(phase == j, rolled(tile, j - source), out)
    return out


def edge_kernel(
    counts, inner, now, rw, scale, term, tails, xa, xb, za, zb, zd_own,
    base, yb, ya, early, mx, mz, xd, zd,
    xu, zu, yu, yd,
):
    index = place()
    unpaired(index[0], xa, xb, xu, xd)
    unpaired(index[2], za, zb, zu, zd)
    lane = lane_of()
    phase = lane & 3
    has_x, has_z = (index[0] > 0).astype(F32), (index[2] > 0).astype(F32)
    kappa, diagonal, d44 = np.float32(KAPPA), np.float32(KAPPA * D[4, 4]), np.float32(D[4, 4])

    own, above, below = zd_own[...], zu[...], zd[...]
    r_first = spread_from(own, lane, 3)
    gain = (spread_from(above, lane, 3) + diagonal * r_first) * has_z
    mz[...] = gain
    s_first = jnp.zeros((8, NZL), F32)
    for k in range(16):
        s_first = jnp.where(lane == 4 * k, rolled(scale[pl.ds(8 * k, 8), :], 4 * k), s_first)
    closing = spread_from(s_first, lane, 0) * (above + kappa * r_first * rolled(above, 64) + gain * own)
    r_tail = tails[pl.ds(24, 8), :]
    s_tail = last_lanes(lambda rows: scale[rows, :], lane)
    weights = [
        lane_table(phase, [E[a, a + k] * D[a + k, 4] if 0 <= a + k <= 3 else 0 for a in range(4)]) for k in range(-3, 4)
    ]
    by_value = s_tail * sum(w * rolled(r_tail, -k) for w, k in zip(weights, range(-3, 4)))
    by_flux = s_tail * lane_table(phase, [E[a, 4] for a in range(4)])
    r_below = spread_from(below, lane, 3)
    last = lane >= NZL - 4
    for c in range(3):
        tail = tails[pl.ds(8 * c, 8), :]
        grad = spread_from(total([(D[4, a], rolled(tail, 3 - a)) for a in range(4)]), lane, 3)
        value = spread_from(below, lane, c)
        taken = by_value * value + by_flux * (r_below * (grad + d44 * value))
        for k in range(16):
            rows = pl.ds(8 * k, 8)
            off = jnp.where(lane == 0, rolled(closing, -(4 * k + c)), 0.0)
            base[c, rows, :] = inner[c, rows, :] - jnp.where(last, rolled(taken, NZL - 4 - 4 * k), off)

    for half in range(2):
        rows = pl.ds(8 * half, 8)
        r = [rw[x_rows(4 + a, half), :] for a in range(4)]
        by_value, by_flux = open_response([scale[x_rows(4 + a, half), :] for a in range(4)], r)
        r0, r8 = rw[x_rows(0, half), :], xd[pl.ds(48 + 8 * half, 8), :]
        gain = (xu[pl.ds(96 + 8 * half, 8), :] + diagonal * r0) * has_x
        mx[rows, :] = gain
        for c in range(3):
            plane = pl.ds(16 * c + 8 * half, 8)
            grad = xu[pl.ds(48 + 16 * c + 8 * half, 8), :]
            carried = xu[plane, :] + kappa * r0 * grad + gain * now[c, x_rows(0, half), :]
            early[plane, :] = carried - term[plane, :]
            base[c, x_rows(0, half), :] = base[c, x_rows(0, half), :] - scale[x_rows(0, half), :] * carried
            value = xd[plane, :]
            flux = r8 * (total([(D[4, a], now[c, x_rows(4 + a, half), :]) for a in range(4)]) + d44 * value)
            for a in range(4):
                at = x_rows(4 + a, half)
                base[c, at, :] = base[c, at, :] - by_value[a] * value - by_flux[a] * flux

    r = [rw[y_rows(12 + a), :] for a in range(4)]
    by_value, by_flux = open_response([scale[y_rows(12 + a), :] for a in range(4)], r)
    planes = [open_scale(r), *open_terms(by_value, r), *open_terms(by_flux, r)]
    for n, plane in enumerate(planes):
        yu[pl.ds(96 + 8 * n, 8), :] = plane
    for c in range(3):
        planes = open_terms([now[c, y_rows(12 + a), :] for a in range(4)], r)
        planes += open_terms([base[c, y_rows(12 + a), :] for a in range(4)], r)
        for n, plane in enumerate(planes):
            yu[pl.ds(24 * n + 8 * c, 8), :] = plane
        yd[pl.ds(8 * c, 8), :] = now[c, y_rows(0), :]
        yd[pl.ds(24 + 8 * c, 8), :] = base[c, y_rows(0), :]
    yd[pl.ds(48, 8), :] = rw[y_rows(0), :]
    yd[pl.ds(56, 8), :] = scale[y_rows(0), :]
    y_pack(index[1], yu, yd, ya, yb)


def open_response(scale, r):
    by_value = [scale[a] * total([(E[a, b] * D[b, 4], r[b]) for b in range(4)]) for a in range(4)]
    by_flux = [scale[a] * np.float32(E[a, 4]) for a in range(4)]
    return by_value, by_flux


def whole_kernel(
    counts, base, now, rw, scale, early, yb, ya, mx, xd, zd, nodes, ids,
    out, to_depth, xa2, xb2, zd2, my, y_low, y_high, r_high,
    slip, yu, yd, xu2, xd2, zu2,
):
    middle = counts[0] // 2
    index = place()
    lane = lane_of()
    kappa, diagonal = np.float32(KAPPA), np.float32(KAPPA * D[4, 4])
    d44 = np.float32(D[4, 4])
    y_unpack(index[1], ya, yb, yu, yd)
    for c in range(3):
        for k in range(16):
            rows = pl.ds(8 * k, 8)
            out[c, rows, :] = base[c, rows, :]
    r = [rw[y_rows(12 + a), :] for a in range(4)]
    by_value, by_flux = open_response([scale[y_rows(12 + a), :] for a in range(4)], r)
    own_scale = open_scale(r)
    r0, s0 = rw[y_rows(0), :], scale[y_rows(0), :]
    r_above, s_above = yd[pl.ds(48, 8), :], yd[pl.ds(56, 8), :]
    r_high[...] = r_above
    gain, value_part, value_grad, flux_part, flux_grad = (yu[pl.ds(96 + 8 * n, 8), :] for n in range(5))
    gain = (gain + diagonal * r0) * (index[1] > 0).astype(F32)
    my[...] = gain
    for c in range(3):
        plane = pl.ds(8 * c, 8)
        part, grad, part2, grad2 = (yu[pl.ds(24 * n + 8 * c, 8), :] for n in range(4))
        v0 = now[c, y_rows(0), :]
        after = base[c, y_rows(0), :] - s0 * (part + kappa * r0 * grad + gain * v0)
        out[c, y_rows(0), :] = after
        flux = r0 * (grad + d44 * v0)
        y_low[plane, :] = (part2 - value_part * v0 - flux_part * flux) + kappa * r0 * (
            grad2 - value_grad * v0 - flux_grad * flux
        )
        above = yd[plane, :]
        part, grad = open_terms([now[c, y_rows(12 + a), :] for a in range(4)], r)
        flux = r_above * (grad + d44 * above)
        y_high[plane, :] = yd[pl.ds(24 + 8 * c, 8), :] - s_above * (part + own_scale * above + kappa * flux)
        for a in range(4):
            after = base[c, y_rows(12 + a), :] - by_value[a] * above - by_flux[a] * flux
            out[c, y_rows(12 + a), :] = after

    on_one, on_two = index[0] == middle - 1, index[0] == middle
    for half in range(2):
        rows = pl.ds(8 * half, 8)
        r = [rw[x_rows(x, half), :] for x in range(8)] + [xd[pl.ds(48 + 8 * half, 8), :]]
        y_pos = lax.broadcasted_iota(jnp.int32, (8, NZL), 0) + 8 * half
        face = axis_weight(y_pos, index[1] == 0) * axis_weight(lane, index[2] == 0) * np.float32(W0)
        for c in range(3):
            plane = pl.ds(16 * c + 8 * half, 8)
            v = [out[c, x_rows(x, half), :] for x in range(8)]
            part, grad = open_terms(v[4:], r[4:8])
            sent = part + kappa * r[8] * grad
            xu2[plane, :] = sent
            xd2[plane, :] = v[0]
            here = early[plane, :] + mx[rows, :] * v[0] - first_term(v[:5], r[:5])
            slip[plane, :] = face * jnp.where(on_one, sent, jnp.where(on_two, here, 0.0))
    back = lambda t: [rolled(t, 3 - a) for a in range(4)]
    r = back(last_lanes(lambda rows: rw[rows, :], lane))
    sent = []
    for c in range(3):
        part, grad = open_terms(back(last_lanes(lambda rows: out[c, rows, :], lane)), r)
        sent.append(part + kappa * zd[...] * grad)
    zu2[...] = interleaved(sent + [None], lane, 0)
    zd2[...] = first_lanes(lambda c, rows: out[c, rows, :], None, lane)
    paired(index[0], xu2, xd2, xa2, xb2)
    tile = patch_tile(counts[2], slip[...], nodes[...], ids[...])
    for d in range(counts[2]):
        halo = jnp.where(d > index[2], zu2[...], zd2[...])
        to_depth[pl.ds(8 * d, 8), :] = with_row(halo, tile[d : d + 1, :], lane)


def with_row(halo, row, lane):
    sub = lax.broadcasted_iota(jnp.int32, (8, NZL), 0)
    row = jnp.broadcast_to(row, (8, NZL))
    spread = jnp.where(sub == 0, rolled(row, 64), jnp.where(sub == 1, row, 0.0))
    return jnp.where(lane < 64, halo, spread)


def sum_kernel(counts, got, to_face):
    summed = got[pl.ds(0, 8), :]
    for d in range(1, counts[2]):
        summed = summed + got[pl.ds(8 * d, 8), :]
    low = jnp.broadcast_to(rolled(summed, 64)[0:1, :], (8, NZL))
    high = jnp.broadcast_to(summed[1:2, :], (8, NZL))
    row = jnp.where(lane_of() < 64, low, high)
    for k in range(counts[0] * counts[1] // 8):
        to_face[pl.ds(8 * k, 8), :] = row


def second_kernel(
    counts, now, prev, rw, scale, xa2, xb2, got_z, zd2_own, mx, my, mz, xd, zd, y_low, y_high, r_high,
    out_hbm, mid_hbm, out, acc, xu2, xd2, zu2, zd2, sems,
):
    index = place()
    copies = [pltpu.make_async_copy(out.at[c], out_hbm.at[c], sems.at[c]) for c in range(3)]
    copies.append(pltpu.make_async_copy(now, mid_hbm, sems.at[3]))
    copies[3].start()
    unpaired(index[0], xa2, xb2, xu2, xd2)
    beside(index[2], counts[2], got_z, zu2, zd2)
    closing_z = zu2[...] + mz[...] * zd2_own[...]

    def low_x(c, offset, plane, v0):
        return xu2[plane, :] + mx[pl.ds(pl.multiple_of(offset, 8), 8), :] * v0

    def low_y(c, v0):
        return y_low[pl.ds(pl.multiple_of(8 * c, 8), 8), :] + my[...] * v0

    def store(c, x, rows, plane, after):
        out[c, rows, :] = after

    def sent(c, half):
        @pl.when(half == 1)
        def _():
            pltpu.make_async_copy(out.at[c], out_hbm.at[c], sems.at[c]).start()

    advance(
        now, prev, rw, (low_x, low_y), (xd2, y_high), (xd.at[pl.ds(48, 16)], r_high), scale,
        zd2[...], rolled(zd[...], -3), closing_z, index, store, acc, lambda *args: None, sent,
    )
    for copy in copies:
        copy.wait()


def patch_tile(count_d, slip, node, patch):
    pairs = node.shape[-1]
    hot_z = (lax.broadcasted_iota(jnp.int32, (NZL, pairs), 0) == (node & (NZL - 1))).astype(F32)
    at_z = jnp.dot(slip, hot_z, precision=HIGHEST, preferred_element_type=F32)
    row_y = lax.broadcasted_iota(jnp.int32, (NYL, pairs), 0) == (node >> 7)
    owner = patch >> 1
    owner_d = owner & (count_d - 1)
    slot = ((owner >> (count_d.bit_length() - 1)) << 1) + (patch & 1)
    hot_slot = lax.broadcasted_iota(jnp.int32, (32, pairs), 0) == slot
    spread = []
    for c in range(3):
        picked = jnp.sum(jnp.where(row_y, at_z[NYL * c : NYL * (c + 1), :], 0.0), axis=0, keepdims=True)
        spread.append(jnp.where(hot_slot, picked, 0.0))
    spread.append(jnp.zeros((32, pairs), F32))
    hot_d = (lax.broadcasted_iota(jnp.int32, (8, pairs), 0) == owner_d).astype(F32)
    return lax.dot_general(
        hot_d, jnp.concatenate(spread, axis=0), (((1,), (1,)), ((), ())), precision=HIGHEST,
        preferred_element_type=F32,
    )


def final_kernel(tiles, out):
    mine = lax.axis_index("strike") * 2
    summed = jnp.sum(tiles[...], axis=0, keepdims=True)
    lane = lax.broadcasted_iota(jnp.int32, (2, NZL), 1)
    place = lax.broadcasted_iota(jnp.int32, (2, NZL), 0)
    for c in range(3):
        hit = lane == 32 * c + mine + place
        out[:, pl.ds(c, 1)] = jnp.sum(jnp.where(hit, summed, 0.0), axis=1, keepdims=True)


def call(kernel, name, outs, scratch=(), flops=0, moved=0, **specs):
    return pl.pallas_call(
        kernel,
        out_shape=[jax.ShapeDtypeStruct(o, F32) if isinstance(o, tuple) else jax.ShapeDtypeStruct(o.shape, o.dtype) for o in outs],
        scratch_shapes=[pltpu.VMEM(shape, F32) if isinstance(shape, tuple) else shape for shape in scratch],
        compiler_params=pltpu.CompilerParams(vmem_limit_bytes=16 * 2**20),
        cost_estimate=pl.CostEstimate(flops=flops, bytes_accessed=moved, transcendentals=0),
        name=name,
        **specs,
    )


def swap_near(value, axis):
    return lax.ppermute(value, axis, [(i, i ^ 1) for i in range(lax.axis_size(axis))])


def swap_far(value, axis):
    lower = range(1, lax.axis_size(axis) - 1, 2)
    return lax.ppermute(value, axis, [(i, i + 1) for i in lower] + [(i + 1, i) for i in lower])


def local(field_now, field_prev, rigidity, density, fault_nodes, patch_ids):
    axes = ("normal", "strike", "depth")
    counts = tuple(lax.axis_size(a) for a in axes)
    flat, block, tile = (3, ROWS, NZL), (ROWS, NZL), (8, NZL)
    now, prev = field_now.reshape(flat), field_prev.reshape(flat)
    rig, rho = rigidity.reshape(block), density.reshape(block)
    nodes, ids = fault_nodes.reshape(1, -1), patch_ids.reshape(1, -1)
    x_up, x_down, y_up, y_down = ((n, NZL) for n in (X_UP, X_DOWN, Y_UP, Y_DOWN))
    faces, strip = (48, NZL), (24, NZL)
    y_sent = jax.ShapeDtypeStruct((16 * Y_TILES, NZL), jnp.bfloat16)
    xa, xb, za, zb, zd_own, tails, rw, now, prev, rho, nodes, ids = call(
        pack_kernel, "pack",
        [x_up, x_up, tile, tile, tile, (32, NZL), block, flat, flat, rho, nodes, ids],
        [pltpu.VMEM(block, jnp.bfloat16), x_up, x_down, tile, pltpu.SemaphoreType.DMA((6,))],
        flops=2_000_000, moved=900_000, in_specs=[pl.BlockSpec(memory_space=pltpu.HBM)] * 6,
    )(*(pltpu.with_memory_space_constraint(x, pltpu.HBM) for x in (now, prev, rig, rho, nodes, ids)))
    xa, xb = swap_near(xa, "normal"), swap_far(xb, "normal")
    zb, za = swap_far(zb, "depth"), swap_near(za, "depth")
    inner, term, scale = call(
        inner_kernel, "inner", [flat, faces, block], [flat], flops=10_000_000, moved=900_000,
    )(now, prev, rw, rho)
    base, yb, ya, early, mx, mz, xd, zd = call(
        functools.partial(edge_kernel, counts), "edge",
        [flat, y_sent, y_sent, faces, (16, NZL), tile, x_down, tile],
        [x_up, tile, y_up, y_down], flops=2_000_000, moved=900_000,
    )(inner, now, rw, scale, term, tails, xa, xb, za, zb, zd_own)
    yb, ya = swap_far(yb, "strike"), swap_near(ya, "strike")
    kept, to_depth, xa2, xb2, zd2, my, y_low, y_high, r_high = call(
        functools.partial(whole_kernel, counts), "whole",
        [flat, (8 * counts[2], NZL), faces, faces, tile, tile, strip, strip, tile],
        [faces, y_up, y_down, faces, faces, tile], flops=2_000_000, moved=900_000,
    )(base, now, rw, scale, early, yb, ya, mx, xd, zd, nodes, ids)
    got_z = lax.all_to_all(to_depth, "depth", 0, 0, tiled=True)
    (to_face,) = call(
        functools.partial(sum_kernel, counts), "add", [(counts[0] * counts[1], NZL)], flops=10_000, moved=80_000,
    )(got_z)
    got_face = lax.all_to_all(to_face, ("strike", "normal"), 0, 0, tiled=True)
    xa2, xb2 = swap_near(xa2, "normal"), swap_far(xb2, "normal")
    (share,) = call(final_kernel, "final", [(2, 3)], flops=10_000, moved=10_000)(got_face)
    following, mid = call(
        functools.partial(second_kernel, counts), "second", [flat, flat],
        [flat, flat, faces, faces, tile, tile, pltpu.SemaphoreType.DMA((4,))],
        flops=10_000_000, moved=900_000, out_specs=[pl.BlockSpec(memory_space=pltpu.HBM)] * 2,
    )(kept, now, rw, scale, xa2, xb2, got_z, zd2, mx, my, mz, xd, zd, y_low, y_high, r_high)
    return following.reshape(field_now.shape), mid.reshape(field_now.shape), share


def solution(mesh):
    field = P(None, "normal", "strike", "depth")
    cells = P("normal", "strike", "depth")
    pairs = P("strike", "depth", None)
    return jax.shard_map(
        local,
        mesh=mesh,
        in_specs=(field, field, cells, cells, pairs, pairs),
        out_specs=(field, field, P(("strike", "depth"), None)),
        check_vma=False,
    )
```
